32 devices in a mesh: fsdp: 8 (over y, x, core), tp: 4 (over z).
Axes of the slice: x: 2, y: 2, z: 4, core: 2. Of those that a mesh axis runs over, the one named last changes fastest.
Arguments:
- tokens: bfloat16 [8192, 2048], P(('fsdp', 'tp')), may hold values from -6 to 6
- lengths: int32 [8, 4], P('fsdp'), may hold values from 1 to 512, 1024 in all within a row
- ln_gains: float32 [2, 2048], P(None, ('fsdp', 'tp')), may hold values from 0.1 to 1.9
- ln_shifts: float32 [2, 2048], P(None, ('fsdp', 'tp')), may hold values from -1.5 to 1.5
- w_qkv: bfloat16 [2048, 3, 2048], P('fsdp', None, 'tp'), may hold values from -0.125 to 0.125
- b_qkv: bfloat16 [3, 2048], P(None, ('tp', 'fsdp')), may hold values from -3 to 3
- w_out: bfloat16 [2048, 2048], P('tp', 'fsdp'), may hold values from -0.5 to 0.5
- w_gate_up: bfloat16 [2048, 2, 5632], P('fsdp', None, 'tp'), may hold values from -0.125 to 0.125
- w_down: bfloat16 [5632, 2048], P('tp', 'fsdp'), may hold values from -0.078125 to 0.078125
- cotangent: bfloat16 [8192, 2048], P(('fsdp', 'tp')), may hold values from -6 to 6
Outputs:
- out_tokens: bfloat16 [8192, 2048], P(('fsdp', 'tp'))
- grad_tokens: float32 [8192, 2048], P(('fsdp', 'tp'))
- grad_ln_gains: float32 [2, 2048], P(None, ('fsdp', 'tp'))
- grad_ln_shifts: float32 [2, 2048], P(None, ('fsdp', 'tp'))
- grad_w_qkv: float32 [2048, 3, 2048], P('fsdp', None, 'tp')
- grad_b_qkv: float32 [3, 2048], P(None, ('tp', 'fsdp'))
- grad_w_out: float32 [2048, 2048], P('tp', 'fsdp')
- grad_w_gate_up: float32 [2048, 2, 5632], P('fsdp', None, 'tp')
- grad_w_down: float32 [5632, 2048], P('tp', 'fsdp')
The draws below stay inside these ranges and needn't reach their ends.
Inputs may be any that keep to these rules, and one draw needn't show every extreme that they name: In each row the lengths sum to 1024 and the largest is exactly 512.
All inputs are finite; a program needn't handle non-finite values.
Results may differ from the reference program's by a relative error of at most 0.03.
Values may be sent and summed in bfloat16 or wider, within the bound.
A program may use at most 192 MiB of HBM per device.

```python
import math
import jax
import jax.numpy as jnp
import numpy as np
from jax import lax

D = 2048
NHEADS = 32
HEAD = 64
ROT = 16
FF = 5632
SEQ = 1024
NDOC = 4
SEQS = 8
TOKENS = 8192
N_TP = 4


def level_of(key, extent, split, smallest, largest):
    factor_of, own = 1.0, jax.random.fold_in(key, 6)
    for dim, shards_of in split:
        heights = jnp.exp(jax.random.uniform(jax.random.fold_in(own, dim), (shards_of,), jnp.float32, smallest / len(split), largest / len(split)))
        factor_of = factor_of * jnp.repeat(heights, extent[dim] // shards_of).reshape([-1 if axis == dim else 1 for axis in range(len(extent))])
    return factor_of


def length_profile(count, total, limit, lean):
    portions = [(1 << 20) // math.isqrt(grade ** lean) + 1 for grade in range(2, count + 1)]
    rest, counts = total - limit - (count - 1), [1] * (count - 1)
    while rest > 0:
        candidates = [i for i in range(count - 1) if counts[i] < limit]
        pool, budget = sum([portions[i] for i in candidates]), rest
        for i in candidates:
            addition = min(limit - counts[i], max(1, budget * portions[i] // pool), rest)
            counts[i] = counts[i] + addition
            rest = rest - addition
    return np.array([limit] + counts)


def uneven(stream_key, amount, total, limit, lean):
    if amount == 2:
        one = jax.random.randint(stream_key, (), max(1, total - limit), min(limit, total - 1) + 1)
        return jnp.stack([one, total - one])
    sizes = jnp.asarray(length_profile(amount, total, limit, lean), jnp.int32)
    pairs = (amount - 1) // 2
    donor, receiver = sizes[1:1 + 2 * pairs:2], sizes[2:2 + 2 * pairs:2]
    margin = jnp.minimum(donor - 1, limit - receiver)
    shifted = jax.random.randint(jax.random.fold_in(stream_key, 1), (pairs,), 0, 1 << 20) % (margin + 1)
    sizes = sizes.at[1:1 + 2 * pairs:2].set(donor - shifted).at[2:2 + 2 * pairs:2].set(receiver + shifted)
    return sizes[jax.random.permutation(jax.random.fold_in(stream_key, 2), amount)]


def noise(rng, extent, scale, bound, cuts=(), kind=jnp.bfloat16):
    array = scale * jax.random.normal(rng, extent, jnp.float32)
    if cuts:
        array = array * level_of(rng, extent, cuts, -0.22, 0.18)
    return jnp.clip(array, -bound, bound).astype(kind)


def setup_inputs(seed: int = 0) -> dict:
    arg_keys = jax.random.split(jax.random.key(seed), 11)
    tokens = noise(arg_keys[0], (TOKENS, D), 1.0, 6.0, ((0, 32),))
    lengths = jax.vmap(lambda own: uneven(own, NDOC, SEQ, SEQ // 2, 0))(jax.random.split(arg_keys[1], SEQS)).reshape((SEQS, NDOC)).astype(jnp.int32)
    ln_gains = jnp.clip(1.0 + 0.18 * jax.random.normal(arg_keys[2], (2, D), jnp.float32), 0.1, 1.9)
    ln_shifts = noise(arg_keys[3], (2, D), 0.3, 1.5, ((1, 32),), jnp.float32)
    w_qkv = noise(arg_keys[4], (D, 3, D), D ** -0.5, 0.125, ((0, 8), (2, 4)))
    b_qkv = noise(arg_keys[5], (3, D), 0.5, 3.0, ((1, 32),))
    w_out = noise(arg_keys[6], (D, D), (D // 16) ** -0.5, 0.5, ((0, 4), (1, 8)))
    w_gate_up = noise(arg_keys[7], (D, 2, FF), D ** -0.5, 0.125, ((0, 8), (2, 4)))
    w_down = noise(arg_keys[8], (FF, D), FF ** -0.5, 0.078125, ((0, 4), (1, 8)))
    cotangent = noise(arg_keys[9], (TOKENS, D), 1.0, 6.0, ((0, 32),))
    return dict(tokens=tokens, lengths=lengths, ln_gains=ln_gains, ln_shifts=ln_shifts, w_qkv=w_qkv, b_qkv=b_qkv, w_out=w_out, w_gate_up=w_gate_up, w_down=w_down, cotangent=cotangent)


@jax.custom_vjp
def low(v):
    return lax.optimization_barrier(v.astype(jnp.bfloat16)).astype(jnp.float32)

@jax.custom_vjp
def low_back(v):
    return v

def low_keep(v):
    return (low(v), None)

def low_pass(kept, grad):
    return (grad,)

def back_keep(v):
    return (v, None)

def back_low(kept, grad):
    return (low(grad),)
low.defvjp(low_keep, low_pass)
low_back.defvjp(back_keep, back_low)
NORM_EPS = 1e-05
HIGHEST_PRECISION = lax.Precision.HIGHEST

def layer_norm(values, gain_row, shift_row):
    average = lax.optimization_barrier(jnp.mean(values, axis=-1, keepdims=True))
    centred = values - average
    variance = lax.optimization_barrier(jnp.mean(centred * centred, axis=-1, keepdims=True))
    return centred * lax.rsqrt(variance + NORM_EPS) * gain_row + shift_row

def doc_layout(length_row, seq_len):
    doc_ends = jnp.cumsum(length_row).astype(jnp.int32)
    columns = jnp.arange(seq_len, dtype=jnp.int32)
    passed = (doc_ends[None, :] <= columns[:, None]).astype(jnp.int32)
    seg_ids = lax.optimization_barrier(jnp.sum(passed, axis=1)).astype(jnp.int32)
    starts = lax.optimization_barrier(jnp.sum(passed * length_row[None, :], axis=1)).astype(jnp.int32)
    return (seg_ids, columns - starts)

def rotate(values, places):
    half_rot = ROT // 2
    frequency = 10000.0 ** (-2.0 * jnp.arange(half_rot, dtype=jnp.float32) / ROT)
    angles = places.astype(jnp.float32)[:, None] * frequency[None, :]
    cosine = jnp.cos(angles)[:, None, :]
    sine_vals = jnp.sin(angles)[:, None, :]
    lower_half = values[..., :half_rot]
    upper_half = values[..., half_rot:ROT]
    return jnp.concatenate([lower_half * cosine - upper_half * sine_vals, upper_half * cosine + lower_half * sine_vals, values[..., ROT:]], axis=-1)

def visible(seg_ids, first_row, block_rows):
    row_segs = lax.dynamic_slice_in_dim(seg_ids, first_row, block_rows, 0)
    row_places = first_row + jnp.arange(block_rows, dtype=jnp.int32)
    columns = jnp.arange(seg_ids.shape[0], dtype=jnp.int32)
    return (row_segs[:, None] == seg_ids[None, :]) & (columns[None, :] <= row_places[:, None])

def attend(queries, key_vals, value_rows, seg_ids):
    seq_len = queries.shape[0]
    block_rows = min(512, seq_len)
    scale = HEAD ** (-0.5)

    def one_block(block_index):
        first_row = (block_index * block_rows).astype(jnp.int32)
        rows_q = lax.dynamic_slice_in_dim(queries, first_row, block_rows, 0)
        scores = jnp.einsum('qhe,khe->hqk', rows_q, key_vals, precision=HIGHEST_PRECISION) * scale
        scores = low_back(scores)
        scores = jnp.where(visible(seg_ids, first_row, block_rows)[None], scores, -1e+30)
        row_max = lax.optimization_barrier(jnp.max(scores, axis=-1, keepdims=True))
        weights = jnp.exp(scores - row_max)
        weights = low(weights / lax.optimization_barrier(jnp.sum(weights, axis=-1, keepdims=True)))
        return jnp.einsum('hqk,khe->qhe', weights, value_rows, precision=HIGHEST_PRECISION)
    outputs = lax.map(jax.checkpoint(one_block), jnp.arange(seq_len // block_rows, dtype=jnp.int32))
    return outputs.reshape(queries.shape)

def layer(token_rows, seg_ids, places, params):
    ln_gains, ln_shifts, w_qkv, b_qkv, w_out, w_gate_up, w_down = params
    seq_len = token_rows.shape[0]
    normed_one = low(layer_norm(token_rows, ln_gains[0], ln_shifts[0]))
    projected = jnp.dot(normed_one, w_qkv.reshape(D, 3 * D), precision=HIGHEST_PRECISION).reshape(seq_len, 3, D) + b_qkv[None]
    projected = low_back(projected)
    queries = low(rotate(projected[:, 0].reshape(seq_len, NHEADS, HEAD), places))
    key_vals = low(rotate(projected[:, 1].reshape(seq_len, NHEADS, HEAD), places))
    value_rows = low(projected[:, 2].reshape(seq_len, NHEADS, HEAD))
    attended = attend(queries, key_vals, value_rows, seg_ids).reshape(seq_len, D)
    attended = low(low_back(attended))
    partial_value = jnp.einsum('sge,ged->gsd', attended.reshape(seq_len, N_TP, D // N_TP), w_out.reshape(N_TP, D // N_TP, D), precision=HIGHEST_PRECISION)
    attn_out = low_back(lax.optimization_barrier(jnp.sum(low(partial_value), axis=0)))
    residual = token_rows + attn_out
    normed_two = low(layer_norm(residual, ln_gains[1], ln_shifts[1]))
    gate_up = jnp.dot(normed_two, w_gate_up.reshape(D, 2 * FF), precision=HIGHEST_PRECISION).reshape(seq_len, 2, FF)
    gate_up = low_back(gate_up)
    hidden = low(jax.nn.silu(gate_up[:, 0]) * gate_up[:, 1])
    partial_two = jnp.einsum('sgf,gfd->gsd', hidden.reshape(seq_len, N_TP, FF // N_TP), w_down.reshape(N_TP, FF // N_TP, D), precision=HIGHEST_PRECISION)
    branch = low_back(lax.optimization_barrier(jnp.sum(low(partial_two), axis=0)))
    return residual + branch

def reference(tokens, lengths, ln_gains, ln_shifts, w_qkv, b_qkv, w_out, w_gate_up, w_down, cotangent):
    seg_ids, places = jax.vmap(lambda length_row: doc_layout(length_row, SEQ))(lengths)
    token_vals = tokens.astype(jnp.float32)
    gains_vals = ln_gains.astype(jnp.float32)
    shifts_vals = ln_shifts.astype(jnp.float32)
    qkv_vals = w_qkv.astype(jnp.float32)
    bias_vals = b_qkv.astype(jnp.float32)
    out_vals = w_out.astype(jnp.float32)
    gate_vals = w_gate_up.astype(jnp.float32)
    down_vals = w_down.astype(jnp.float32)

    def forward(token_in, gains_in, shifts_in, qkv_in, bias_in, out_in, gate_in, down_in):
        params = (gains_in, shifts_in, qkv_in, bias_in, out_in, gate_in, down_in)

        def scan_step(carried, inputs):
            token_rows, seq_segs, seq_places = inputs
            return (carried, jax.checkpoint(layer)(token_rows, seq_segs, seq_places, params))
        _, outputs = lax.scan(scan_step, None, (token_in.reshape(SEQS, SEQ, D), seg_ids, places))
        return outputs.reshape(SEQS * SEQ, D)
    result, pullback = jax.vjp(forward, token_vals, gains_vals, shifts_vals, qkv_vals, bias_vals, out_vals, gate_vals, down_vals)
    gradients = pullback(cotangent.astype(jnp.float32))
    return (result.astype(jnp.bfloat16), gradients[0], gradients[1], gradients[2], gradients[3], gradients[4], gradients[5], gradients[6], gradients[7])
```

```python
import functools

import jax
import jax.numpy as jnp
from jax import lax
from jax.experimental import pallas as pl
from jax.experimental.pallas import tpu as pltpu
from jax.sharding import PartitionSpec as P

HEAD = 64
ROT = 16
NORM_EPS = 1e-05
LANES = 128
MESH = pl.DeviceIdType.MESH
NN = (((1,), (0,)), ((), ()))
NT = (((1,), (1,)), ((), ()))
TN = (((0,), (0,)), ((), ()))
F32 = jnp.float32
BF16 = jnp.bfloat16


def dot(left, right, dims):
    return lax.dot_general(left, right, dims, preferred_element_type=F32)


def layer_norm(values, gain_row, shift_row):
    average = jnp.mean(values, axis=-1, keepdims=True)
    centred = values - average
    variance = jnp.mean(centred * centred, axis=-1, keepdims=True)
    return centred * lax.rsqrt(variance + NORM_EPS) * gain_row + shift_row


def swiglu(gate_vals, up_vals):
    return jax.nn.silu(gate_vals) * up_vals


def exchange_kernel(sizes, scatter, send_ref, got_ref, send_sems, recv_sems):
    outer, inner = sizes
    count = outer * inner
    me = lax.axis_index("fsdp") * inner + lax.axis_index("tp")
    barrier = pltpu.get_barrier_semaphore()

    def greet(step, carry):
        other = lax.rem(me + step, count)
        pl.semaphore_signal(
            barrier, inc=1, device_id=(other // inner, lax.rem(other, inner)), device_id_type=MESH
        )
        return carry

    lax.fori_loop(1, count, greet, 0)
    pl.semaphore_wait(barrier, count - 1)

    def copy_to(step):
        other = lax.rem(me + step, count)
        return pltpu.make_async_remote_copy(
            src_ref=send_ref.at[other] if scatter else send_ref.at[0],
            dst_ref=got_ref.at[me],
            send_sem=send_sems.at[step],
            recv_sem=recv_sems.at[me],
            device_id=(other // inner, lax.rem(other, inner)),
            device_id_type=MESH,
        )

    def start(step, carry):
        copy_to(step).start()
        return carry

    lax.fori_loop(1, count, start, 0)
    got_ref[me] = send_ref[me] if scatter else send_ref[0]

    def finish(step, carry):
        source = lax.rem(me + step, count)
        copy_to(step).wait_send()
        pltpu.make_async_remote_copy(
            src_ref=send_ref.at[0],
            dst_ref=got_ref.at[source],
            send_sem=send_sems.at[step],
            recv_sem=recv_sems.at[source],
            device_id=(source // inner, lax.rem(source, inner)),
            device_id_type=MESH,
        ).wait_recv()
        return carry

    lax.fori_loop(1, count, finish, 0)


def exchange(tiles, sizes, scatter, collective_id):
    count = sizes[0] * sizes[1]
    return pl.pallas_call(
        functools.partial(exchange_kernel, sizes, scatter),
        out_shape=jax.ShapeDtypeStruct((count, 8, LANES), F32),
        in_specs=[pl.BlockSpec(memory_space=pltpu.VMEM)],
        out_specs=pl.BlockSpec(memory_space=pltpu.VMEM),
        scratch_shapes=[
            pltpu.SemaphoreType.DMA((count,)),
            pltpu.SemaphoreType.DMA((count,)),
        ],
        compiler_params=pltpu.CompilerParams(collective_id=collective_id, has_side_effects=True),
    )(tiles)


def turn(values, cosine, sine_low, sine_high):
    return (
        values * cosine
        + pltpu.roll(values, LANES - ROT // 2, 1) * sine_low
        + pltpu.roll(values, ROT // 2, 1) * sine_high
    )


def key_range(block, rows, widest):
    first = max(0, block * rows - widest)
    return first, (block + 1) * rows


def seen_weights(key_rows, query_cols, starts_row, first_key, first_query):
    scores = dot(key_rows, query_cols, NN)
    key_ids = first_key + lax.broadcasted_iota(jnp.int32, scores.shape, 0)
    query_ids = first_query + lax.broadcasted_iota(jnp.int32, scores.shape, 1)
    seen = (key_ids <= query_ids) & (key_ids >= starts_row)
    scores = jnp.where(seen, scores, -1e30)
    top = jnp.max(scores, axis=0, keepdims=True)
    weights = jnp.exp(scores - top)
    return weights, jnp.sum(weights, axis=0, keepdims=True)


def attend_kernel(rows, widest, q_in, k_in, v_in, cos, s_low, s_high, starts, q_out, k_out, v_out, o_out, vt):
    seq_len = q_in.shape[0]
    cosine, sine_low, sine_high = cos[...], s_low[...], s_high[...]
    q_out[...] = turn(q_in[...], cosine, sine_low, sine_high).astype(BF16)
    k_out[...] = turn(k_in[...], cosine, sine_low, sine_high).astype(BF16)
    v_low = v_in[...].astype(BF16)
    v_out[...] = v_low
    vt[...] = v_low.astype(F32).T.astype(BF16)
    for block in range(seq_len // rows):
        here = slice(block * rows, (block + 1) * rows)
        first, last = key_range(block, rows, widest)
        query_cols = (q_out[here, :].astype(F32) * HEAD**-0.5).T.astype(BF16)
        head_of = lax.broadcasted_iota(jnp.int32, query_cols.shape, 0) // HEAD
        parts = []
        for head in range(LANES // HEAD):
            own_cols = jnp.where(head_of == head, query_cols, jnp.zeros_like(query_cols))
            weights, total = seen_weights(
                k_out[first:last, :], own_cols, starts[:, here], first, block * rows
            )
            part = dot(vt[head * HEAD : (head + 1) * HEAD, first:last], weights.astype(BF16), NN)
            parts.append(part / total)
        o_out[here, :] = jnp.concatenate(parts, axis=0).T.astype(BF16)


def attend_back_kernel(
    rows, widest, q_in, k_in, v_in, g_in, cos, s_low, s_high, starts, g_out, b_out, kt, dk, dv
):
    seq_len = q_in.shape[0]
    cosine, sine_low, sine_high = cos[...], s_low[...], s_high[...]
    kt[...] = k_in[...].astype(F32).T.astype(BF16)
    dk[...] = jnp.zeros_like(dk)
    dv[...] = jnp.zeros_like(dv)
    for block in range(seq_len // rows):
        here = slice(block * rows, (block + 1) * rows)
        first, last = key_range(block, rows, widest)
        query_rows = (q_in[here, :].astype(F32) * HEAD**-0.5).astype(BF16)
        grad_rows = g_in[here, :]
        query_cols = query_rows.astype(F32).T.astype(BF16)
        grad_cols = grad_rows.astype(F32).T.astype(BF16)
        head_down = lax.broadcasted_iota(jnp.int32, query_cols.shape, 0) // HEAD
        head_along = lax.broadcasted_iota(jnp.int32, query_rows.shape, 1) // HEAD
        none_down, none_along = jnp.zeros_like(query_cols), jnp.zeros_like(query_rows)
        parts = []
        for head in range(LANES // HEAD):
            weights, total = seen_weights(
                k_in[first:last, :],
                jnp.where(head_down == head, query_cols, none_down),
                starts[:, here],
                first,
                block * rows,
            )
            probs = weights * (1.0 / total)
            grad_probs = dot(
                v_in[first:last, :], jnp.where(head_down == head, grad_cols, none_down), NN
            )
            inner = jnp.sum(probs * grad_probs, axis=0, keepdims=True)
            grad_scores = (probs * (grad_probs - inner)).astype(BF16)
            dk[first:last, :] += dot(
                grad_scores, jnp.where(head_along == head, query_rows, none_along), NN
            )
            dv[first:last, :] += dot(
                probs.astype(BF16), jnp.where(head_along == head, grad_rows, none_along), NN
            )
            parts.append(dot(kt[head * HEAD : (head + 1) * HEAD, first:last], grad_scores, NN))
        grad_queries = jnp.concatenate(parts, axis=0).T * HEAD**-0.5
        g_out[0, here, :] = turn(
            grad_queries, cosine[here, :], -sine_low[here, :], -sine_high[here, :]
        ).astype(BF16)
    g_out[1] = turn(dk[...], cosine, -sine_low, -sine_high).astype(BF16)
    g_out[2] = dv[...].astype(BF16)
    b_out[...] = jnp.sum(g_out[...].astype(F32), axis=1, keepdims=True)


def attend_forward(projected, tables, starts, widest):
    seq_len, width = projected.shape[0], projected.shape[1] // 3
    pairs = width // LANES
    rows = min(256, seq_len)
    column = lambda part: pl.BlockSpec((seq_len, LANES), lambda i, part=part: (0, part * pairs + i))
    whole = lambda shape: pl.BlockSpec(shape, lambda i: (0, 0))
    out = jax.ShapeDtypeStruct((seq_len, width), BF16)
    return pl.pallas_call(
        functools.partial(attend_kernel, rows, widest),
        grid=(pairs,),
        in_specs=[column(0), column(1), column(2)]
        + [whole((seq_len, LANES))] * 3
        + [whole((1, seq_len))],
        out_specs=[column(0)] * 4,
        out_shape=[out] * 4,
        scratch_shapes=[pltpu.VMEM((LANES, seq_len), BF16)],
        compiler_params=pltpu.CompilerParams(vmem_limit_bytes=48 * 2**20),
        cost_estimate=pl.CostEstimate(
            flops=4 * seq_len * seq_len * width, bytes_accessed=20 * seq_len * width, transcendentals=0
        ),
    )(projected, projected, projected, *tables, starts)


def attend_backward(queries, key_vals, value_rows, grad_attended, tables, starts, widest):
    seq_len, width = queries.shape
    pairs = width // LANES
    rows = min(256, seq_len)
    column = pl.BlockSpec((seq_len, LANES), lambda i: (0, i))
    whole = lambda shape: pl.BlockSpec(shape, lambda i: (0, 0))
    return pl.pallas_call(
        functools.partial(attend_back_kernel, rows, widest),
        grid=(pairs,),
        in_specs=[column] * 4 + [whole((seq_len, LANES))] * 3 + [whole((1, seq_len))],
        out_specs=[
            pl.BlockSpec((3, seq_len, LANES), lambda i: (0, 0, i)),
            pl.BlockSpec((3, 1, LANES), lambda i: (0, 0, i)),
        ],
        out_shape=[
            jax.ShapeDtypeStruct((3, seq_len, width), BF16),
            jax.ShapeDtypeStruct((3, 1, width), F32),
        ],
        scratch_shapes=[
            pltpu.VMEM((LANES, seq_len), BF16),
            pltpu.VMEM((seq_len, LANES), F32),
            pltpu.VMEM((seq_len, LANES), F32),
        ],
        compiler_params=pltpu.CompilerParams(vmem_limit_bytes=48 * 2**20),
        cost_estimate=pl.CostEstimate(
            flops=10 * seq_len * seq_len * width, bytes_accessed=20 * seq_len * width, transcendentals=0
        ),
    )(queries, key_vals, value_rows, grad_attended, *tables, starts)


def hop(values, axis, size, partner):
    return lax.ppermute(values, axis, [(i, partner(i)) for i in range(size)])


def gather_fsdp(own, size):
    me = lax.axis_index("fsdp")
    near = [own] + [
        hop(own, "fsdp", size, lambda i, k=k: i ^ (2 * k)) for k in range(1, size // 2)
    ]
    far = [hop(block, "fsdp", size, lambda i: i ^ 1) for block in near]
    whole = jnp.zeros((size,) + own.shape, own.dtype)
    for k in range(size // 2):
        whole = lax.dynamic_update_index_in_dim(whole, near[k], me ^ (2 * k), 0)
        whole = lax.dynamic_update_index_in_dim(whole, far[k], me ^ (2 * k) ^ 1, 0)
    return whole


def scatter_fsdp(blocks, size):
    me = lax.axis_index("fsdp")
    core, chip = me % 2, me // 2
    pairs = blocks.reshape((size // 2, 2) + blocks.shape[1:])
    mine = lax.dynamic_index_in_dim(pairs, core, 1, keepdims=False)
    other = lax.dynamic_index_in_dim(pairs, 1 - core, 1, keepdims=False)
    got = hop(other, "fsdp", size, lambda i: i ^ 1)
    sums = (mine.astype(F32) + got.astype(F32)).astype(BF16)
    total = lax.dynamic_index_in_dim(sums, chip, 0, keepdims=False).astype(F32)
    for k in range(1, size // 2):
        block = lax.dynamic_index_in_dim(sums, chip ^ k, 0, keepdims=False)
        total = total + hop(block, "fsdp", size, lambda i, k=k: i ^ (2 * k)).astype(F32)
    return total


def swap_tp(blocks, size):
    me = lax.axis_index("tp")
    got = blocks
    for k in range(1, size):
        block = lax.dynamic_index_in_dim(blocks, (me + k) % size, 0, keepdims=False)
        came = hop(block, "tp", size, lambda i, k=k: (i + k) % size)
        got = lax.dynamic_update_index_in_dim(got, came, (me + size - k) % size, 0)
    return got


def gather_tp_small(own, size):
    me = lax.axis_index("tp")
    whole = jnp.zeros((size,) + own.shape, own.dtype)
    whole = lax.dynamic_update_index_in_dim(whole, own, me, 0)
    for k in range(1, size):
        came = hop(own, "tp", size, lambda i, k=k: (i + k) % size)
        whole = lax.dynamic_update_index_in_dim(whole, came, (me + size - k) % size, 0)
    return whole


def gather_rows(values):
    return lax.all_gather(values, "tp", axis=0, tiled=True)


def reduce_rows(values):
    return lax.psum_scatter(values.astype(BF16), "tp", scatter_dimension=0, tiled=True).astype(F32)


def local(tokens, lengths, ln_gains, ln_shifts, w_qkv, b_qkv, w_out, w_gate_up, w_down, cotangent):
    n_fsdp, n_tp = lax.axis_size("fsdp"), lax.axis_size("tp")
    sizes = (n_fsdp, n_tp)
    at_tp = lax.axis_index("tp")
    slab_rows, model_width = tokens.shape
    seq_len = slab_rows * n_tp
    small = ln_gains.shape[1]
    local_width = w_qkv.shape[2]
    hidden_width = w_gate_up.shape[2]
    part_rows = w_qkv.shape[0]

    tile = jnp.concatenate([ln_gains, ln_shifts, b_qkv.astype(F32), jnp.zeros((1, small), F32)], 0)
    tile = jnp.pad(tile, ((0, 0), (0, LANES - small)))
    got = exchange(tile[None], sizes, False, 1)
    rows_all = got[:, :, :small]
    norm_rows = rows_all[:, :4].transpose(1, 0, 2).reshape(4, model_width)
    gains_all, shifts_all = norm_rows[:2], norm_rows[2:]
    bias = lax.dynamic_index_in_dim(rows_all.reshape(n_fsdp, n_tp, 8, small), at_tp, 1, keepdims=False)
    bias = bias[:, 4:7].transpose(1, 0, 2).reshape(1, 3 * local_width)

    qkv_all = gather_fsdp(w_qkv.reshape(part_rows, 3 * local_width), n_fsdp).reshape(
        model_width, 3 * local_width
    )
    out_part = gather_tp_small(w_out.T, n_tp).transpose(1, 0, 2).reshape(part_rows, model_width)
    out_all = gather_fsdp(out_part, n_fsdp).reshape(model_width, model_width)
    gu_all = gather_fsdp(w_gate_up.reshape(part_rows, 2 * hidden_width), n_fsdp).reshape(
        model_width, 2 * hidden_width
    )
    down_all = gather_fsdp(w_down.T, n_fsdp).reshape(model_width, hidden_width)

    length_row = lengths[0]
    doc_ends = jnp.cumsum(length_row)
    ids = jnp.arange(seq_len, dtype=jnp.int32)
    passed = (doc_ends[None, :] <= ids[:, None]).astype(jnp.int32)
    starts = jnp.sum(passed * length_row[None, :], axis=1)
    places = (ids - starts).astype(F32)
    lane = jnp.arange(LANES, dtype=jnp.int32) % HEAD
    frequency = 10000.0 ** (-2.0 * (lane % (ROT // 2)).astype(F32) / ROT)
    angles = places[:, None] * frequency[None, :]
    cosine = jnp.where(lane[None] < ROT, jnp.cos(angles), 1.0)
    sine = jnp.sin(angles)
    sine_low = jnp.where(lane[None] < ROT // 2, -sine, 0.0)
    sine_high = jnp.where((lane[None] >= ROT // 2) & (lane[None] < ROT), sine, 0.0)
    tables = (cosine, sine_low, sine_high)
    starts_row = starts.reshape(1, seq_len).astype(jnp.int32)
    widest = seq_len // 2

    token_rows = tokens.astype(F32)
    normed_one = layer_norm(token_rows, gains_all[0], shifts_all[0])
    full_one = gather_rows(normed_one.astype(BF16))
    projected = dot(full_one, qkv_all, NN) + bias
    queries, key_vals, value_rows, attended = attend_forward(projected, tables, starts_row, widest)
    attended_own = (
        swap_tp(attended.reshape(n_tp, slab_rows, local_width), n_tp)
        .transpose(1, 0, 2)
        .reshape(slab_rows, model_width)
    )
    residual = token_rows + dot(attended_own, out_all, NT)

    normed_two = layer_norm(residual, gains_all[1], shifts_all[1])
    full_two = gather_rows(normed_two.astype(BF16))
    grad_branch = gather_rows(cotangent)
    gate_up = dot(full_two, gu_all, NN)
    gate, up = gate_up[:, :hidden_width], gate_up[:, hidden_width:]
    hidden_low = swiglu(gate, up).astype(BF16)
    branch = reduce_rows(dot(hidden_low, down_all, NT))
    result = (residual + branch).astype(BF16)
    grad_out = cotangent.astype(F32)
    grad_hidden = dot(grad_branch, down_all, NN)
    _, swiglu_pull = jax.vjp(swiglu, gate, up)
    grad_gate, grad_up = swiglu_pull(grad_hidden)
    grad_gate_up = jnp.concatenate([grad_gate, grad_up], axis=1).astype(BF16)
    grad_normed_two = reduce_rows(dot(grad_gate_up, gu_all, NT))
    grad_gu = dot(full_two, grad_gate_up, TN).astype(BF16)
    grad_down = dot(grad_branch, hidden_low, TN).astype(BF16)
    gu_share = scatter_fsdp(grad_gu.reshape(n_fsdp, part_rows, 2 * hidden_width), n_fsdp)
    down_share = scatter_fsdp(grad_down.reshape(n_fsdp, part_rows, hidden_width), n_fsdp)
    _, second_pull = jax.vjp(layer_norm, residual, gains_all[1], shifts_all[1])
    grad_resid_norm, grad_gain_two, grad_shift_two = second_pull(grad_normed_two)
    grad_residual = grad_out + grad_resid_norm

    grad_attn = grad_residual.astype(BF16)
    grad_o = dot(grad_attn, attended_own, TN).astype(BF16)
    grad_attended_own = dot(grad_attn, out_all, NN).astype(BF16)
    grad_attended = swap_tp(
        grad_attended_own.reshape(slab_rows, n_tp, local_width).transpose(1, 0, 2), n_tp
    ).reshape(seq_len, local_width)
    grad_projected, grad_bias = attend_backward(
        queries, key_vals, value_rows, grad_attended, tables, starts_row, widest
    )
    grad_projected = grad_projected.transpose(1, 0, 2).reshape(seq_len, 3 * local_width)
    grad_qkv = dot(full_one, grad_projected, TN).astype(BF16)
    grad_normed_one = reduce_rows(dot(grad_projected, qkv_all, NT))
    _, first_pull = jax.vjp(layer_norm, token_rows, gains_all[0], shifts_all[0])
    grad_token_norm, grad_gain_one, grad_shift_one = first_pull(grad_normed_one)
    grad_tokens = grad_residual + grad_token_norm

    out_share = scatter_fsdp(grad_o.reshape(n_fsdp, part_rows, model_width), n_fsdp).astype(BF16)
    out_share = jnp.sum(
        swap_tp(out_share.reshape(part_rows, n_tp, local_width).transpose(1, 0, 2), n_tp).astype(F32),
        axis=0,
    ).T
    qkv_share = scatter_fsdp(grad_qkv.reshape(n_fsdp, part_rows, 3 * local_width), n_fsdp)

    count = n_fsdp * n_tp
    norm_grads = jnp.stack([grad_gain_one, grad_gain_two, grad_shift_one, grad_shift_two])
    norm_grads = norm_grads.reshape(4, count, small).transpose(1, 0, 2)
    bias_grads = grad_bias.reshape(3, n_fsdp, small).transpose(1, 0, 2)
    bias_grads = jnp.where(
        (jnp.arange(n_tp) == at_tp)[None, :, None, None], bias_grads[:, None], 0.0
    ).reshape(count, 3, small)
    tiles = jnp.concatenate([norm_grads, bias_grads, jnp.zeros((count, 1, small), F32)], axis=1)
    tiles = jnp.pad(tiles, ((0, 0), (0, 0), (0, LANES - small)))
    shares = jnp.sum(exchange(tiles, sizes, True, 2), axis=0)[:, :small]

    return (
        result,
        grad_tokens,
        shares[0:2],
        shares[2:4],
        qkv_share.reshape(part_rows, 3, local_width),
        shares[4:7],
        out_share,
        gu_share.reshape(part_rows, 2, hidden_width),
        down_share.T,
    )


def solution(mesh):
    placed = (
        P(("fsdp", "tp"), None),
        P("fsdp", None),
        P(None, ("fsdp", "tp")),
        P(None, ("fsdp", "tp")),
        P("fsdp", None, "tp"),
        P(None, ("tp", "fsdp")),
        P("tp", "fsdp"),
        P("fsdp", None, "tp"),
        P("tp", "fsdp"),
        P(("fsdp", "tp"), None),
    )
    return jax.shard_map(
        local,
        mesh=mesh,
        in_specs=placed,
        out_specs=(
            P(("fsdp", "tp"), None),
            P(("fsdp", "tp"), None),
            P(None, ("fsdp", "tp")),
            P(None, ("fsdp", "tp")),
            P("fsdp", None, "tp"),
            P(None, ("tp", "fsdp")),
            P("tp", "fsdp"),
            P("fsdp", None, "tp"),
            P("tp", "fsdp"),
        ),
        check_vma=False,
    )
```

```python
import functools

import jax
import jax.numpy as jnp
from jax import lax
from jax.experimental import pallas as pl
from jax.experimental.pallas import tpu as pltpu
from jax.sharding import PartitionSpec as P

HEAD = 64
ROT = 16
NORM_EPS = 1e-05
LANES = 128
MESH = pl.DeviceIdType.MESH
NN = (((1,), (0,)), ((), ()))
NT = (((1,), (1,)), ((), ()))
TN = (((0,), (0,)), ((), ()))
F32 = jnp.float32
BF16 = jnp.bfloat16


def dot(left, right, dims):
    return lax.dot_general(left, right, dims, preferred_element_type=F32)


def layer_norm(values, gain_row, shift_row):
    average = jnp.mean(values, axis=-1, keepdims=True)
    centred = values - average
    variance = jnp.mean(centred * centred, axis=-1, keepdims=True)
    return centred * lax.rsqrt(variance + NORM_EPS) * gain_row + shift_row


def swiglu(gate_vals, up_vals):
    return jax.nn.silu(gate_vals) * up_vals


def exchange_kernel(sizes, scatter, send_ref, got_ref, send_sems, recv_sems):
    outer, inner = sizes
    count = outer * inner
    me = lax.axis_index("fsdp") * inner + lax.axis_index("tp")
    barrier = pltpu.get_barrier_semaphore()

    def greet(step, carry):
        other = lax.rem(me + step, count)
        pl.semaphore_signal(
            barrier, inc=1, device_id=(other // inner, lax.rem(other, inner)), device_id_type=MESH
        )
        return carry

    lax.fori_loop(1, count, greet, 0)
    pl.semaphore_wait(barrier, count - 1)

    def copy_to(step):
        other = lax.rem(me + step, count)
        return pltpu.make_async_remote_copy(
            src_ref=send_ref.at[other] if scatter else send_ref.at[0],
            dst_ref=got_ref.at[me],
            send_sem=send_sems.at[step],
            recv_sem=recv_sems.at[me],
            device_id=(other // inner, lax.rem(other, inner)),
            device_id_type=MESH,
        )

    def start(step, carry):
        copy_to(step).start()
        return carry

    lax.fori_loop(1, count, start, 0)
    got_ref[me] = send_ref[me] if scatter else send_ref[0]

    def finish(step, carry):
        source = lax.rem(me + step, count)
        copy_to(step).wait_send()
        pltpu.make_async_remote_copy(
            src_ref=send_ref.at[0],
            dst_ref=got_ref.at[source],
            send_sem=send_sems.at[step],
            recv_sem=recv_sems.at[source],
            device_id=(source // inner, lax.rem(source, inner)),
            device_id_type=MESH,
        ).wait_recv()
        return carry

    lax.fori_loop(1, count, finish, 0)


def exchange(tiles, sizes, scatter, collective_id):
    count = sizes[0] * sizes[1]
    return pl.pallas_call(
        functools.partial(exchange_kernel, sizes, scatter),
        out_shape=jax.ShapeDtypeStruct((count, 8, LANES), F32),
        in_specs=[pl.BlockSpec(memory_space=pltpu.VMEM)],
        out_specs=pl.BlockSpec(memory_space=pltpu.VMEM),
        scratch_shapes=[
            pltpu.SemaphoreType.DMA((count,)),
            pltpu.SemaphoreType.DMA((count,)),
        ],
        compiler_params=pltpu.CompilerParams(collective_id=collective_id, has_side_effects=True),
    )(tiles)


def turn(values, cosine, sine_low, sine_high):
    return (
        values * cosine
        + pltpu.roll(values, LANES - ROT // 2, 1) * sine_low
        + pltpu.roll(values, ROT // 2, 1) * sine_high
    )


def key_range(block, rows, widest):
    first = max(0, block * rows - widest)
    return first, (block + 1) * rows


def seen_weights(key_rows, query_cols, starts_row, first_key, first_query):
    scores = dot(key_rows, query_cols, NN)
    key_ids = first_key + lax.broadcasted_iota(jnp.int32, scores.shape, 0)
    query_ids = first_query + lax.broadcasted_iota(jnp.int32, scores.shape, 1)
    seen = (key_ids <= query_ids) & (key_ids >= starts_row)
    scores = jnp.where(seen, scores, -1e30)
    top = jnp.max(scores, axis=0, keepdims=True)
    weights = jnp.exp(scores - top)
    return weights, jnp.sum(weights, axis=0, keepdims=True)


def attend_back_kernel(
    rows, widest, q_in, k_in, v_in, g_in, cos, s_low, s_high, starts, g_out, b_out, kt, dk, dv
):
    seq_len = q_in.shape[0]
    cosine, sine_low, sine_high = cos[...], s_low[...], s_high[...]
    kt[...] = k_in[...].astype(F32).T.astype(BF16)
    dk[...] = jnp.zeros_like(dk)
    dv[...] = jnp.zeros_like(dv)
    for block in range(seq_len // rows):
        here = slice(block * rows, (block + 1) * rows)
        first, last = key_range(block, rows, widest)
        query_rows = (q_in[here, :].astype(F32) * HEAD**-0.5).astype(BF16)
        grad_rows = g_in[here, :]
        query_cols = query_rows.astype(F32).T.astype(BF16)
        grad_cols = grad_rows.astype(F32).T.astype(BF16)
        head_down = lax.broadcasted_iota(jnp.int32, query_cols.shape, 0) // HEAD
        head_along = lax.broadcasted_iota(jnp.int32, query_rows.shape, 1) // HEAD
        none_down, none_along = jnp.zeros_like(query_cols), jnp.zeros_like(query_rows)
        parts = []
        for head in range(LANES // HEAD):
            weights, total = seen_weights(
                k_in[first:last, :],
                jnp.where(head_down == head, query_cols, none_down),
                starts[:, here],
                first,
                block * rows,
            )
            probs = weights * (1.0 / total)
            grad_probs = dot(
                v_in[first:last, :], jnp.where(head_down == head, grad_cols, none_down), NN
            )
            inner = jnp.sum(probs * grad_probs, axis=0, keepdims=True)
            grad_scores = (probs * (grad_probs - inner)).astype(BF16)
            dk[first:last, :] += dot(
                grad_scores, jnp.where(head_along == head, query_rows, none_along), NN
            )
            dv[first:last, :] += dot(
                probs.astype(BF16), jnp.where(head_along == head, grad_rows, none_along), NN
            )
            parts.append(dot(kt[head * HEAD : (head + 1) * HEAD, first:last], grad_scores, NN))
        grad_queries = jnp.concatenate(parts, axis=0).T * HEAD**-0.5
        g_out[0, here, :] = turn(
            grad_queries, cosine[here, :], -sine_low[here, :], -sine_high[here, :]
        ).astype(BF16)
    g_out[1] = turn(dk[...], cosine, -sine_low, -sine_high).astype(BF16)
    g_out[2] = dv[...].astype(BF16)
    b_out[...] = jnp.sum(g_out[...].astype(F32), axis=1, keepdims=True)


def attend_backward(queries, key_vals, value_rows, grad_attended, tables, starts, widest):
    seq_len, width = queries.shape
    pairs = width // LANES
    rows = min(256, seq_len)
    column = pl.BlockSpec((seq_len, LANES), lambda i: (0, i))
    whole = lambda shape: pl.BlockSpec(shape, lambda i: (0, 0))
    return pl.pallas_call(
        functools.partial(attend_back_kernel, rows, widest),
        grid=(pairs,),
        in_specs=[column] * 4 + [whole((seq_len, LANES))] * 3 + [whole((1, seq_len))],
        out_specs=[
            pl.BlockSpec((3, seq_len, LANES), lambda i: (0, 0, i)),
            pl.BlockSpec((3, 1, LANES), lambda i: (0, 0, i)),
        ],
        out_shape=[
            jax.ShapeDtypeStruct((3, seq_len, width), BF16),
            jax.ShapeDtypeStruct((3, 1, width), F32),
        ],
        scratch_shapes=[
            pltpu.VMEM((LANES, seq_len), BF16),
            pltpu.VMEM((seq_len, LANES), F32),
            pltpu.VMEM((seq_len, LANES), F32),
        ],
        compiler_params=pltpu.CompilerParams(vmem_limit_bytes=48 * 2**20),
        cost_estimate=pl.CostEstimate(
            flops=10 * seq_len * seq_len * width, bytes_accessed=20 * seq_len * width, transcendentals=0
        ),
    )(queries, key_vals, value_rows, grad_attended, *tables, starts)


def xor(value, mask):
    bit = 1
    while bit <= mask:
        if mask & bit:
            value = value + bit * (1 - 2 * lax.rem(value // bit, 2))
        bit *= 2
    return value


class Places:
    def __init__(self, n_fsdp, n_tp):
        self.n_fsdp, self.n_tp = n_fsdp, n_tp
        self.f, self.t = lax.axis_index("fsdp"), lax.axis_index("tp")
        self.chip, self.core = self.f // 2, lax.rem(self.f, 2)

    def near_f(self, k):
        return xor(self.chip, k) * 2 + self.core

    def near(self, k):
        return (self.near_f(k), self.t)

    def sibling(self):
        return (self.chip * 2 + 1 - self.core, self.t)

    def along(self, t):
        return (self.f, t)

    def greet(self):
        barrier = pltpu.get_barrier_semaphore()
        partners = [self.near(k) for k in range(1, self.n_fsdp // 2)] + [self.sibling()]
        partners += [self.along(lax.rem(self.t + k, self.n_tp)) for k in range(1, self.n_tp)]
        for partner in partners:
            pl.semaphore_signal(barrier, inc=1, device_id=partner, device_id_type=MESH)
        pl.semaphore_wait(barrier, len(partners))


def send(src, dst, send_sem, recv_sem, device):
    return pltpu.make_async_remote_copy(
        src_ref=src,
        dst_ref=dst,
        send_sem=send_sem,
        recv_sem=recv_sem,
        device_id=device,
        device_id_type=MESH,
    )


class Line:
    def __init__(self, at, own, slots, send_sems, recv_sems):
        self.at, self.own, self.slots = at, own, slots
        self.send_sems, self.recv_sems = send_sems, recv_sems

    def copy(self, slot, way, first):
        at = self.at
        return send(
            self.own if first else self.slots.at[slot],
            self.slots.at[slot],
            self.send_sems.at[way, slot],
            self.recv_sems.at[slot],
            at.along(at.t + 1 - 2 * way),
        )

    def start(self):
        at = self.at
        pl.when(at.t < at.n_tp - 1)(lambda: self.copy(at.t, 0, True).start())
        pl.when(at.t > 0)(lambda: self.copy(at.t, 1, True).start())

    def step(self, s):
        at = self.at

        @pl.when(at.t >= s)
        def _():
            self.copy(at.t - s, 0, False).wait_recv()
            pl.when(at.t < at.n_tp - 1)(lambda: self.copy(at.t - s, 0, False).start())

        @pl.when(at.t + s < at.n_tp)
        def _():
            self.copy(at.t + s, 1, False).wait_recv()
            pl.when(at.t > 0)(lambda: self.copy(at.t + s, 1, False).start())

    def finish(self):
        at = self.at
        for s in range(at.n_tp):
            pl.when((at.t >= s) & (at.t < at.n_tp - 1))(
                lambda s=s: self.copy(at.t - s, 0, s == 0).wait_send()
            )
            pl.when((at.t + s < at.n_tp) & (at.t > 0))(
                lambda s=s: self.copy(at.t + s, 1, s == 0).wait_send()
            )


class Shards:
    def __init__(self, at, own, whole, by_rows, near_sems, sib_sems, index):
        self.at, self.own, self.whole, self.by_rows = at, own, whole, by_rows
        self.near_sems, self.sib_sems, self.index = near_sems, sib_sems, index
        self.half = at.n_fsdp // 2
        self.relay = at.n_fsdp == 8
        self.direct = [1, 2] if self.relay else list(range(1, self.half))

    def slot(self, f, part=None):
        if self.by_rows:
            rows = self.whole.shape[0] // self.at.n_fsdp
            first = f * rows
            if part is not None:
                rows = rows // 2
                first = first + part * rows
            return self.whole.at[pl.ds(pl.multiple_of(first, rows), rows), :]
        width = self.whole.shape[1] // self.at.n_fsdp
        columns = pl.ds(pl.multiple_of(f * width, LANES), width)
        if part is None:
            return self.whole.at[:, columns]
        rows = self.whole.shape[0] // 2
        return self.whole.at[pl.ds(part * rows, rows), columns]

    def near_copy(self, k):
        return send(
            self.own,
            self.slot(self.at.f),
            self.near_sems.at[self.index, 0, k],
            self.near_sems.at[self.index, 1, k],
            self.at.near(k),
        )

    def start(self):
        for k in self.direct:
            self.near_copy(k).start()
        self.sib_copy(0).start()

    def arrived(self, k):
        slot = self.slot(self.at.near_f(k))
        send(
            slot,
            slot,
            self.near_sems.at[self.index, 0, k],
            self.near_sems.at[self.index, 1, k],
            self.at.near(k),
        ).wait_recv()

    def relay_copy(self, part):
        source, target = (1, 2) if part == 0 else (2, 1)
        slot = self.slot(self.at.near_f(source), part)
        return send(
            slot,
            slot,
            self.near_sems.at[self.index, 0, 3 + part],
            self.near_sems.at[self.index, 1, 3 + part],
            self.at.near(target),
        )

    def sib_copy(self, k):
        f = self.at.near_f(k)
        return send(
            self.own if k == 0 else self.slot(f),
            self.slot(f),
            self.sib_sems.at[self.index, 0, k],
            self.sib_sems.at[self.index, 1, k],
            self.at.sibling(),
        )

    def pass_on(self):
        for k in self.direct:
            self.arrived(k)
            if self.relay:
                self.relay_copy(k - 1).start()
        for k in self.direct:
            self.sib_copy(k).start()

    def pass_last(self):
        if self.relay:
            for part in range(2):
                slot = self.slot(self.at.near_f(3), part)
                send(
                    slot,
                    slot,
                    self.near_sems.at[self.index, 0, 3 + part],
                    self.near_sems.at[self.index, 1, 3 + part],
                    self.at.near(2 - part),
                ).wait_recv()
            self.sib_copy(3).start()

    def complete(self):
        for k in range(self.half):
            f = xor(self.at.chip, k) * 2 + 1 - self.at.core
            slot = self.slot(f)
            send(
                slot,
                slot,
                self.sib_sems.at[self.index, 0, k],
                self.sib_sems.at[self.index, 1, k],
                self.at.sibling(),
            ).wait_recv()

    def finish(self):
        for k in self.direct:
            self.near_copy(k).wait_send()
        if self.relay:
            for part in range(2):
                self.relay_copy(part).wait_send()
        for k in range(self.half):
            self.sib_copy(k).wait_send()


def norm_rows(values, gain_row, shift_row):
    average = jnp.mean(values, axis=-1, keepdims=True)
    centred = values - average
    variance = jnp.mean(centred * centred, axis=-1, keepdims=True)
    return centred * lax.rsqrt(variance + NORM_EPS) * gain_row + shift_row


def front_kernel(
    sizes, widest,
    tok, cot, wq, wo, wgu, wd, tile, cos, s_low, s_high, starts,
    one, q_out, k_out, v_out, resid, two, rows_out, att_out, cot_all, wq_all, wo_all, wgu_all, wd_all,
    toks, wq_v, wo_v, att, heads, vt, small, bias,
    tok_send, tok_recv, cot_send, cot_recv, near_sems, sib_sems, wz_sems, small_sems,
    swap_send, swap_recv, local_sems,
):
    n_fsdp, n_tp = sizes
    half = n_fsdp // 2
    at = Places(n_fsdp, n_tp)
    slab, model = tok.shape
    width = q_out.shape[1]
    each = wo.shape[0]
    at.greet()

    line = Line(at, tok, toks, tok_send, tok_recv)
    line.start()
    grads = Line(at, cot, cot_all, cot_send, cot_recv)
    weights = [
        Shards(at, wq, wq_all, True, near_sems, sib_sems, 0),
        None,
        Shards(at, wgu, wgu_all, True, near_sems, sib_sems, 2),
        Shards(at, wd, wd_all, False, near_sems, sib_sems, 3),
    ]
    weights[1] = Shards(at, None, wo_all, False, near_sems, sib_sems, 1)
    weights[1].own = weights[1].slot(at.f)
    weights[0].start()

    own_columns = pl.ds(pl.multiple_of(at.f * (model // n_fsdp), LANES), model // n_fsdp)

    def wo_rows(t):
        return wo_all.at[pl.ds(pl.multiple_of(t * each, each), each), own_columns]

    def wo_copy(k):
        return send(wo, wo_rows(at.t), wz_sems.at[0, k], wz_sems.at[1, k], at.along(lax.rem(at.t + k, n_tp)))

    for k in range(1, n_tp):
        wo_copy(k).start()
    own_copies = [
        pltpu.make_async_copy(tok, toks.at[at.t], local_sems.at[0]),
        pltpu.make_async_copy(wq, weights[0].slot(at.f), local_sems.at[1]),
        pltpu.make_async_copy(wo, wo_rows(at.t), local_sems.at[2]),
        pltpu.make_async_copy(wgu, weights[2].slot(at.f), local_sems.at[3]),
        pltpu.make_async_copy(wd, weights[3].slot(at.f), local_sems.at[4]),
        pltpu.make_async_copy(cot, cot_all.at[at.t], local_sems.at[5]),
    ]
    for copy in own_copies:
        copy.start()

    small[at.t, at.f] = tile[...]
    mine = small.at[at.t, at.f]
    to_sib = send(mine, mine, small_sems.at[0, 0], small_sems.at[1, 0], at.sibling())
    to_sib.start()
    to_sib.wait()
    pair = small.at[at.t, pl.ds(at.chip * 2, 2)]
    to_near = [
        send(pair, pair, small_sems.at[0, k], small_sems.at[1, k], at.near(k)) for k in range(1, half)
    ]
    for copy in to_near:
        copy.start()
    for k in range(1, half):
        to_near[k - 1].wait_send()
        came = small.at[at.t, pl.ds(xor(at.chip, k) * 2, 2)]
        send(came, came, small_sems.at[0, k], small_sems.at[1, k], at.near(k)).wait_recv()
    plane = small.at[at.t]
    to_line = [
        send(
            plane, plane, small_sems.at[0, half + k], small_sems.at[1, half + k],
            at.along(lax.rem(at.t + k, n_tp)),
        )
        for k in range(1, n_tp)
    ]
    for copy in to_line:
        copy.start()
    for k in range(1, n_tp):
        to_line[k - 1].wait_send()
        came = small.at[lax.rem(at.t + n_tp - k, n_tp)]
        send(
            came, came, small_sems.at[0, half + k], small_sems.at[1, half + k],
            at.along(lax.rem(at.t + k, n_tp)),
        ).wait_recv()
    lanes_each = model // (n_fsdp * n_tp)
    group = LANES // lanes_each
    for i in range(model // LANES):
        total = jnp.zeros((8, LANES), F32)
        for j in range(group):
            linear = i * group + j
            total = total + pltpu.roll(small[linear % n_tp, linear // n_tp], j * lanes_each, 1)
        rows_out[:, i * LANES : (i + 1) * LANES] = total
    for i in range(width // LANES):
        total = jnp.zeros((8, LANES), F32)
        for j in range(group):
            total = total + pltpu.roll(small[at.t, i * group + j], j * lanes_each, 1)
        bias[:, i * LANES : (i + 1) * LANES] = total
    own_copies[0].wait()

    def normalise(slot):
        step = 32

        def some(i, carry):
            here = pl.ds(pl.multiple_of(i * step, step), step)
            one[slot, here, :] = norm_rows(
                toks[slot, here, :].astype(F32), rows_out[0:1, :], rows_out[2:3, :]
            ).astype(BF16)
            return carry

        lax.fori_loop(0, slab // step, some, 0)

    wide = 256

    def project(slot):
        here = pl.ds(pl.multiple_of(slot * slab, slab), slab)
        for part, out in enumerate((q_out, k_out, v_out)):

            def some(i, carry, part=part, out=out):
                values = dot(
                    one[slot], wq_v[:, pl.ds(pl.multiple_of(part * width + i * wide, wide), wide)], NN
                )
                for j in range(wide // LANES):
                    lanes = pl.ds(pl.multiple_of(i * wide + j * LANES, LANES), LANES)
                    piece = values[:, j * LANES : (j + 1) * LANES] + bias[4 + part : 5 + part, lanes]
                    if part < 2:
                        piece = turn(piece, cos[here, :], s_low[here, :], s_high[here, :])
                    out[here, lanes] = piece.astype(BF16)
                return carry

            lax.fori_loop(0, width // wide, some, 0)

    def each_from(first, last, work):
        def some(i, carry):
            s = (i + 1) // 2
            slot = at.t + s * (2 * lax.rem(i, 2) - 1)
            pl.when((slot >= 0) & (slot < n_tp))(lambda: work(slot))
            return carry

        lax.fori_loop(max(0, 2 * first - 1), 2 * last - 1, some, 0)

    normalise(at.t)
    for s in range(1, n_tp - 1):
        line.step(s)
        if s == 1:
            weights[0].pass_on()
            own_copies[2].wait()
            for k in range(1, n_tp):
                wo_copy(k).wait_send()
                came = wo_rows(lax.rem(at.t + n_tp - k, n_tp))
                send(came, came, wz_sems.at[0, k], wz_sems.at[1, k], at.along(at.t)).wait_recv()
            weights[1].start()
        each_from(s, s + 1, normalise)
    weights[0].pass_last()
    own_copies[1].wait()
    weights[0].complete()
    load = pltpu.make_async_copy(wq_all, wq_v, local_sems.at[6])
    load.start()
    load.wait()
    each_from(0, n_tp - 1, project)
    weights[1].pass_on()
    weights[2].start()
    weights[3].start()
    line.step(n_tp - 1)
    grads.start()
    each_from(n_tp - 1, n_tp, normalise)
    each_from(n_tp - 1, n_tp, project)

    def swap_copy(i, k):
        lanes = pl.ds(pl.multiple_of(i * LANES, LANES), LANES)
        columns = pl.ds(pl.multiple_of(at.t * width + i * LANES, LANES), LANES)
        other = lax.rem(at.t + k, n_tp)
        return send(
            heads.at[other, :, lanes], att.at[:, columns],
            swap_send.at[i, k], swap_recv.at[i, k], at.along(other),
        )

    def some_heads(i, carry):
        lanes = pl.ds(pl.multiple_of(i * LANES, LANES), LANES)
        attend(widest, q_out, k_out, v_out, starts, heads, vt, lanes, slab)
        for k in range(1, n_tp):
            swap_copy(i, k).start()
        columns = pl.ds(pl.multiple_of(at.t * width + i * LANES, LANES), LANES)
        att[:, columns] = heads[at.t, :, lanes]
        return carry

    lax.fori_loop(0, width // LANES, some_heads, 0)
    weights[1].pass_last()
    weights[1].complete()
    load = pltpu.make_async_copy(wo_all, wo_v, local_sems.at[7])
    load.start()

    def took_heads(i, carry):
        for k in range(1, n_tp):
            swap_copy(i, k).wait_send()
            source = lax.rem(at.t + n_tp - k, n_tp)
            came = att.at[:, pl.ds(pl.multiple_of(source * width + i * LANES, LANES), LANES)]
            send(came, came, swap_send.at[i, k], swap_recv.at[i, k], at.along(source)).wait_recv()
        return carry

    lax.fori_loop(0, width // LANES, took_heads, 0)
    grads.step(1)
    keep = pltpu.make_async_copy(att, att_out, local_sems.at[8])
    keep.start()
    load.wait()

    def out_columns(i, carry):
        here = pl.ds(pl.multiple_of(i * wide, wide), wide)
        resid[:, here] = toks[at.t, :, here].astype(F32) + dot(att[...], wo_v[:, here], NN)
        return carry

    lax.fori_loop(0, model // wide, out_columns, 0)

    def second_norm(i, carry):
        here = pl.ds(pl.multiple_of(i * 32, 32), 32)
        two[here, :] = norm_rows(resid[here, :], rows_out[1:2, :], rows_out[3:4, :]).astype(BF16)
        return carry

    lax.fori_loop(0, slab // 32, second_norm, 0)

    weights[2].pass_on()
    weights[3].pass_on()
    for s in range(2, n_tp):
        grads.step(s)
    weights[2].pass_last()
    weights[3].pass_last()
    for copy in own_copies[3:]:
        copy.wait()
    weights[2].complete()
    weights[3].complete()
    keep.wait()
    line.finish()
    grads.finish()
    for weight in weights:
        weight.finish()


def attend(widest, q_in, k_in, v_in, starts, heads, vt, lanes, slab):
    seq_len = q_in.shape[0]
    rows = min(256, seq_len)
    vt[...] = v_in[:, lanes].astype(F32).T.astype(BF16)
    for block in range(seq_len // rows):
        here = slice(block * rows, (block + 1) * rows)
        first, last = key_range(block, rows, widest)
        query_cols = (q_in[here, lanes].astype(F32) * HEAD**-0.5).T.astype(BF16)
        head_of = lax.broadcasted_iota(jnp.int32, query_cols.shape, 0) // HEAD
        parts = []
        for head in range(LANES // HEAD):
            own_cols = jnp.where(head_of == head, query_cols, jnp.zeros_like(query_cols))
            weights, total = seen_weights(
                k_in[first:last, lanes], own_cols, starts[:, here], first, block * rows
            )
            part = dot(vt[head * HEAD : (head + 1) * HEAD, first:last], weights.astype(BF16), NN)
            parts.append(part / total)
        found = jnp.concatenate(parts, axis=0).T.astype(BF16)
        for j in range(max(1, rows // slab)):
            count = min(slab, rows)
            row = block * rows + j * count
            heads[row // slab, row % slab : row % slab + count, lanes] = found[
                j * count : (j + 1) * count, :
            ]


def front(sizes, widest, tok, cot, wq, wo, wgu, wd, tile, tables, starts):
    n_fsdp, n_tp = sizes
    half = n_fsdp // 2
    slab, model = tok.shape
    seq_len = slab * n_tp
    width = wq.shape[1] // 3
    hidden = wd.shape[0]
    hbm = pl.BlockSpec(memory_space=pl.ANY)
    vmem = pl.BlockSpec(memory_space=pltpu.VMEM)
    shape = jax.ShapeDtypeStruct
    outs = [
        (shape((n_tp, slab, model), BF16), vmem),
        (shape((seq_len, width), BF16), vmem),
        (shape((seq_len, width), BF16), vmem),
        (shape((seq_len, width), BF16), vmem),
        (shape((slab, model), F32), vmem),
        (shape((slab, model), BF16), vmem),
        (shape((8, model), F32), vmem),
        (shape((slab, model), BF16), hbm),
        (shape((n_tp, slab, model), BF16), hbm),
        (shape((model, 3 * width), BF16), hbm),
        (shape((model, model), BF16), hbm),
        (shape((model, 2 * hidden), BF16), hbm),
        (shape((hidden, model), BF16), hbm),
    ]
    dma = pltpu.SemaphoreType.DMA
    pairs = width // LANES
    return pl.pallas_call(
        functools.partial(front_kernel, sizes, widest),
        in_specs=[hbm] * 6 + [vmem] * 5,
        out_specs=[spec for _, spec in outs],
        out_shape=[out for out, _ in outs],
        scratch_shapes=[
            pltpu.VMEM((n_tp, slab, model), BF16),
            pltpu.VMEM((model, 3 * width), BF16),
            pltpu.VMEM((model, model), BF16),
            pltpu.VMEM((slab, model), BF16),
            pltpu.VMEM((n_tp, slab, width), BF16),
            pltpu.VMEM((LANES, seq_len), BF16),
            pltpu.VMEM((n_tp, n_fsdp, 8, LANES), F32),
            pltpu.VMEM((8, width), F32),
            dma((2, n_tp)), dma((n_tp,)), dma((2, n_tp)), dma((n_tp,)),
            dma((4, 2, half + 1)), dma((4, 2, half)), dma((2, n_tp)), dma((2, half + n_tp)),
            dma((pairs, n_tp)), dma((pairs, n_tp)), dma((9,)),
        ],
        compiler_params=pltpu.CompilerParams(
            collective_id=1, has_side_effects=True, vmem_limit_bytes=60 * 2**20
        ),
        cost_estimate=pl.CostEstimate(flops=10**11, bytes_accessed=10**8, transcendentals=0),
    )(tok, cot, wq, wo, wgu, wd, tile, *tables, starts)


def hop(values, axis, size, partner):
    return lax.ppermute(values, axis, [(i, partner(i)) for i in range(size)])


def scatter_fsdp(blocks, size):
    me = lax.axis_index("fsdp")
    core, chip = me % 2, me // 2
    pairs = blocks.reshape((size // 2, 2) + blocks.shape[1:])
    mine = lax.dynamic_index_in_dim(pairs, core, 1, keepdims=False)
    other = lax.dynamic_index_in_dim(pairs, 1 - core, 1, keepdims=False)
    got = hop(other, "fsdp", size, lambda i: i ^ 1)
    sums = (mine.astype(F32) + got.astype(F32)).astype(BF16)
    total = lax.dynamic_index_in_dim(sums, chip, 0, keepdims=False).astype(F32)
    for k in range(1, size // 2):
        block = lax.dynamic_index_in_dim(sums, chip ^ k, 0, keepdims=False)
        total = total + hop(block, "fsdp", size, lambda i, k=k: i ^ (2 * k)).astype(F32)
    return total


def swap_tp(blocks, size):
    me = lax.axis_index("tp")
    got = blocks
    for k in range(1, size):
        block = lax.dynamic_index_in_dim(blocks, (me + k) % size, 0, keepdims=False)
        came = hop(block, "tp", size, lambda i, k=k: (i + k) % size)
        got = lax.dynamic_update_index_in_dim(got, came, (me + size - k) % size, 0)
    return got


def gather_rows(values):
    return lax.all_gather(values, "tp", axis=0, tiled=True)


def reduce_rows(values):
    return lax.psum_scatter(values.astype(BF16), "tp", scatter_dimension=0, tiled=True).astype(F32)


def local(tokens, lengths, ln_gains, ln_shifts, w_qkv, b_qkv, w_out, w_gate_up, w_down, cotangent):
    n_fsdp, n_tp = lax.axis_size("fsdp"), lax.axis_size("tp")
    sizes = (n_fsdp, n_tp)
    at_tp = lax.axis_index("tp")
    slab_rows, model_width = tokens.shape
    seq_len = slab_rows * n_tp
    small = ln_gains.shape[1]
    local_width = w_qkv.shape[2]
    hidden_width = w_gate_up.shape[2]
    part_rows = w_qkv.shape[0]

    length_row = lengths[0]
    doc_ends = jnp.cumsum(length_row)
    ids = jnp.arange(seq_len, dtype=jnp.int32)
    passed = (doc_ends[None, :] <= ids[:, None]).astype(jnp.int32)
    starts = jnp.sum(passed * length_row[None, :], axis=1)
    places = (ids - starts).astype(F32)
    lane = jnp.arange(LANES, dtype=jnp.int32) % HEAD
    frequency = 10000.0 ** (-2.0 * (lane % (ROT // 2)).astype(F32) / ROT)
    angles = places[:, None] * frequency[None, :]
    cosine = jnp.where(lane[None] < ROT, jnp.cos(angles), 1.0)
    sine = jnp.sin(angles)
    sine_low = jnp.where(lane[None] < ROT // 2, -sine, 0.0)
    sine_high = jnp.where((lane[None] >= ROT // 2) & (lane[None] < ROT), sine, 0.0)
    tables = (cosine, sine_low, sine_high)
    starts_row = starts.reshape(1, seq_len).astype(jnp.int32)
    widest = seq_len // 2

    tile = jnp.concatenate([ln_gains, ln_shifts, b_qkv.astype(F32), jnp.zeros((1, small), F32)], 0)
    tile = jnp.pad(tile, ((0, 0), (0, LANES - small)))
    token_rows = tokens.astype(F32)
    (
        full_one, queries, key_vals, value_rows, residual, normed_two, norm_rows_all, attended_own,
        grad_branch, qkv_all, out_all, gu_all, down_all,
    ) = front(
        sizes, widest, tokens, cotangent, w_qkv.reshape(part_rows, 3 * local_width), w_out,
        w_gate_up.reshape(part_rows, 2 * hidden_width), w_down, tile, tables, starts_row,
    )
    full_one = full_one.reshape(seq_len, model_width)
    grad_branch = grad_branch.reshape(seq_len, model_width)
    gains_all, shifts_all = norm_rows_all[0:2], norm_rows_all[2:4]

    full_two = gather_rows(normed_two)
    gate_up = dot(full_two, gu_all, NN)
    gate, up = gate_up[:, :hidden_width], gate_up[:, hidden_width:]
    hidden_low = swiglu(gate, up).astype(BF16)
    branch = reduce_rows(dot(hidden_low, down_all, NN))
    result = (residual + branch).astype(BF16)
    grad_out = cotangent.astype(F32)
    grad_hidden = dot(grad_branch, down_all, NT)
    _, swiglu_pull = jax.vjp(swiglu, gate, up)
    grad_gate, grad_up = swiglu_pull(grad_hidden)
    grad_gate_up = jnp.concatenate([grad_gate, grad_up], axis=1).astype(BF16)
    grad_normed_two = reduce_rows(dot(grad_gate_up, gu_all, NT))
    grad_gu = dot(full_two, grad_gate_up, TN).astype(BF16)
    grad_down = dot(grad_branch, hidden_low, TN).astype(BF16)
    gu_share = scatter_fsdp(grad_gu.reshape(n_fsdp, part_rows, 2 * hidden_width), n_fsdp)
    down_share = scatter_fsdp(grad_down.reshape(n_fsdp, part_rows, hidden_width), n_fsdp)
    _, second_pull = jax.vjp(layer_norm, residual, gains_all[1], shifts_all[1])
    grad_resid_norm, grad_gain_two, grad_shift_two = second_pull(grad_normed_two)
    grad_residual = grad_out + grad_resid_norm

    grad_attn = grad_residual.astype(BF16)
    grad_o = dot(grad_attn, attended_own, TN).astype(BF16)
    grad_attended_own = dot(grad_attn, out_all, NT).astype(BF16)
    grad_attended = swap_tp(
        grad_attended_own.reshape(slab_rows, n_tp, local_width).transpose(1, 0, 2), n_tp
    ).reshape(seq_len, local_width)
    grad_projected, grad_bias = attend_backward(
        queries, key_vals, value_rows, grad_attended, tables, starts_row, widest
    )
    grad_projected = grad_projected.transpose(1, 0, 2).reshape(seq_len, 3 * local_width)
    grad_qkv = dot(full_one, grad_projected, TN).astype(BF16)
    grad_normed_one = reduce_rows(dot(grad_projected, qkv_all, NT))
    _, first_pull = jax.vjp(layer_norm, token_rows, gains_all[0], shifts_all[0])
    grad_token_norm, grad_gain_one, grad_shift_one = first_pull(grad_normed_one)
    grad_tokens = grad_residual + grad_token_norm

    out_share = scatter_fsdp(grad_o.reshape(n_fsdp, part_rows, model_width), n_fsdp).astype(BF16)
    out_share = jnp.sum(
        swap_tp(out_share.reshape(part_rows, n_tp, local_width).transpose(1, 0, 2), n_tp).astype(F32),
        axis=0,
    ).T
    qkv_share = scatter_fsdp(grad_qkv.reshape(n_fsdp, part_rows, 3 * local_width), n_fsdp)

    count = n_fsdp * n_tp
    norm_grads = jnp.stack([grad_gain_one, grad_gain_two, grad_shift_one, grad_shift_two])
    norm_grads = norm_grads.reshape(4, count, small).transpose(1, 0, 2)
    bias_grads = grad_bias.reshape(3, n_fsdp, small).transpose(1, 0, 2)
    bias_grads = jnp.where(
        (jnp.arange(n_tp) == at_tp)[None, :, None, None], bias_grads[:, None], 0.0
    ).reshape(count, 3, small)
    tiles = jnp.concatenate([norm_grads, bias_grads, jnp.zeros((count, 1, small), F32)], axis=1)
    tiles = jnp.pad(tiles, ((0, 0), (0, 0), (0, LANES - small)))
    shares = jnp.sum(exchange(tiles, sizes, True, 2), axis=0)[:, :small]

    return (
        result,
        grad_tokens,
        shares[0:2],
        shares[2:4],
        qkv_share.reshape(part_rows, 3, local_width),
        shares[4:7],
        out_share,
        gu_share.reshape(part_rows, 2, hidden_width),
        down_share.T,
    )


def solution(mesh):
    placed = (
        P(("fsdp", "tp"), None),
        P("fsdp", None),
        P(None, ("fsdp", "tp")),
        P(None, ("fsdp", "tp")),
        P("fsdp", None, "tp"),
        P(None, ("tp", "fsdp")),
        P("tp", "fsdp"),
        P("fsdp", None, "tp"),
        P("tp", "fsdp"),
        P(("fsdp", "tp"), None),
    )
    return jax.shard_map(
        local,
        mesh=mesh,
        in_specs=placed,
        out_specs=(
            P(("fsdp", "tp"), None),
            P(("fsdp", "tp"), None),
            P(None, ("fsdp", "tp")),
            P(None, ("fsdp", "tp")),
            P("fsdp", None, "tp"),
            P(None, ("tp", "fsdp")),
            P("tp", "fsdp"),
            P("fsdp", None, "tp"),
            P("tp", "fsdp"),
        ),
        check_vma=False,
    )
```

```python
import functools

import jax
import jax.numpy as jnp
from jax import lax
from jax.experimental import pallas as pl
from jax.experimental.pallas import tpu as pltpu
from jax.sharding import PartitionSpec as P

HEAD = 64
ROT = 16
NORM_EPS = 1e-05
LANES = 128
MESH = pl.DeviceIdType.MESH
NN = (((1,), (0,)), ((), ()))
NT = (((1,), (1,)), ((), ()))
TN = (((0,), (0,)), ((), ()))
F32 = jnp.float32
BF16 = jnp.bfloat16


def dot(left, right, dims):
    return lax.dot_general(left, right, dims, preferred_element_type=F32)


def turn(values, cosine, sine_low, sine_high):
    return (
        values * cosine
        + pltpu.roll(values, LANES - ROT // 2, 1) * sine_low
        + pltpu.roll(values, ROT // 2, 1) * sine_high
    )


def key_range(block, rows, widest):
    first = max(0, block * rows - widest)
    return first, (block + 1) * rows


def seen_weights(key_rows, query_cols, starts_row, first_key, first_query):
    scores = dot(key_rows, query_cols, NN)
    key_ids = first_key + lax.broadcasted_iota(jnp.int32, scores.shape, 0)
    query_ids = first_query + lax.broadcasted_iota(jnp.int32, scores.shape, 1)
    seen = (key_ids <= query_ids) & (key_ids >= starts_row)
    scores = jnp.where(seen, scores, -1e30)
    top = jnp.max(scores, axis=0, keepdims=True)
    weights = jnp.exp(scores - top)
    return weights, jnp.sum(weights, axis=0, keepdims=True)


def xor(value, mask):
    bit = 1
    while bit <= mask:
        if mask & bit:
            value = value + bit * (1 - 2 * lax.rem(value // bit, 2))
        bit *= 2
    return value


class Places:
    def __init__(self, n_fsdp, n_tp):
        self.n_fsdp, self.n_tp = n_fsdp, n_tp
        self.f, self.t = lax.axis_index("fsdp"), lax.axis_index("tp")
        self.chip, self.core = self.f // 2, lax.rem(self.f, 2)

    def near_f(self, k):
        return xor(self.chip, k) * 2 + self.core

    def near(self, k):
        return (self.near_f(k), self.t)

    def sibling(self):
        return (self.chip * 2 + 1 - self.core, self.t)

    def along(self, t):
        return (self.f, t)

    def greet(self):
        barrier = pltpu.get_barrier_semaphore()
        partners = [self.near(k) for k in range(1, self.n_fsdp // 2)] + [self.sibling()]
        partners += [self.along(lax.rem(self.t + k, self.n_tp)) for k in range(1, self.n_tp)]
        for partner in partners:
            pl.semaphore_signal(barrier, inc=1, device_id=partner, device_id_type=MESH)
        pl.semaphore_wait(barrier, len(partners))


def send(src, dst, send_sem, recv_sem, device):
    return pltpu.make_async_remote_copy(
        src_ref=src,
        dst_ref=dst,
        send_sem=send_sem,
        recv_sem=recv_sem,
        device_id=device,
        device_id_type=MESH,
    )


class Line:
    def __init__(self, at, own, slots, send_sems, recv_sems):
        self.at, self.own, self.slots = at, own, slots
        self.send_sems, self.recv_sems = send_sems, recv_sems

    def copy(self, slot, way, first):
        at = self.at
        return send(
            self.own if first else self.slots.at[slot],
            self.slots.at[slot],
            self.send_sems.at[way, slot],
            self.recv_sems.at[slot],
            at.along(at.t + 1 - 2 * way),
        )

    def start(self):
        at = self.at
        pl.when(at.t < at.n_tp - 1)(lambda: self.copy(at.t, 0, True).start())
        pl.when(at.t > 0)(lambda: self.copy(at.t, 1, True).start())

    def step(self, s):
        at = self.at

        @pl.when(at.t >= s)
        def _():
            self.copy(at.t - s, 0, False).wait_recv()
            pl.when(at.t < at.n_tp - 1)(lambda: self.copy(at.t - s, 0, False).start())

        @pl.when(at.t + s < at.n_tp)
        def _():
            self.copy(at.t + s, 1, False).wait_recv()
            pl.when(at.t > 0)(lambda: self.copy(at.t + s, 1, False).start())

    def finish(self):
        at = self.at
        for s in range(at.n_tp):
            pl.when((at.t >= s) & (at.t < at.n_tp - 1))(
                lambda s=s: self.copy(at.t - s, 0, s == 0).wait_send()
            )
            pl.when((at.t + s < at.n_tp) & (at.t > 0))(
                lambda s=s: self.copy(at.t + s, 1, s == 0).wait_send()
            )


class Shards:
    def __init__(self, at, own, whole, by_rows, near_sems, sib_sems, index):
        self.at, self.own, self.whole, self.by_rows = at, own, whole, by_rows
        self.near_sems, self.sib_sems, self.index = near_sems, sib_sems, index
        self.half = at.n_fsdp // 2
        self.relay = at.n_fsdp == 8
        self.direct = [1, 2] if self.relay else list(range(1, self.half))

    def slot(self, f, part=None):
        if self.by_rows:
            rows = self.whole.shape[-2] // self.at.n_fsdp
            first = f * rows
            if part is not None:
                rows = rows // 2
                first = first + part * rows
            here = pl.ds(pl.multiple_of(first, rows), rows)
            return self.whole.at[:, here, :] if len(self.whole.shape) == 3 else self.whole.at[here, :]
        width = self.whole.shape[1] // self.at.n_fsdp
        columns = pl.ds(pl.multiple_of(f * width, LANES), width)
        if part is None:
            return self.whole.at[:, columns]
        rows = self.whole.shape[0] // 2
        return self.whole.at[pl.ds(part * rows, rows), columns]

    def near_copy(self, k):
        return send(
            self.own,
            self.slot(self.at.f),
            self.near_sems.at[self.index, 0, k],
            self.near_sems.at[self.index, 1, k],
            self.at.near(k),
        )

    def start(self):
        for k in self.direct:
            self.near_copy(k).start()
        self.sib_copy(0).start()

    def arrived(self, k):
        slot = self.slot(self.at.near_f(k))
        send(
            slot,
            slot,
            self.near_sems.at[self.index, 0, k],
            self.near_sems.at[self.index, 1, k],
            self.at.near(k),
        ).wait_recv()

    def relay_copy(self, part):
        source, target = (1, 2) if part == 0 else (2, 1)
        slot = self.slot(self.at.near_f(source), part)
        return send(
            slot,
            slot,
            self.near_sems.at[self.index, 0, 3 + part],
            self.near_sems.at[self.index, 1, 3 + part],
            self.at.near(target),
        )

    def sib_copy(self, k):
        f = self.at.near_f(k)
        return send(
            self.own if k == 0 else self.slot(f),
            self.slot(f),
            self.sib_sems.at[self.index, 0, k],
            self.sib_sems.at[self.index, 1, k],
            self.at.sibling(),
        )

    def pass_on(self):
        for k in self.direct:
            self.arrived(k)
            if self.relay:
                self.relay_copy(k - 1).start()
        for k in self.direct:
            self.sib_copy(k).start()

    def pass_last(self):
        if self.relay:
            for part in range(2):
                slot = self.slot(self.at.near_f(3), part)
                send(
                    slot,
                    slot,
                    self.near_sems.at[self.index, 0, 3 + part],
                    self.near_sems.at[self.index, 1, 3 + part],
                    self.at.near(2 - part),
                ).wait_recv()
            self.sib_copy(3).start()

    def complete(self):
        for k in range(self.half):
            f = xor(self.at.chip, k) * 2 + 1 - self.at.core
            slot = self.slot(f)
            send(
                slot,
                slot,
                self.sib_sems.at[self.index, 0, k],
                self.sib_sems.at[self.index, 1, k],
                self.at.sibling(),
            ).wait_recv()

    def finish(self):
        for k in self.direct:
            self.near_copy(k).wait_send()
        if self.relay:
            for part in range(2):
                self.relay_copy(part).wait_send()
        for k in range(self.half):
            self.sib_copy(k).wait_send()


def norm_rows(values, gain_row, shift_row):
    average = jnp.mean(values, axis=-1, keepdims=True)
    centred = values - average
    variance = jnp.mean(centred * centred, axis=-1, keepdims=True)
    return centred * lax.rsqrt(variance + NORM_EPS) * gain_row + shift_row


def front_kernel(
    sizes, widest,
    tok, cot, wq, wo, wgu, wd, tile, cos, s_low, s_high, starts,
    one, q_out, k_out, v_out, resid, two, rows_out, att_out, cot_all, wq_all, wo_all, wgu_all, wd_all,
    toks, wq_v, wo_v, att, heads, vt, small, bias,
    tok_send, tok_recv, cot_send, cot_recv, near_sems, sib_sems, wz_sems, small_sems,
    swap_send, swap_recv, local_sems,
):
    n_fsdp, n_tp = sizes
    half = n_fsdp // 2
    at = Places(n_fsdp, n_tp)
    slab, model = tok.shape
    width = q_out.shape[1]
    each = wo.shape[0]
    at.greet()

    line = Line(at, tok, toks, tok_send, tok_recv)
    line.start()
    grads = Line(at, cot, cot_all, cot_send, cot_recv)
    weights = [
        Shards(at, wq, wq_all, True, near_sems, sib_sems, 0),
        None,
        Shards(at, wgu, wgu_all, True, near_sems, sib_sems, 2),
        Shards(at, wd, wd_all, False, near_sems, sib_sems, 3),
    ]
    weights[1] = Shards(at, None, wo_all, False, near_sems, sib_sems, 1)
    weights[1].own = weights[1].slot(at.f)
    weights[0].start()

    own_columns = pl.ds(pl.multiple_of(at.f * (model // n_fsdp), LANES), model // n_fsdp)

    def wo_rows(t):
        return wo_all.at[pl.ds(pl.multiple_of(t * each, each), each), own_columns]

    def wo_copy(k):
        return send(wo, wo_rows(at.t), wz_sems.at[0, k], wz_sems.at[1, k], at.along(lax.rem(at.t + k, n_tp)))

    for k in range(1, n_tp):
        wo_copy(k).start()
    own_copies = [
        pltpu.make_async_copy(tok, toks.at[at.t], local_sems.at[0]),
        pltpu.make_async_copy(wq, weights[0].slot(at.f), local_sems.at[1]),
        pltpu.make_async_copy(wo, wo_rows(at.t), local_sems.at[2]),
        pltpu.make_async_copy(wgu, weights[2].slot(at.f), local_sems.at[3]),
        pltpu.make_async_copy(wd, weights[3].slot(at.f), local_sems.at[4]),
        pltpu.make_async_copy(cot, cot_all.at[at.t], local_sems.at[5]),
    ]
    for copy in own_copies:
        copy.start()

    small[at.t, at.f] = tile[...]
    mine = small.at[at.t, at.f]
    to_sib = send(mine, mine, small_sems.at[0, 0], small_sems.at[1, 0], at.sibling())
    to_sib.start()
    to_sib.wait()
    pair = small.at[at.t, pl.ds(at.chip * 2, 2)]
    to_near = [
        send(pair, pair, small_sems.at[0, k], small_sems.at[1, k], at.near(k)) for k in range(1, half)
    ]
    for copy in to_near:
        copy.start()
    for k in range(1, half):
        to_near[k - 1].wait_send()
        came = small.at[at.t, pl.ds(xor(at.chip, k) * 2, 2)]
        send(came, came, small_sems.at[0, k], small_sems.at[1, k], at.near(k)).wait_recv()
    plane = small.at[at.t]
    to_line = [
        send(
            plane, plane, small_sems.at[0, half + k], small_sems.at[1, half + k],
            at.along(lax.rem(at.t + k, n_tp)),
        )
        for k in range(1, n_tp)
    ]
    for copy in to_line:
        copy.start()
    for k in range(1, n_tp):
        to_line[k - 1].wait_send()
        came = small.at[lax.rem(at.t + n_tp - k, n_tp)]
        send(
            came, came, small_sems.at[0, half + k], small_sems.at[1, half + k],
            at.along(lax.rem(at.t + k, n_tp)),
        ).wait_recv()
    lanes_each = model // (n_fsdp * n_tp)
    group = LANES // lanes_each
    for i in range(model // LANES):
        total = jnp.zeros((8, LANES), F32)
        for j in range(group):
            linear = i * group + j
            total = total + pltpu.roll(small[linear % n_tp, linear // n_tp], j * lanes_each, 1)
        rows_out[:, i * LANES : (i + 1) * LANES] = total
    for i in range(width // LANES):
        total = jnp.zeros((8, LANES), F32)
        for j in range(group):
            total = total + pltpu.roll(small[at.t, i * group + j], j * lanes_each, 1)
        bias[:, i * LANES : (i + 1) * LANES] = total
    own_copies[0].wait()

    def normalise(slot):
        step = 32

        def some(i, carry):
            here = pl.ds(pl.multiple_of(i * step, step), step)
            one[slot, here, :] = norm_rows(
                toks[slot, here, :].astype(F32), rows_out[0:1, :], rows_out[2:3, :]
            ).astype(BF16)
            return carry

        lax.fori_loop(0, slab // step, some, 0)

    wide = 256

    def project(slot):
        here = pl.ds(pl.multiple_of(slot * slab, slab), slab)
        for part, out in enumerate((q_out, k_out, v_out)):

            def some(i, carry, part=part, out=out):
                values = dot(
                    one[slot], wq_v[:, pl.ds(pl.multiple_of(part * width + i * wide, wide), wide)], NN
                )
                for j in range(wide // LANES):
                    lanes = pl.ds(pl.multiple_of(i * wide + j * LANES, LANES), LANES)
                    piece = values[:, j * LANES : (j + 1) * LANES] + bias[4 + part : 5 + part, lanes]
                    if part < 2:
                        piece = turn(piece, cos[here, :], s_low[here, :], s_high[here, :])
                    out[here, lanes] = piece.astype(BF16)
                return carry

            lax.fori_loop(0, width // wide, some, 0)

    def each_from(first, last, work):
        def some(i, carry):
            s = (i + 1) // 2
            slot = at.t + s * (2 * lax.rem(i, 2) - 1)
            pl.when((slot >= 0) & (slot < n_tp))(lambda: work(slot))
            return carry

        lax.fori_loop(max(0, 2 * first - 1), 2 * last - 1, some, 0)

    normalise(at.t)
    for s in range(1, n_tp - 1):
        line.step(s)
        if s == 1:
            weights[0].pass_on()
            own_copies[2].wait()
            for k in range(1, n_tp):
                wo_copy(k).wait_send()
                came = wo_rows(lax.rem(at.t + n_tp - k, n_tp))
                send(came, came, wz_sems.at[0, k], wz_sems.at[1, k], at.along(at.t)).wait_recv()
            weights[1].start()
        each_from(s, s + 1, normalise)
    weights[0].pass_last()
    own_copies[1].wait()
    weights[0].complete()
    load = pltpu.make_async_copy(wq_all, wq_v, local_sems.at[6])
    load.start()
    load.wait()
    each_from(0, n_tp - 1, project)
    weights[1].pass_on()
    weights[2].start()
    weights[3].start()
    line.step(n_tp - 1)
    grads.start()
    each_from(n_tp - 1, n_tp, normalise)
    each_from(n_tp - 1, n_tp, project)

    def swap_copy(i, k):
        lanes = pl.ds(pl.multiple_of(i * LANES, LANES), LANES)
        columns = pl.ds(pl.multiple_of(at.t * width + i * LANES, LANES), LANES)
        other = lax.rem(at.t + k, n_tp)
        return send(
            heads.at[other, :, lanes], att.at[:, columns],
            swap_send.at[i, k], swap_recv.at[i, k], at.along(other),
        )

    def some_heads(i, carry):
        lanes = pl.ds(pl.multiple_of(i * LANES, LANES), LANES)
        attend(widest, q_out, k_out, v_out, starts, heads, vt, lanes, slab)
        for k in range(1, n_tp):
            swap_copy(i, k).start()
        columns = pl.ds(pl.multiple_of(at.t * width + i * LANES, LANES), LANES)
        att[:, columns] = heads[at.t, :, lanes]
        return carry

    lax.fori_loop(0, width // LANES, some_heads, 0)
    weights[1].pass_last()
    weights[1].complete()
    load = pltpu.make_async_copy(wo_all, wo_v, local_sems.at[7])
    load.start()

    def took_heads(i, carry):
        for k in range(1, n_tp):
            swap_copy(i, k).wait_send()
            source = lax.rem(at.t + n_tp - k, n_tp)
            came = att.at[:, pl.ds(pl.multiple_of(source * width + i * LANES, LANES), LANES)]
            send(came, came, swap_send.at[i, k], swap_recv.at[i, k], at.along(source)).wait_recv()
        return carry

    lax.fori_loop(0, width // LANES, took_heads, 0)
    grads.step(1)
    keep = pltpu.make_async_copy(att, att_out, local_sems.at[8])
    keep.start()
    load.wait()

    def out_columns(i, carry):
        here = pl.ds(pl.multiple_of(i * wide, wide), wide)
        resid[:, here] = toks[at.t, :, here].astype(F32) + dot(att[...], wo_v[:, here], NN)
        return carry

    lax.fori_loop(0, model // wide, out_columns, 0)

    def second_norm(i, carry):
        here = pl.ds(pl.multiple_of(i * 32, 32), 32)
        two[here, :] = norm_rows(resid[here, :], rows_out[1:2, :], rows_out[3:4, :]).astype(BF16)
        return carry

    lax.fori_loop(0, slab // 32, second_norm, 0)

    weights[2].pass_on()
    weights[3].pass_on()
    for s in range(2, n_tp):
        grads.step(s)
    weights[2].pass_last()
    weights[3].pass_last()
    for copy in own_copies[3:]:
        copy.wait()
    weights[2].complete()
    weights[3].complete()
    keep.wait()
    line.finish()
    grads.finish()
    for weight in weights:
        weight.finish()


def attend(widest, q_in, k_in, v_in, starts, heads, vt, lanes, slab):
    seq_len = q_in.shape[0]
    rows = min(256, seq_len)
    vt[...] = v_in[:, lanes].astype(F32).T.astype(BF16)
    for block in range(seq_len // rows):
        here = slice(block * rows, (block + 1) * rows)
        first, last = key_range(block, rows, widest)
        query_cols = (q_in[here, lanes].astype(F32) * HEAD**-0.5).T.astype(BF16)
        head_of = lax.broadcasted_iota(jnp.int32, query_cols.shape, 0) // HEAD
        parts = []
        for head in range(LANES // HEAD):
            own_cols = jnp.where(head_of == head, query_cols, jnp.zeros_like(query_cols))
            weights, total = seen_weights(
                k_in[first:last, lanes], own_cols, starts[:, here], first, block * rows
            )
            part = dot(vt[head * HEAD : (head + 1) * HEAD, first:last], weights.astype(BF16), NN)
            parts.append(part / total)
        found = jnp.concatenate(parts, axis=0).T.astype(BF16)
        for j in range(max(1, rows // slab)):
            count = min(slab, rows)
            row = block * rows + j * count
            heads[row // slab, row % slab : row % slab + count, lanes] = found[
                j * count : (j + 1) * count, :
            ]


def front(sizes, widest, tok, cot, wq, wo, wgu, wd, tile, tables, starts):
    n_fsdp, n_tp = sizes
    half = n_fsdp // 2
    slab, model = tok.shape
    seq_len = slab * n_tp
    width = wq.shape[1] // 3
    hidden = wd.shape[0]
    hbm = pl.BlockSpec(memory_space=pl.ANY)
    vmem = pl.BlockSpec(memory_space=pltpu.VMEM)
    shape = jax.ShapeDtypeStruct
    outs = [
        (shape((n_tp, slab, model), BF16), vmem),
        (shape((seq_len, width), BF16), vmem),
        (shape((seq_len, width), BF16), vmem),
        (shape((seq_len, width), BF16), vmem),
        (shape((slab, model), F32), vmem),
        (shape((slab, model), BF16), vmem),
        (shape((8, model), F32), vmem),
        (shape((slab, model), BF16), hbm),
        (shape((n_tp, slab, model), BF16), hbm),
        (shape((model, 3 * width), BF16), hbm),
        (shape((model, model), BF16), hbm),
        (shape((2, model, hidden), BF16), hbm),
        (shape((hidden, model), BF16), hbm),
    ]
    dma = pltpu.SemaphoreType.DMA
    pairs = width // LANES
    return pl.pallas_call(
        functools.partial(front_kernel, sizes, widest),
        in_specs=[vmem] * 11,
        out_specs=[spec for _, spec in outs],
        out_shape=[out for out, _ in outs],
        scratch_shapes=[
            pltpu.VMEM((n_tp, slab, model), BF16),
            pltpu.VMEM((model, 3 * width), BF16),
            pltpu.VMEM((model, model), BF16),
            pltpu.VMEM((slab, model), BF16),
            pltpu.VMEM((n_tp, slab, width), BF16),
            pltpu.VMEM((LANES, seq_len), BF16),
            pltpu.VMEM((n_tp, n_fsdp, 8, LANES), F32),
            pltpu.VMEM((8, width), F32),
            dma((2, n_tp)), dma((n_tp,)), dma((2, n_tp)), dma((n_tp,)),
            dma((4, 2, half + 1)), dma((4, 2, half)), dma((2, n_tp)), dma((2, half + n_tp)),
            dma((pairs, n_tp)), dma((pairs, n_tp)), dma((9,)),
        ],
        compiler_params=pltpu.CompilerParams(
            collective_id=1, has_side_effects=True, vmem_limit_bytes=60 * 2**20
        ),
        cost_estimate=pl.CostEstimate(flops=10**11, bytes_accessed=10**8, transcendentals=0),
    )(tok, cot, wq, wo, wgu, wd, tile, *tables, starts)


def xor_any(value, mask, bits):
    total = 0
    for b in range(bits):
        both = lax.rem(value // 2**b, 2) + lax.rem(mask // 2**b, 2)
        total = total + lax.rem(both, 2) * 2**b
    return total


class Fold:
    def __init__(self, at, total, going, came, tile, send_sems, recv_sems):
        self.at, self.total, self.going, self.came, self.tile = at, total, going, came, tile
        self.send_sems, self.recv_sems = send_sems, recv_sems
        self.tiles = total.shape[1] // tile

    def lanes(self, c):
        return pl.ds(pl.multiple_of(c * self.tile, self.tile), self.tile)

    def copy(self, j, c, way):
        at = self.at
        slot = j if way == 0 else j + (at.n_tp - j) * lax.max(0, j - at.t + 2)
        return send(
            self.going.at[j, :, self.lanes(c)],
            self.came.at[slot, :, self.lanes(c)],
            self.send_sems.at[j, c],
            self.recv_sems.at[slot, c],
            at.along(at.t + 1 - 2 * way),
        )

    def put(self, j, c, values):
        at = self.at

        @pl.when(j == at.t)
        def _():
            self.total[:, self.lanes(c)] = values

        @pl.when(j != at.t)
        def _():
            self.going[j, :, self.lanes(c)] = values.astype(BF16)

        pl.when((j > at.t) & (at.t == 0))(lambda: self.copy(j, c, 0).start())
        pl.when((j < at.t) & (at.t == at.n_tp - 1))(lambda: self.copy(j, c, 1).start())

    def arrived(self, slot, c):
        tile = self.came.at[slot, :, self.lanes(c)]
        send(
            tile, tile, self.send_sems.at[0, c], self.recv_sems.at[slot, c], self.at.along(self.at.t)
        ).wait_recv()

    def forward(self, key, c):
        at = self.at

        def some(j, way):
            self.arrived(j, c)
            here = self.lanes(c)
            self.going[j, :, here] = (
                self.going[j, :, here].astype(F32) + self.came[j, :, here].astype(F32)
            ).astype(BF16)
            self.copy(j, c, way).start()

        pl.when((key > at.t) & (at.t > 0))(lambda: some(key, 0))
        down = at.n_tp - 1 - key
        pl.when((down < at.t) & (at.t < at.n_tp - 1))(lambda: some(down, 1))

    def end(self):
        at = self.at

        def some(c, carry):
            here = self.lanes(c)

            @pl.when(at.t > 0)
            def _():
                self.arrived(at.t, c)
                self.total[:, here] = self.total[:, here] + self.came[at.t, :, here].astype(F32)

            @pl.when(at.t < at.n_tp - 1)
            def _():
                self.arrived(at.n_tp, c)
                self.total[:, here] = self.total[:, here] + self.came[at.n_tp, :, here].astype(F32)

            return carry

        lax.fori_loop(0, self.tiles, some, 0)

    def finish(self):
        at = self.at

        def some(i, carry):
            j, c = i // self.tiles, lax.rem(i, self.tiles)
            pl.when(j > at.t)(lambda: self.copy(j, c, 0).wait_send())
            pl.when(j < at.t)(lambda: self.copy(j, c, 1).wait_send())
            return carry

        lax.fori_loop(0, at.n_tp * self.tiles, some, 0)


def middle_kernel(
    sizes,
    two, cot_all, wgu_all, wd_all,
    gn2, hidden, sum_gu, sum_d, sib_gu, sib_d,
    x, cots, wgu_v, wd_v, ggu, acts, came, going, stage_gu, stage_d, in_gu, in_d,
    line_send, line_recv, fold_send, fold_recv, sib_send, sib_recv, local_sems,
):
    n_fsdp, n_tp = sizes
    half = n_fsdp // 2
    bits = half.bit_length() - 1
    at = Places(n_fsdp, n_tp)
    slab, model = two.shape
    part_rows = model // n_fsdp
    at.greet()
    line = Line(at, two, x, line_send, line_recv)
    line.start()
    loads = [
        pltpu.make_async_copy(two, x.at[at.t], local_sems.at[0]),
        pltpu.make_async_copy(wgu_all, wgu_v, local_sems.at[1]),
        pltpu.make_async_copy(wd_all, wd_v, local_sems.at[2]),
        pltpu.make_async_copy(cot_all, cots, local_sems.at[3]),
    ]
    for load in loads:
        load.start()
    for load in loads:
        load.wait()
    fold = Fold(at, gn2, going, came, min(512, model), fold_send, fold_recv)

    def unit(slot):
        here = pl.ds(pl.multiple_of(slot * slab, slab), slab)
        acts[0] = dot(x[slot], wgu_v[0], NN)
        acts[1] = dot(x[slot], wgu_v[1], NN)
        acts[2] = dot(cots[slot], wd_v[...], NT)
        step = 16

        def some(i, carry):
            local_rows = pl.ds(pl.multiple_of(i * step, step), step)
            rows = pl.ds(pl.multiple_of(slot * slab + i * step, step), step)
            gate, up, grad = acts[0, local_rows, :], acts[1, local_rows, :], acts[2, local_rows, :]
            low = jax.nn.sigmoid(gate)
            act = gate * low
            hidden[rows, :] = (act * up).astype(BF16)
            ggu[0, rows, :] = (grad * up * low * (1.0 + gate * (1.0 - low))).astype(BF16)
            ggu[1, rows, :] = (grad * act).astype(BF16)
            return carry

        lax.fori_loop(0, slab // step, some, 0)

        def tiles(c, carry):
            rows = fold.lanes(c)
            fold.put(
                slot,
                c,
                dot(ggu[0, here, :], wgu_v[0, rows, :], NT) + dot(ggu[1, here, :], wgu_v[1, rows, :], NT),
            )
            return carry

        lax.fori_loop(0, fold.tiles, tiles, 0)

    def each_from(first, last, work):
        def some(i, carry):
            s = (i + 1) // 2
            slot = at.t + s * (2 * lax.rem(i, 2) - 1)
            pl.when((slot >= 0) & (slot < n_tp))(lambda: work(slot))
            return carry

        lax.fori_loop(max(0, 2 * first - 1), 2 * last - 1, some, 0)

    for s in range(n_tp):
        if s:
            line.step(s)
        each_from(s, s + 1, unit)

    for key in range(1, n_tp - 2):
        for c in range(fold.tiles):
            fold.forward(key, c)

    def block(f, take):
        columns = pl.ds(pl.multiple_of(f * part_rows, part_rows), part_rows)
        for part in range(2):
            rows = x[:, :, columns].reshape(n_tp * slab, part_rows)
            take(part, dot(rows, ggu[part], TN))
        grads = cots[:, :, columns].reshape(n_tp * slab, part_rows)
        take(2, dot(hidden[...], grads, TN))

    def sib_copies(i):
        return [
            send(stage_gu.at[lax.rem(i, 2)], sib_gu.at[i], sib_send.at[0, i], sib_recv.at[0, i], at.sibling()),
            send(stage_d.at[lax.rem(i, 2)], sib_d.at[i], sib_send.at[1, i], sib_recv.at[1, i], at.sibling()),
        ]

    def keep_copies(i):
        return [
            pltpu.make_async_copy(stage_gu.at[lax.rem(i, 2)], sum_gu.at[i], local_sems.at[4 + lax.rem(i, 2)]),
            pltpu.make_async_copy(stage_d.at[lax.rem(i, 2)], sum_d.at[i], local_sems.at[6 + lax.rem(i, 2)]),
        ]

    def others(i, carry):
        pl.when(i < fold.tiles)(lambda: fold.forward(n_tp - 2, i))

        @pl.when(i >= 2)
        def _():
            for copy in sib_copies(i - 2):
                copy.wait_send()

        def take(part, values):
            if part < 2:
                stage_gu[lax.rem(i, 2), part] = values.astype(BF16)
            else:
                stage_d[lax.rem(i, 2)] = values.astype(BF16)

        block(xor_any(at.chip, i, bits) * 2 + 1 - at.core, take)
        for copy in sib_copies(i):
            copy.start()
        return carry

    lax.fori_loop(0, half, others, 0)
    for i in range(half - 2, half):
        for copy in sib_copies(jnp.int32(i)):
            copy.wait_send()

    def mine(i, carry):
        pl.when(i < fold.tiles)(lambda: fold.forward(n_tp - 1, i))
        for copy in sib_copies(i):
            copy.wait_recv()
        takes = [
            pltpu.make_async_copy(sib_gu.at[i], in_gu, local_sems.at[8]),
            pltpu.make_async_copy(sib_d.at[i], in_d, local_sems.at[9]),
        ]
        for take in takes:
            take.start()

        @pl.when(i >= 2)
        def _():
            for copy in keep_copies(i - 2):
                copy.wait()

        def take(part, values):
            if part == 0:
                for copy in takes:
                    copy.wait()
            if part < 2:
                stage_gu[lax.rem(i, 2), part] = (values + in_gu[part].astype(F32)).astype(BF16)
            else:
                stage_d[lax.rem(i, 2)] = (values + in_d[...].astype(F32)).astype(BF16)

        block(xor_any(at.chip, i, bits) * 2 + at.core, take)
        for copy in keep_copies(i):
            copy.start()
        return carry

    lax.fori_loop(0, half, mine, 0)
    fold.end()
    for i in range(half - 2, half):
        for copy in keep_copies(jnp.int32(i)):
            copy.wait()
    line.finish()
    fold.finish()


def middle(sizes, two, cot_all, wgu_all, wd_all):
    n_fsdp, n_tp = sizes
    half = n_fsdp // 2
    slab, model = two.shape
    hidden = wd_all.shape[0]
    part_rows = model // n_fsdp
    tile = min(512, model)
    hbm = pl.BlockSpec(memory_space=pl.ANY)
    vmem = pl.BlockSpec(memory_space=pltpu.VMEM)
    shape = jax.ShapeDtypeStruct
    outs = [
        (shape((slab, model), F32), vmem),
        (shape((n_tp * slab, hidden), BF16), vmem),
        (shape((half, 2, part_rows, hidden), BF16), hbm),
        (shape((half, hidden, part_rows), BF16), hbm),
        (shape((half, 2, part_rows, hidden), BF16), hbm),
        (shape((half, hidden, part_rows), BF16), hbm),
    ]
    dma = pltpu.SemaphoreType.DMA
    return pl.pallas_call(
        functools.partial(middle_kernel, sizes),
        in_specs=[hbm] * 4,
        out_specs=[spec for _, spec in outs],
        out_shape=[out for out, _ in outs],
        scratch_shapes=[
            pltpu.VMEM((n_tp, slab, model), BF16),
            pltpu.VMEM((n_tp, slab, model), BF16),
            pltpu.VMEM((2, model, hidden), BF16),
            pltpu.VMEM((hidden, model), BF16),
            pltpu.VMEM((2, n_tp * slab, hidden), BF16),
            pltpu.VMEM((3, slab, hidden), F32),
            pltpu.VMEM((n_tp + 1, slab, model), BF16),
            pltpu.VMEM((n_tp, slab, model), BF16),
            pltpu.VMEM((2, 2, part_rows, hidden), BF16),
            pltpu.VMEM((2, hidden, part_rows), BF16),
            pltpu.VMEM((2, part_rows, hidden), BF16),
            pltpu.VMEM((hidden, part_rows), BF16),
            dma((2, n_tp)), dma((n_tp,)), dma((n_tp, model // tile)), dma((n_tp + 1, model // tile)),
            dma((2, half)), dma((2, half)), dma((10,)),
        ],
        compiler_params=pltpu.CompilerParams(
            collective_id=3, has_side_effects=True, vmem_limit_bytes=62 * 2**20
        ),
        cost_estimate=pl.CostEstimate(flops=10**11, bytes_accessed=10**8, transcendentals=0),
    )(two, cot_all, wgu_all, wd_all)


class Spread:
    def __init__(self, at, sums, near, relay, boxes, sems, local_sems):
        self.at, self.sums, self.near, self.relay, self.boxes = at, sums, near, relay, boxes
        self.sems, self.local_sems = sems, local_sems
        self.half = at.n_fsdp // 2
        self.by_relay = at.n_fsdp == 8
        self.direct = [1, 2] if self.by_relay else list(range(1, self.half))
        self.rows = sums.shape[1] // 2

    def part(self, i, part):
        return self.sums.at[i, pl.ds(part * self.rows, self.rows)]

    def relay_copy(self, part):
        return send(
            self.part(3, part), self.relay.at[part],
            self.sems.at[0, 3 + part], self.sems.at[1, 3 + part], self.at.near(1 + part),
        )

    def near_copy(self, i):
        return send(
            self.sums.at[i], self.near.at[i], self.sems.at[0, i], self.sems.at[1, i], self.at.near(i)
        )

    def start(self):
        if self.by_relay:
            for part in range(2):
                self.relay_copy(part).start()
        else:
            for i in self.direct:
                self.near_copy(i).start()

    def add(self):
        if not self.by_relay:
            return
        for part, i in ((0, 2), (1, 1)):
            self.relay_copy(part).wait_recv()
            takes = [
                pltpu.make_async_copy(self.part(i, part), self.boxes.at[0], self.local_sems.at[0]),
                pltpu.make_async_copy(self.relay.at[part], self.boxes.at[1], self.local_sems.at[1]),
            ]
            for take in takes:
                take.start()
            for take in takes:
                take.wait()
            self.boxes[0] = (self.boxes[0].astype(F32) + self.boxes[1].astype(F32)).astype(BF16)
            keep = pltpu.make_async_copy(self.boxes.at[0], self.part(i, part), self.local_sems.at[0])
            keep.start()
            keep.wait()
            self.near_copy(i).start()

    def arrived(self):
        for i in self.direct:
            self.near_copy(i).wait_recv()

    def finish(self):
        if self.by_relay:
            for part in range(2):
                self.relay_copy(part).wait_send()
        for i in self.direct:
            self.near_copy(i).wait_send()


class Pair:
    def __init__(self, at, stage, sib, sums, inbox, sems, local_sems):
        self.at, self.stage, self.sib, self.sums, self.inbox = at, stage, sib, sums, inbox
        self.sems, self.local_sems = sems, local_sems

    def sib_copy(self, i):
        return send(
            self.stage.at[lax.rem(i, 2)], self.sib.at[i], self.sems.at[0, i], self.sems.at[1, i], self.at.sibling()
        )

    def keep_copy(self, i):
        return pltpu.make_async_copy(
            self.stage.at[lax.rem(i, 2)], self.sums.at[i], self.local_sems.at[lax.rem(i, 2)]
        )

    def give(self, i, values):
        pl.when(i >= 2)(lambda: self.sib_copy(i - 2).wait_send())
        self.stage[lax.rem(i, 2)] = values().astype(BF16)
        self.sib_copy(i).start()

    def given(self, half):
        for i in range(half - 2, half):
            self.sib_copy(jnp.int32(i)).wait_send()

    def keep(self, i, values):
        self.sib_copy(i).wait_recv()
        take = pltpu.make_async_copy(self.sib.at[i], self.inbox, self.local_sems.at[2])
        take.start()
        pl.when(i >= 2)(lambda: self.keep_copy(i - 2).wait())
        own = values()
        take.wait()
        self.stage[lax.rem(i, 2)] = (own + self.inbox[...].astype(F32)).astype(BF16)
        self.keep_copy(i).start()

    def kept(self, half):
        for i in range(half - 2, half):
            self.keep_copy(jnp.int32(i)).wait()


def norm_back(values, incoming, gain_row):
    average = jnp.mean(values, axis=-1, keepdims=True)
    centred = values - average
    scale = lax.rsqrt(jnp.mean(centred * centred, axis=-1, keepdims=True) + NORM_EPS)
    unit = centred * scale
    grads = incoming * gain_row
    inner = jnp.mean(grads * unit, axis=-1, keepdims=True)
    back = scale * (grads - jnp.mean(grads, axis=-1, keepdims=True) - unit * inner)
    return back, jnp.sum(incoming * unit, axis=0, keepdims=True), jnp.sum(incoming, axis=0, keepdims=True)


def attend_back(widest, q_in, k_in, v_in, g_in, cos, s_low, s_high, starts, g_out, bias, kt, dk, dv, first_lane):
    seq_len, width = q_in.shape
    rows = min(256, seq_len)
    lanes = pl.ds(pl.multiple_of(first_lane, LANES), LANES)
    kt[...] = k_in[:, lanes].astype(F32).T.astype(BF16)
    dk[...] = jnp.zeros_like(dk)
    dv[...] = jnp.zeros_like(dv)

    def put(part, here, values):
        columns = pl.ds(pl.multiple_of(part * width + first_lane, LANES), LANES)
        low = values.astype(BF16)
        g_out[here, columns] = low
        return jnp.sum(low.astype(F32), axis=0, keepdims=True)

    total_q = jnp.zeros((1, LANES), F32)
    for block in range(seq_len // rows):
        here = slice(block * rows, (block + 1) * rows)
        first, last = key_range(block, rows, widest)
        query_rows = (q_in[here, lanes].astype(F32) * HEAD**-0.5).astype(BF16)
        grad_rows = g_in[here, lanes]
        query_cols = query_rows.astype(F32).T.astype(BF16)
        grad_cols = grad_rows.astype(F32).T.astype(BF16)
        head_down = lax.broadcasted_iota(jnp.int32, query_cols.shape, 0) // HEAD
        head_along = lax.broadcasted_iota(jnp.int32, query_rows.shape, 1) // HEAD
        none_down, none_along = jnp.zeros_like(query_cols), jnp.zeros_like(query_rows)
        parts = []
        for head in range(LANES // HEAD):
            weights, total = seen_weights(
                k_in[first:last, lanes],
                jnp.where(head_down == head, query_cols, none_down),
                starts[:, here],
                first,
                block * rows,
            )
            probs = weights * (1.0 / total)
            grad_probs = dot(
                v_in[first:last, lanes], jnp.where(head_down == head, grad_cols, none_down), NN
            )
            inner = jnp.sum(probs * grad_probs, axis=0, keepdims=True)
            grad_scores = (probs * (grad_probs - inner)).astype(BF16)
            dk[first:last, :] += dot(
                grad_scores, jnp.where(head_along == head, query_rows, none_along), NN
            )
            dv[first:last, :] += dot(
                probs.astype(BF16), jnp.where(head_along == head, grad_rows, none_along), NN
            )
            parts.append(dot(kt[head * HEAD : (head + 1) * HEAD, first:last], grad_scores, NN))
        grad_queries = jnp.concatenate(parts, axis=0).T * HEAD**-0.5
        total_q = total_q + put(
            0, here, turn(grad_queries, cos[here, :], -s_low[here, :], -s_high[here, :])
        )
    everywhere = slice(0, seq_len)
    bias[4:5, lanes] = total_q
    bias[5:6, lanes] = put(1, everywhere, turn(dk[...], cos[...], -s_low[...], -s_high[...]))
    bias[6:7, lanes] = put(2, everywhere, dv[...])


def back_kernel(
    sizes, widest,
    gn2, resid, tok, cot, att_own, wo_all, wq_all, q_in, k_in, v_in, one, sum_gu_in, sum_d_in,
    rows_in, cos, s_low, s_high, starts,
    grad_tok, small_out, near_gu, near_d, own_gu, own_d, sum_q, near_q, sib_q, relay_q,
    sum_o, near_o, sib_o, relay_o, zo, relay_gu, relay_d,
    gres, res_v, tok_v, cot_v, att_v, gattn, wo_v, wq_v, q_v, k_v, v_v, gp, gatt, ghead, came, going,
    kt, dk, dv, stage_o, inbox_o, stage_q, inbox_q, box_gu, box_d, box_o, box_q, zo_stage, zo_box,
    norm_sums, bias, tiles, land_z, land_near, land_sib,
    swap_send, swap_recv, fold_send, fold_recv, pair_o_sems, pair_q_sems, gu_sems, d_sems, o_sems, q_sems,
    zo_sems, small_sems, local_sems, pair_o_local, pair_q_local,
):
    n_fsdp, n_tp = sizes
    half = n_fsdp // 2
    bits = half.bit_length() - 1
    at = Places(n_fsdp, n_tp)
    slab, model = tok.shape
    seq_len, width = q_in.shape
    part_rows = model // n_fsdp
    pairs = width // LANES
    loads = [
        pltpu.make_async_copy(src, dst, local_sems.at[i])
        for i, (src, dst) in enumerate(
            [
                (gn2, gres), (resid, res_v), (cot, cot_v), (wo_all, wo_v), (tok, tok_v), (att_own, att_v),
                (q_in, q_v), (k_in, k_v), (v_in, v_v), (wq_all, wq_v),
            ]
        )
    ]
    for load in loads:
        load.start()
    at.greet()
    spread_gu = Spread(at, own_gu, near_gu, relay_gu, box_gu, gu_sems, local_sems.at[pl.ds(13, 2)])
    spread_d = Spread(at, own_d, near_d, relay_d, box_d, d_sems, local_sems.at[pl.ds(13, 2)])
    spread_o = Spread(at, sum_o, near_o, relay_o, box_o, o_sems, local_sems.at[pl.ds(13, 2)])
    spread_q = Spread(at, sum_q, near_q, relay_q, box_q, q_sems, local_sems.at[pl.ds(13, 2)])
    spread_gu.start()
    spread_d.start()
    norm_sums[...] = jnp.zeros_like(norm_sums)
    bias[...] = jnp.zeros_like(bias)
    for load in loads[:4]:
        load.wait()

    step = 16

    def second(i, carry):
        here = pl.ds(pl.multiple_of(i * step, step), step)
        back, gain, shift = norm_back(res_v[here, :], gres[here, :], rows_in[1:2, :])
        total = cot_v[here, :].astype(F32) + back
        gres[here, :] = total
        gattn[here, :] = total.astype(BF16)
        norm_sums[1:2, :] = norm_sums[1:2, :] + gain
        norm_sums[3:4, :] = norm_sums[3:4, :] + shift
        return carry

    lax.fori_loop(0, slab // step, second, 0)

    def swap_copy(i, k):
        lanes = pl.ds(pl.multiple_of(i * LANES, LANES), LANES)
        other = lax.rem(at.t + k, n_tp)
        return send(
            ghead.at[other, :, lanes],
            gatt.at[pl.ds(pl.multiple_of(at.t * slab, slab), slab), lanes],
            swap_send.at[i, k], swap_recv.at[i, k], at.along(other),
        )

    def give_heads(i, carry):
        lanes = pl.ds(pl.multiple_of(i * LANES, LANES), LANES)

        def to(k, carry):
            other = lax.rem(at.t + k, n_tp)
            rows = pl.ds(pl.multiple_of(other * width + i * LANES, LANES), LANES)
            ghead[other, :, lanes] = dot(gattn[...], wo_v[rows, :], NT).astype(BF16)
            pl.when(k > 0)(lambda: swap_copy(i, k).start())
            return carry

        lax.fori_loop(0, n_tp, to, 0)
        gatt[pl.ds(pl.multiple_of(at.t * slab, slab), slab), lanes] = ghead[at.t, :, lanes]
        return carry

    lax.fori_loop(0, pairs, give_heads, 0)

    loads[5].wait()
    pair_o = Pair(at, stage_o, sib_o, sum_o, inbox_o, pair_o_sems, pair_o_local)
    pair_q = Pair(at, stage_q, sib_q, sum_q, inbox_q, pair_q_sems, pair_q_local)

    def piece(f):
        return pl.ds(pl.multiple_of(f * part_rows, part_rows), part_rows)

    def owner(i, core):
        return xor_any(at.chip, i, bits) * 2 + core

    def give_o(i, carry):
        pair_o.give(i, lambda: dot(att_v[...], gattn[:, piece(owner(i, 1 - at.core))], TN))
        return carry

    lax.fori_loop(0, half, give_o, 0)
    for load in loads[6:9]:
        load.wait()
    load_one = pltpu.make_async_copy(one, wo_v.at[pl.ds(0, seq_len), :], local_sems.at[12])
    load_one.start()

    def some_heads(i, carry):
        for k in range(1, n_tp):
            source = lax.rem(at.t + n_tp - k, n_tp)
            lanes = pl.ds(pl.multiple_of(i * LANES, LANES), LANES)
            came_rows = gatt.at[pl.ds(pl.multiple_of(source * slab, slab), slab), lanes]
            send(came_rows, came_rows, swap_send.at[i, k], swap_recv.at[i, k], at.along(source)).wait_recv()
        attend_back(
            widest, q_v, k_v, v_v, gatt, cos, s_low, s_high, starts, gp, bias, kt, dk, dv, i * LANES
        )
        return carry

    lax.fori_loop(0, pairs, some_heads, 0)

    loads[9].wait()
    fold = Fold(at, grad_tok, going, came, min(512, model), fold_send, fold_recv)

    def term(slot):
        rows = gp[pl.ds(pl.multiple_of(slot * slab, slab), slab), :]

        def some(c, carry):
            fold.put(slot, c, dot(rows, wq_v[fold.lanes(c), :], NT))
            return carry

        lax.fori_loop(0, fold.tiles, some, 0)

    def far_first(i, carry):
        s = (2 * n_tp - 1 - i) // 2
        slot = at.t + s * (2 * lax.rem(i, 2) - 1)
        pl.when((slot >= 0) & (slot < n_tp))(lambda: term(slot))
        return carry

    lax.fori_loop(0, 2 * n_tp - 1, far_first, 0)

    spread_gu.add()
    spread_d.add()
    pair_o.given(half)

    def forward(key, i):
        pl.when(i < fold.tiles)(lambda: fold.forward(key, i))

    def keep_o(i, carry):
        forward(n_tp - 1, i)
        pair_o.keep(i, lambda: dot(att_v[...], gattn[:, piece(owner(i, at.core))], TN))
        return carry

    lax.fori_loop(0, half, keep_o, 0)
    pair_o.kept(half)
    spread_o.start()
    load_one.wait()

    def give_q(i, carry):
        forward(n_tp - 2, i)
        pair_q.give(i, lambda: dot(wo_v[0:seq_len, piece(owner(i, 1 - at.core))], gp[...], TN))
        return carry

    lax.fori_loop(0, half, give_q, 0)
    pair_q.given(half)

    def keep_q(i, carry):
        pair_q.keep(i, lambda: dot(wo_v[0:seq_len, piece(owner(i, at.core))], gp[...], TN))
        return carry

    lax.fori_loop(0, half, keep_q, 0)
    pair_q.kept(half)
    spread_q.start()
    spread_o.add()
    for key in range(n_tp - 3, 0, -1):
        for c in range(fold.tiles):
            fold.forward(key, c)
    spread_q.add()

    each = model // n_tp
    spread_o.arrived()

    def zo_copy(k):
        other = lax.rem(at.t + k, n_tp)
        return send(zo_stage.at[other], zo.at[at.t], zo_sems.at[0, k], zo_sems.at[1, k], at.along(other))

    def group(k, carry):
        other = lax.rem(at.t + k, n_tp)
        rows = pl.ds(pl.multiple_of(other * each, each), each)
        takes = [
            pltpu.make_async_copy(
                (sum_o if i == 0 else near_o).at[i, rows, :], zo_box.at[n], local_sems.at[16 + n]
            )
            for n, i in enumerate([0] + spread_o.direct)
        ]
        for take in takes:
            take.start()
        total = jnp.zeros(zo_box.shape[1:], F32)
        for n, take in enumerate(takes):
            take.wait()
            total = total + zo_box[n].astype(F32)
        zo_stage[other] = total.astype(BF16)
        pl.when(k > 0)(lambda: zo_copy(k).start())
        return carry

    lax.fori_loop(0, n_tp, group, 0)
    own_zo = pltpu.make_async_copy(zo_stage.at[at.t], zo.at[at.t], local_sems.at[15])
    own_zo.start()

    fold.end()
    loads[4].wait()

    def first(i, carry):
        here = pl.ds(pl.multiple_of(i * step, step), step)
        back, gain, shift = norm_back(tok_v[here, :].astype(F32), grad_tok[here, :], rows_in[0:1, :])
        grad_tok[here, :] = gres[here, :] + back
        norm_sums[0:1, :] = norm_sums[0:1, :] + gain
        norm_sums[2:3, :] = norm_sums[2:3, :] + shift
        return carry

    lax.fori_loop(0, slab // step, first, 0)

    lanes_each = model // (n_fsdp * n_tp)
    kept = lax.broadcasted_iota(jnp.int32, (8, LANES), 1) < lanes_each

    def tile_of(ref, index):
        start = index * lanes_each
        tile = ref[:, start // LANES * LANES : start // LANES * LANES + LANES]
        return jnp.where(kept, pltpu.roll(tile, (LANES - start % LANES) % LANES, 1), 0.0)

    for f in range(n_fsdp):
        for t in range(n_tp):
            tiles[t, f] = tile_of(norm_sums, f * n_tp + t)
    for f in range(n_fsdp):
        tiles[at.t, f] = tiles[at.t, f] + tile_of(bias, f)

    def z_copy(k):
        other = lax.rem(at.t + k, n_tp)
        return send(
            tiles.at[other], land_z.at[k], small_sems.at[0, half + k], small_sems.at[1, half + k], at.along(other)
        )

    for k in range(1, n_tp):
        z_copy(k).start()
    total = tiles[at.t]
    for k in range(1, n_tp):
        z_copy(k).wait_recv()
        total = total + land_z[k]
    land_z[0] = total

    def chip_copy(k):
        return send(
            land_z.at[0, pl.ds(xor(at.chip, k) * 2, 2)], land_near.at[k],
            small_sems.at[0, k], small_sems.at[1, k], at.near(k),
        )

    for k in range(1, half):
        chip_copy(k).start()
    total = land_z[0, pl.ds(at.chip * 2, 2)]
    for k in range(1, half):
        chip_copy(k).wait_recv()
        total = total + land_near[k]
    land_near[0] = total
    to_sib = send(
        land_near.at[0, 1 - at.core], land_sib, small_sems.at[0, 0], small_sems.at[1, 0], at.sibling()
    )
    to_sib.start()
    to_sib.wait_recv()
    small_out[...] = land_near[0, at.core] + land_sib[...]

    to_sib.wait_send()
    for k in range(1, half):
        chip_copy(k).wait_send()
    for k in range(1, n_tp):
        z_copy(k).wait_send()
        zo_copy(k).wait_send()
        source = lax.rem(at.t + n_tp - k, n_tp)
        send(zo.at[source], zo.at[source], zo_sems.at[0, k], zo_sems.at[1, k], at.along(source)).wait_recv()
    own_zo.wait()

    def swapped(i, carry):
        for k in range(1, n_tp):
            swap_copy(i, k).wait_send()
        return carry

    lax.fori_loop(0, pairs, swapped, 0)
    fold.finish()
    for spread in (spread_gu, spread_d, spread_q):
        spread.arrived()
    for spread in (spread_gu, spread_d, spread_q, spread_o):
        spread.finish()


def back(sizes, widest, gn2, resid, tok, cot, att_own, wo_all, wq_all, q_in, k_in, v_in, one, sum_gu, sum_d, rows_in, tables, starts):
    n_fsdp, n_tp = sizes
    half = n_fsdp // 2
    slab, model = tok.shape
    seq_len, width = q_in.shape
    hidden = sum_d.shape[1]
    part_rows = model // n_fsdp
    pairs = width // LANES
    each = model // n_tp
    tile = min(512, model)
    hbm = pl.BlockSpec(memory_space=pl.ANY)
    vmem = pl.BlockSpec(memory_space=pltpu.VMEM)
    shape = jax.ShapeDtypeStruct
    piece_q, piece_o = (part_rows, 3 * width), (model, part_rows)
    piece_gu, piece_d = sum_gu.shape[1:], sum_d.shape[1:]
    halved = lambda piece: (piece[0] // 2,) + tuple(piece[1:])
    outs = [
        (shape((slab, model), F32), vmem),
        (shape((8, LANES), F32), vmem),
        (shape(sum_gu.shape, BF16), hbm),
        (shape(sum_d.shape, BF16), hbm),
        (shape(sum_gu.shape, BF16), hbm),
        (shape(sum_d.shape, BF16), hbm),
        (shape((half,) + piece_q, BF16), hbm),
        (shape((half,) + piece_q, BF16), hbm),
        (shape((half,) + piece_q, BF16), hbm),
        (shape((2,) + halved(piece_q), BF16), hbm),
        (shape((half,) + piece_o, BF16), hbm),
        (shape((half,) + piece_o, BF16), hbm),
        (shape((half,) + piece_o, BF16), hbm),
        (shape((2,) + halved(piece_o), BF16), hbm),
        (shape((n_tp, each, part_rows), BF16), hbm),
        (shape((2,) + halved(piece_gu), BF16), hbm),
        (shape((2,) + halved(piece_d), BF16), hbm),
    ]
    dma = pltpu.SemaphoreType.DMA
    return pl.pallas_call(
        functools.partial(back_kernel, sizes, widest),
        in_specs=[hbm] * 13 + [vmem] * 5,
        out_specs=[spec for _, spec in outs],
        out_shape=[out for out, _ in outs],
        scratch_shapes=[
            pltpu.VMEM((slab, model), F32),
            pltpu.VMEM((slab, model), F32),
            pltpu.VMEM((slab, model), BF16),
            pltpu.VMEM((slab, model), BF16),
            pltpu.VMEM((slab, model), BF16),
            pltpu.VMEM((slab, model), BF16),
            pltpu.VMEM((model, model), BF16),
            pltpu.VMEM((model, 3 * width), BF16),
            pltpu.VMEM((seq_len, width), BF16),
            pltpu.VMEM((seq_len, width), BF16),
            pltpu.VMEM((seq_len, width), BF16),
            pltpu.VMEM((seq_len, 3 * width), BF16),
            pltpu.VMEM((seq_len, width), BF16),
            pltpu.VMEM((n_tp, slab, width), BF16),
            pltpu.VMEM((n_tp + 1, slab, model), BF16),
            pltpu.VMEM((n_tp, slab, model), BF16),
            pltpu.VMEM((LANES, seq_len), BF16),
            pltpu.VMEM((seq_len, LANES), F32),
            pltpu.VMEM((seq_len, LANES), F32),
            pltpu.VMEM((2,) + piece_o, BF16),
            pltpu.VMEM(piece_o, BF16),
            pltpu.VMEM((2,) + piece_q, BF16),
            pltpu.VMEM(piece_q, BF16),
            pltpu.VMEM((2,) + halved(piece_gu), BF16),
            pltpu.VMEM((2,) + halved(piece_d), BF16),
            pltpu.VMEM((2,) + halved(piece_o), BF16),
            pltpu.VMEM((2,) + halved(piece_q), BF16),
            pltpu.VMEM((n_tp, each, part_rows), BF16),
            pltpu.VMEM((half, each, part_rows), BF16),
            pltpu.VMEM((8, model), F32),
            pltpu.VMEM((8, width), F32),
            pltpu.VMEM((n_tp, n_fsdp, 8, LANES), F32),
            pltpu.VMEM((n_tp, n_fsdp, 8, LANES), F32),
            pltpu.VMEM((half, 2, 8, LANES), F32),
            pltpu.VMEM((8, LANES), F32),
            dma((pairs, n_tp)), dma((pairs, n_tp)),
            dma((n_tp, model // tile)), dma((n_tp + 1, model // tile)),
            dma((2, half)), dma((2, half)),
            dma((2, half + 1)), dma((2, half + 1)), dma((2, half + 1)), dma((2, half + 1)),
            dma((2, n_tp)), dma((2, half + n_tp)), dma((16 + half,)), dma((3,)), dma((3,)),
        ],
        input_output_aliases={11: 4, 12: 5},
        compiler_params=pltpu.CompilerParams(
            collective_id=2, has_side_effects=True, vmem_limit_bytes=62 * 2**20
        ),
        cost_estimate=pl.CostEstimate(flops=10**11, bytes_accessed=10**8, transcendentals=0),
    )(
        gn2, resid, tok, cot, att_own, wo_all, wq_all, q_in, k_in, v_in, one, sum_gu, sum_d,
        rows_in, *tables, starts,
    )


def reduce_rows(values):
    return lax.psum_scatter(values.astype(BF16), "tp", scatter_dimension=0, tiled=True).astype(F32)


def local(tokens, lengths, ln_gains, ln_shifts, w_qkv, b_qkv, w_out, w_gate_up, w_down, cotangent):
    n_fsdp, n_tp = lax.axis_size("fsdp"), lax.axis_size("tp")
    sizes = (n_fsdp, n_tp)
    at_tp = lax.axis_index("tp")
    slab_rows, model_width = tokens.shape
    seq_len = slab_rows * n_tp
    small = ln_gains.shape[1]
    local_width = w_qkv.shape[2]
    hidden_width = w_gate_up.shape[2]
    part_rows = w_qkv.shape[0]

    length_row = lengths[0]
    doc_ends = jnp.cumsum(length_row)
    ids = jnp.arange(seq_len, dtype=jnp.int32)
    passed = (doc_ends[None, :] <= ids[:, None]).astype(jnp.int32)
    starts = jnp.sum(passed * length_row[None, :], axis=1)
    places = (ids - starts).astype(F32)
    lane = jnp.arange(LANES, dtype=jnp.int32) % HEAD
    frequency = 10000.0 ** (-2.0 * (lane % (ROT // 2)).astype(F32) / ROT)
    angles = places[:, None] * frequency[None, :]
    cosine = jnp.where(lane[None] < ROT, jnp.cos(angles), 1.0)
    sine = jnp.sin(angles)
    sine_low = jnp.where(lane[None] < ROT // 2, -sine, 0.0)
    sine_high = jnp.where((lane[None] >= ROT // 2) & (lane[None] < ROT), sine, 0.0)
    tables = (cosine, sine_low, sine_high)
    starts_row = starts.reshape(1, seq_len).astype(jnp.int32)
    widest = seq_len // 2

    tile = jnp.concatenate([ln_gains, ln_shifts, b_qkv.astype(F32), jnp.zeros((1, small), F32)], 0)
    tile = jnp.pad(tile, ((0, 0), (0, LANES - small)))
    (
        full_one, queries, key_vals, value_rows, residual, normed_two, norm_rows_all, attended_own,
        grad_branch, qkv_all, out_all, gu_all, down_all,
    ) = front(
        sizes, widest, tokens, cotangent, w_qkv.reshape(part_rows, 3 * local_width), w_out,
        w_gate_up.transpose(1, 0, 2), w_down, tile, tables, starts_row,
    )
    full_one = full_one.reshape(seq_len, model_width)

    grad_normed_two, hidden_low, sum_gu, sum_down, _, _ = middle(
        sizes, normed_two, grad_branch, gu_all, down_all
    )
    (
        grad_tokens, shares, near_gu, near_down, own_gu, own_down, sum_qkv, near_qkv, _, _, _, _, _, _,
        out_parts, _, _,
    ) = back(
        sizes, widest, grad_normed_two, residual, tokens, cotangent, attended_own, out_all, qkv_all,
        queries, key_vals, value_rows, full_one, sum_gu, sum_down, norm_rows_all, tables, starts_row,
    )
    branch = reduce_rows(dot(hidden_low, down_all, NN))
    result = (residual + branch).astype(BF16)
    direct = [1, 2] if n_fsdp == 8 else list(range(1, n_fsdp // 2))

    def total(sums, near):
        return sum([near[i].astype(F32) for i in direct], sums[0].astype(F32))

    shares = shares[:, :small]
    return (
        result,
        grad_tokens,
        shares[0:2],
        shares[2:4],
        total(sum_qkv, near_qkv).reshape(part_rows, 3, local_width),
        shares[4:7],
        jnp.sum(out_parts.astype(F32), axis=0),
        total(own_gu, near_gu).transpose(1, 0, 2),
        total(own_down, near_down),
    )


def solution(mesh):
    placed = (
        P(("fsdp", "tp"), None),
        P("fsdp", None),
        P(None, ("fsdp", "tp")),
        P(None, ("fsdp", "tp")),
        P("fsdp", None, "tp"),
        P(None, ("tp", "fsdp")),
        P("tp", "fsdp"),
        P("fsdp", None, "tp"),
        P("tp", "fsdp"),
        P(("fsdp", "tp"), None),
    )
    return jax.shard_map(
        local,
        mesh=mesh,
        in_specs=placed,
        out_specs=(
            P(("fsdp", "tp"), None),
            P(("fsdp", "tp"), None),
            P(None, ("fsdp", "tp")),
            P(None, ("fsdp", "tp")),
            P("fsdp", None, "tp"),
            P(None, ("tp", "fsdp")),
            P("tp", "fsdp"),
            P("fsdp", None, "tp"),
            P("tp", "fsdp"),
        ),
        check_vma=False,
    )
```

```python
import functools

import jax
import jax.numpy as jnp
from jax import lax
from jax.experimental import pallas as pl
from jax.experimental.pallas import tpu as pltpu
from jax.sharding import PartitionSpec as P

HEAD = 64
ROT = 16
NORM_EPS = 1e-05
LANES = 128
MESH = pl.DeviceIdType.MESH
NN = (((1,), (0,)), ((), ()))
NT = (((1,), (1,)), ((), ()))
TN = (((0,), (0,)), ((), ()))
F32 = jnp.float32
BF16 = jnp.bfloat16


def dot(left, right, dims):
    return lax.dot_general(left, right, dims, preferred_element_type=F32)


def turn(values, cosine, sine_low, sine_high):
    return (
        values * cosine
        + pltpu.roll(values, LANES - ROT // 2, 1) * sine_low
        + pltpu.roll(values, ROT // 2, 1) * sine_high
    )


def key_range(block, rows, widest):
    first = max(0, block * rows - widest)
    return first, (block + 1) * rows


def seen_weights(key_rows, query_cols, starts_row, first_key, first_query):
    scores = dot(key_rows, query_cols, NN)
    key_ids = first_key + lax.broadcasted_iota(jnp.int32, scores.shape, 0)
    query_ids = first_query + lax.broadcasted_iota(jnp.int32, scores.shape, 1)
    seen = (key_ids <= query_ids) & (key_ids >= starts_row)
    scores = jnp.where(seen, scores, -1e30)
    top = jnp.max(scores, axis=0, keepdims=True)
    weights = jnp.exp(scores - top)
    return weights, jnp.sum(weights, axis=0, keepdims=True)


def xor(value, mask):
    bit = 1
    while bit <= mask:
        if mask & bit:
            value = value + bit * (1 - 2 * lax.rem(value // bit, 2))
        bit *= 2
    return value


class Places:
    def __init__(self, n_fsdp, n_tp):
        self.n_fsdp, self.n_tp = n_fsdp, n_tp
        self.f, self.t = lax.axis_index("fsdp"), lax.axis_index("tp")
        self.chip, self.core = self.f // 2, lax.rem(self.f, 2)

    def near_f(self, k):
        return xor(self.chip, k) * 2 + self.core

    def near(self, k):
        return (self.near_f(k), self.t)

    def sibling(self):
        return (self.chip * 2 + 1 - self.core, self.t)

    def along(self, t):
        return (self.f, t)

    def greet(self):
        barrier = pltpu.get_barrier_semaphore()
        partners = [self.near(k) for k in range(1, self.n_fsdp // 2)] + [self.sibling()]
        partners += [self.along(lax.rem(self.t + k, self.n_tp)) for k in range(1, self.n_tp)]
        for partner in partners:
            pl.semaphore_signal(barrier, inc=1, device_id=partner, device_id_type=MESH)
        pl.semaphore_wait(barrier, len(partners))


def send(src, dst, send_sem, recv_sem, device):
    return pltpu.make_async_remote_copy(
        src_ref=src,
        dst_ref=dst,
        send_sem=send_sem,
        recv_sem=recv_sem,
        device_id=device,
        device_id_type=MESH,
    )


class Line:
    def __init__(self, at, own, slots, send_sems, recv_sems):
        self.at, self.own, self.slots = at, own, slots
        self.send_sems, self.recv_sems = send_sems, recv_sems

    def copy(self, slot, way, first):
        at = self.at
        return send(
            self.own if first else self.slots.at[slot],
            self.slots.at[slot],
            self.send_sems.at[way, slot],
            self.recv_sems.at[slot],
            at.along(at.t + 1 - 2 * way),
        )

    def start(self):
        at = self.at
        pl.when(at.t < at.n_tp - 1)(lambda: self.copy(at.t, 0, True).start())
        pl.when(at.t > 0)(lambda: self.copy(at.t, 1, True).start())

    def start_inner(self):
        at = self.at
        pl.when(at.t < at.n_tp - 2)(lambda: self.copy(at.t, 0, True).start())
        pl.when(at.t > 1)(lambda: self.copy(at.t, 1, True).start())

    def start_outer(self):
        at = self.at
        pl.when(at.t == at.n_tp - 2)(lambda: self.copy(at.t, 0, True).start())
        pl.when(at.t == 1)(lambda: self.copy(at.t, 1, True).start())

    def step(self, s, on=True):
        at = self.at

        @pl.when(at.t >= s)
        def _():
            self.copy(at.t - s, 0, False).wait_recv()
            if on:
                pl.when(at.t < at.n_tp - 1)(lambda: self.copy(at.t - s, 0, False).start())

        @pl.when(at.t + s < at.n_tp)
        def _():
            self.copy(at.t + s, 1, False).wait_recv()
            if on:
                pl.when(at.t > 0)(lambda: self.copy(at.t + s, 1, False).start())

    def finish(self, last=None):
        at = self.at
        for s in range(at.n_tp if last is None else last):
            pl.when((at.t >= s) & (at.t < at.n_tp - 1))(
                lambda s=s: self.copy(at.t - s, 0, s == 0).wait_send()
            )
            pl.when((at.t + s < at.n_tp) & (at.t > 0))(
                lambda s=s: self.copy(at.t + s, 1, s == 0).wait_send()
            )


class Shards:
    def __init__(self, at, own, whole, by_rows, near_sems, sib_sems, index):
        self.at, self.own, self.whole, self.by_rows = at, own, whole, by_rows
        self.near_sems, self.sib_sems, self.index = near_sems, sib_sems, index
        self.half = at.n_fsdp // 2
        self.relay = at.n_fsdp == 8
        self.direct = [1, 2] if self.relay else list(range(1, self.half))

    def slot(self, f, part=None):
        if self.by_rows:
            rows = self.whole.shape[-2] // self.at.n_fsdp
            first = f * rows
            if part is not None:
                rows = rows // 2
                first = first + part * rows
            here = pl.ds(pl.multiple_of(first, rows), rows)
            return self.whole.at[:, here, :] if len(self.whole.shape) == 3 else self.whole.at[here, :]
        width = self.whole.shape[1] // self.at.n_fsdp
        columns = pl.ds(pl.multiple_of(f * width, LANES), width)
        if part is None:
            return self.whole.at[:, columns]
        rows = self.whole.shape[0] // 2
        return self.whole.at[pl.ds(part * rows, rows), columns]

    def near_copy(self, k):
        return send(
            self.own,
            self.slot(self.at.f),
            self.near_sems.at[self.index, 0, k],
            self.near_sems.at[self.index, 1, k],
            self.at.near(k),
        )

    def start(self):
        for k in self.direct:
            self.near_copy(k).start()
        self.sib_copy(0).start()

    def arrived(self, k):
        slot = self.slot(self.at.near_f(k))
        send(
            slot,
            slot,
            self.near_sems.at[self.index, 0, k],
            self.near_sems.at[self.index, 1, k],
            self.at.near(k),
        ).wait_recv()

    def relay_copy(self, part):
        source, target = (1, 2) if part == 0 else (2, 1)
        slot = self.slot(self.at.near_f(source), part)
        return send(
            slot,
            slot,
            self.near_sems.at[self.index, 0, 3 + part],
            self.near_sems.at[self.index, 1, 3 + part],
            self.at.near(target),
        )

    def sib_copy(self, k):
        f = self.at.near_f(k)
        return send(
            self.own if k == 0 else self.slot(f),
            self.slot(f),
            self.sib_sems.at[self.index, 0, k],
            self.sib_sems.at[self.index, 1, k],
            self.at.sibling(),
        )

    def pass_on(self):
        for k in self.direct:
            self.arrived(k)
            if self.relay:
                self.relay_copy(k - 1).start()
        for k in self.direct:
            self.sib_copy(k).start()

    def pass_last(self):
        if self.relay:
            for part in range(2):
                slot = self.slot(self.at.near_f(3), part)
                send(
                    slot,
                    slot,
                    self.near_sems.at[self.index, 0, 3 + part],
                    self.near_sems.at[self.index, 1, 3 + part],
                    self.at.near(2 - part),
                ).wait_recv()
            self.sib_copy(3).start()

    def complete(self):
        for k in range(self.half):
            f = xor(self.at.chip, k) * 2 + 1 - self.at.core
            slot = self.slot(f)
            send(
                slot,
                slot,
                self.sib_sems.at[self.index, 0, k],
                self.sib_sems.at[self.index, 1, k],
                self.at.sibling(),
            ).wait_recv()

    def finish(self):
        for k in self.direct:
            self.near_copy(k).wait_send()
        if self.relay:
            for part in range(2):
                self.relay_copy(part).wait_send()
        for k in range(self.half):
            self.sib_copy(k).wait_send()


def norm_rows(values, gain_row, shift_row):
    average = jnp.mean(values, axis=-1, keepdims=True)
    centred = values - average
    variance = jnp.mean(centred * centred, axis=-1, keepdims=True)
    return centred * lax.rsqrt(variance + NORM_EPS) * gain_row + shift_row


def front_kernel(
    sizes, widest,
    tok, cot, wq, wo, wgu, wd, tile, cos, s_low, s_high, starts,
    one, q_out, k_out, v_out, resid, two, rows_out, att_out, cot_all, wq_all, wo_all, wgu_all, wd_all,
    toks, wq_v, wo_v, att, heads, vt, small, bias,
    tok_send, tok_recv, cot_send, cot_recv, near_sems, sib_sems, wz_sems, small_sems,
    swap_send, swap_recv, local_sems,
):
    n_fsdp, n_tp = sizes
    half = n_fsdp // 2
    at = Places(n_fsdp, n_tp)
    slab, model = tok.shape
    width = q_out.shape[1]
    each = wo.shape[0]
    at.greet()

    line = Line(at, tok, toks, tok_send, tok_recv)
    line.start()
    grads = Line(at, cot, cot_all, cot_send, cot_recv)
    weights = [
        Shards(at, wq, wq_all, True, near_sems, sib_sems, 0),
        None,
        Shards(at, wgu, wgu_all, True, near_sems, sib_sems, 2),
        Shards(at, wd, wd_all, False, near_sems, sib_sems, 3),
    ]
    weights[1] = Shards(at, None, wo_all, False, near_sems, sib_sems, 1)
    weights[1].own = weights[1].slot(at.f)
    weights[0].start()

    own_columns = pl.ds(pl.multiple_of(at.f * (model // n_fsdp), LANES), model // n_fsdp)

    def wo_rows(t):
        return wo_all.at[pl.ds(pl.multiple_of(t * each, each), each), own_columns]

    def wo_copy(k):
        return send(wo, wo_rows(at.t), wz_sems.at[0, k], wz_sems.at[1, k], at.along(lax.rem(at.t + k, n_tp)))

    for k in range(1, n_tp):
        wo_copy(k).start()
    own_copies = [
        pltpu.make_async_copy(tok, toks.at[at.t], local_sems.at[0]),
        pltpu.make_async_copy(wq, weights[0].slot(at.f), local_sems.at[1]),
        pltpu.make_async_copy(wo, wo_rows(at.t), local_sems.at[2]),
        pltpu.make_async_copy(wgu, weights[2].slot(at.f), local_sems.at[3]),
        pltpu.make_async_copy(wd, weights[3].slot(at.f), local_sems.at[4]),
        pltpu.make_async_copy(cot, cot_all.at[at.t], local_sems.at[5]),
    ]
    for copy in own_copies:
        copy.start()

    small[at.t, at.f] = tile[...]
    mine = small.at[at.t, at.f]
    to_sib = send(mine, mine, small_sems.at[0, 0], small_sems.at[1, 0], at.sibling())
    to_sib.start()
    to_sib.wait()
    pair = small.at[at.t, pl.ds(at.chip * 2, 2)]
    to_near = [
        send(pair, pair, small_sems.at[0, k], small_sems.at[1, k], at.near(k)) for k in range(1, half)
    ]
    for copy in to_near:
        copy.start()
    for k in range(1, half):
        to_near[k - 1].wait_send()
        came = small.at[at.t, pl.ds(xor(at.chip, k) * 2, 2)]
        send(came, came, small_sems.at[0, k], small_sems.at[1, k], at.near(k)).wait_recv()
    plane = small.at[at.t]
    to_line = [
        send(
            plane, plane, small_sems.at[0, half + k], small_sems.at[1, half + k],
            at.along(lax.rem(at.t + k, n_tp)),
        )
        for k in range(1, n_tp)
    ]
    for copy in to_line:
        copy.start()
    for k in range(1, n_tp):
        to_line[k - 1].wait_send()
        came = small.at[lax.rem(at.t + n_tp - k, n_tp)]
        send(
            came, came, small_sems.at[0, half + k], small_sems.at[1, half + k],
            at.along(lax.rem(at.t + k, n_tp)),
        ).wait_recv()
    lanes_each = model // (n_fsdp * n_tp)
    group = LANES // lanes_each
    for i in range(model // LANES):
        total = jnp.zeros((8, LANES), F32)
        for j in range(group):
            linear = i * group + j
            total = total + pltpu.roll(small[linear % n_tp, linear // n_tp], j * lanes_each, 1)
        rows_out[:, i * LANES : (i + 1) * LANES] = total
    for i in range(width // LANES):
        total = jnp.zeros((8, LANES), F32)
        for j in range(group):
            total = total + pltpu.roll(small[at.t, i * group + j], j * lanes_each, 1)
        bias[:, i * LANES : (i + 1) * LANES] = total
    own_copies[0].wait()

    def normalise(slot):
        step = 32

        def some(i, carry):
            here = pl.ds(pl.multiple_of(i * step, step), step)
            one[slot, here, :] = norm_rows(
                toks[slot, here, :].astype(F32), rows_out[0:1, :], rows_out[2:3, :]
            ).astype(BF16)
            return carry

        lax.fori_loop(0, slab // step, some, 0)

    wide = 256

    def project(slot):
        here = pl.ds(pl.multiple_of(slot * slab, slab), slab)
        for part, out in enumerate((q_out, k_out, v_out)):

            def some(i, carry, part=part, out=out):
                values = dot(
                    one[slot], wq_v[:, pl.ds(pl.multiple_of(part * width + i * wide, wide), wide)], NN
                )
                for j in range(wide // LANES):
                    lanes = pl.ds(pl.multiple_of(i * wide + j * LANES, LANES), LANES)
                    piece = values[:, j * LANES : (j + 1) * LANES] + bias[4 + part : 5 + part, lanes]
                    if part < 2:
                        piece = turn(piece, cos[here, :], s_low[here, :], s_high[here, :])
                    out[here, lanes] = piece.astype(BF16)
                return carry

            lax.fori_loop(0, width // wide, some, 0)

    def each_from(first, last, work):
        def some(i, carry):
            s = (i + 1) // 2
            slot = at.t + s * (2 * lax.rem(i, 2) - 1)
            pl.when((slot >= 0) & (slot < n_tp))(lambda: work(slot))
            return carry

        lax.fori_loop(max(0, 2 * first - 1), 2 * last - 1, some, 0)

    normalise(at.t)
    for s in range(1, n_tp - 1):
        line.step(s)
        if s == 1:
            weights[0].pass_on()
            own_copies[2].wait()
            for k in range(1, n_tp):
                wo_copy(k).wait_send()
                came = wo_rows(lax.rem(at.t + n_tp - k, n_tp))
                send(came, came, wz_sems.at[0, k], wz_sems.at[1, k], at.along(at.t)).wait_recv()
            weights[1].start()
        if s == 2:
            weights[0].pass_last()
            weights[2].start()
            grads.start_inner()
        each_from(s, s + 1, normalise)
    own_copies[1].wait()
    weights[0].complete()
    load = pltpu.make_async_copy(wq_all, wq_v, local_sems.at[6])
    load.start()
    load.wait()
    each_from(0, n_tp - 1, project)
    weights[1].pass_on()
    weights[3].start()
    line.step(n_tp - 1)
    grads.start_outer()
    each_from(n_tp - 1, n_tp, normalise)
    each_from(n_tp - 1, n_tp, project)

    def swap_copy(i, k):
        lanes = pl.ds(pl.multiple_of(i * LANES, LANES), LANES)
        columns = pl.ds(pl.multiple_of(at.t * width + i * LANES, LANES), LANES)
        other = lax.rem(at.t + k, n_tp)
        return send(
            heads.at[other, :, lanes], att.at[:, columns],
            swap_send.at[i, k], swap_recv.at[i, k], at.along(other),
        )

    def some_heads(i, carry):
        lanes = pl.ds(pl.multiple_of(i * LANES, LANES), LANES)
        attend(widest, q_out, k_out, v_out, starts, heads, vt, lanes, slab)
        for k in range(1, n_tp):
            swap_copy(i, k).start()
        columns = pl.ds(pl.multiple_of(at.t * width + i * LANES, LANES), LANES)
        att[:, columns] = heads[at.t, :, lanes]
        pl.when(i == width // LANES // 2 - 1)(weights[1].pass_last)
        return carry

    lax.fori_loop(0, width // LANES, some_heads, 0)
    weights[2].pass_on()
    weights[1].complete()
    load = pltpu.make_async_copy(wo_all, wo_v, local_sems.at[7])
    load.start()

    def took_heads(i, carry):
        for k in range(1, n_tp):
            swap_copy(i, k).wait_send()
            source = lax.rem(at.t + n_tp - k, n_tp)
            came = att.at[:, pl.ds(pl.multiple_of(source * width + i * LANES, LANES), LANES)]
            send(came, came, swap_send.at[i, k], swap_recv.at[i, k], at.along(source)).wait_recv()
        return carry

    lax.fori_loop(0, width // LANES, took_heads, 0)
    grads.step(1)
    keep = pltpu.make_async_copy(att, att_out, local_sems.at[8])
    keep.start()
    load.wait()

    def out_columns(i, carry):
        here = pl.ds(pl.multiple_of(i * wide, wide), wide)
        resid[:, here] = toks[at.t, :, here].astype(F32) + dot(att[...], wo_v[:, here], NN)
        return carry

    lax.fori_loop(0, model // wide, out_columns, 0)
    weights[3].pass_on()

    def second_norm(i, carry):
        here = pl.ds(pl.multiple_of(i * 32, 32), 32)
        two[here, :] = norm_rows(resid[here, :], rows_out[1:2, :], rows_out[3:4, :]).astype(BF16)
        return carry

    lax.fori_loop(0, slab // 32, second_norm, 0)

    weights[2].pass_last()
    weights[3].pass_last()
    for s in range(2, n_tp - 1):
        grads.step(s, on=s < n_tp - 2)
    for copy in own_copies[3:]:
        copy.wait()
    weights[2].complete()
    weights[3].complete()
    keep.wait()
    line.finish()
    grads.finish(n_tp - 2)
    for weight in weights:
        weight.finish()


def attend(widest, q_in, k_in, v_in, starts, heads, vt, lanes, slab):
    seq_len = q_in.shape[0]
    rows = min(256, seq_len)
    vt[...] = v_in[:, lanes].astype(F32).T.astype(BF16)
    for block in range(seq_len // rows):
        here = slice(block * rows, (block + 1) * rows)
        first, last = key_range(block, rows, widest)
        query_cols = (q_in[here, lanes].astype(F32) * HEAD**-0.5).T.astype(BF16)
        head_of = lax.broadcasted_iota(jnp.int32, query_cols.shape, 0) // HEAD
        parts = []
        for head in range(LANES // HEAD):
            own_cols = jnp.where(head_of == head, query_cols, jnp.zeros_like(query_cols))
            weights, total = seen_weights(
                k_in[first:last, lanes], own_cols, starts[:, here], first, block * rows
            )
            part = dot(vt[head * HEAD : (head + 1) * HEAD, first:last], weights.astype(BF16), NN)
            parts.append(part / total)
        found = jnp.concatenate(parts, axis=0).T.astype(BF16)
        for j in range(max(1, rows // slab)):
            count = min(slab, rows)
            row = block * rows + j * count
            heads[row // slab, row % slab : row % slab + count, lanes] = found[
                j * count : (j + 1) * count, :
            ]


def front(sizes, widest, tok, cot, wq, wo, wgu, wd, tile, tables, starts):
    n_fsdp, n_tp = sizes
    half = n_fsdp // 2
    slab, model = tok.shape
    seq_len = slab * n_tp
    width = wq.shape[1] // 3
    hidden = wd.shape[0]
    hbm = pl.BlockSpec(memory_space=pl.ANY)
    vmem = pl.BlockSpec(memory_space=pltpu.VMEM)
    shape = jax.ShapeDtypeStruct
    outs = [
        (shape((n_tp, slab, model), BF16), vmem),
        (shape((seq_len, width), BF16), vmem),
        (shape((seq_len, width), BF16), vmem),
        (shape((seq_len, width), BF16), vmem),
        (shape((slab, model), F32), vmem),
        (shape((slab, model), BF16), vmem),
        (shape((8, model), F32), vmem),
        (shape((slab, model), BF16), hbm),
        (shape((n_tp, slab, model), BF16), hbm),
        (shape((model, 3 * width), BF16), hbm),
        (shape((model, model), BF16), hbm),
        (shape((2, model, hidden), BF16), hbm),
        (shape((hidden, model), BF16), hbm),
    ]
    dma = pltpu.SemaphoreType.DMA
    pairs = width // LANES
    return pl.pallas_call(
        functools.partial(front_kernel, sizes, widest),
        in_specs=[vmem] * 11,
        out_specs=[spec for _, spec in outs],
        out_shape=[out for out, _ in outs],
        scratch_shapes=[
            pltpu.VMEM((n_tp, slab, model), BF16),
            pltpu.VMEM((model, 3 * width), BF16),
            pltpu.VMEM((model, model), BF16),
            pltpu.VMEM((slab, model), BF16),
            pltpu.VMEM((n_tp, slab, width), BF16),
            pltpu.VMEM((LANES, seq_len), BF16),
            pltpu.VMEM((n_tp, n_fsdp, 8, LANES), F32),
            pltpu.VMEM((8, width), F32),
            dma((2, n_tp)), dma((n_tp,)), dma((2, n_tp)), dma((n_tp,)),
            dma((4, 2, half + 1)), dma((4, 2, half)), dma((2, n_tp)), dma((2, half + n_tp)),
            dma((pairs, n_tp)), dma((pairs, n_tp)), dma((9,)),
        ],
        compiler_params=pltpu.CompilerParams(
            collective_id=1, has_side_effects=True, vmem_limit_bytes=60 * 2**20
        ),
        cost_estimate=pl.CostEstimate(flops=10**11, bytes_accessed=10**8, transcendentals=0),
    )(tok, cot, wq, wo, wgu, wd, tile, *tables, starts)


def xor_any(value, mask, bits):
    total = 0
    for b in range(bits):
        both = lax.rem(value // 2**b, 2) + lax.rem(mask // 2**b, 2)
        total = total + lax.rem(both, 2) * 2**b
    return total


class Fold:
    def __init__(self, at, total, going, came, tile, send_sems, recv_sems):
        self.at, self.total, self.going, self.came, self.tile = at, total, going, came, tile
        self.send_sems, self.recv_sems = send_sems, recv_sems
        self.tiles = total.shape[1] // tile

    def lanes(self, c):
        return pl.ds(pl.multiple_of(c * self.tile, self.tile), self.tile)

    def copy(self, j, c, way):
        at = self.at
        slot = j if way == 0 else j + (at.n_tp - j) * lax.max(0, j - at.t + 2)
        return send(
            self.going.at[j, :, self.lanes(c)],
            self.came.at[slot, :, self.lanes(c)],
            self.send_sems.at[j, c],
            self.recv_sems.at[slot, c],
            at.along(at.t + 1 - 2 * way),
        )

    def put(self, j, c, values):
        at = self.at

        @pl.when(j == at.t)
        def _():
            self.total[:, self.lanes(c)] = values

        @pl.when(j != at.t)
        def _():
            self.going[j, :, self.lanes(c)] = values.astype(BF16)

        pl.when((j > at.t) & (at.t == 0))(lambda: self.copy(j, c, 0).start())
        pl.when((j < at.t) & (at.t == at.n_tp - 1))(lambda: self.copy(j, c, 1).start())

    def arrived(self, slot, c):
        tile = self.came.at[slot, :, self.lanes(c)]
        send(
            tile, tile, self.send_sems.at[0, c], self.recv_sems.at[slot, c], self.at.along(self.at.t)
        ).wait_recv()

    def forward(self, key, c):
        at = self.at

        def some(j, way):
            self.arrived(j, c)
            here = self.lanes(c)
            self.going[j, :, here] = (
                self.going[j, :, here].astype(F32) + self.came[j, :, here].astype(F32)
            ).astype(BF16)
            self.copy(j, c, way).start()

        pl.when((key > at.t) & (at.t > 0))(lambda: some(key, 0))
        down = at.n_tp - 1 - key
        pl.when((down < at.t) & (at.t < at.n_tp - 1))(lambda: some(down, 1))

    def end(self):
        at = self.at

        def some(c, carry):
            here = self.lanes(c)

            @pl.when(at.t > 0)
            def _():
                self.arrived(at.t, c)
                self.total[:, here] = self.total[:, here] + self.came[at.t, :, here].astype(F32)

            @pl.when(at.t < at.n_tp - 1)
            def _():
                self.arrived(at.n_tp, c)
                self.total[:, here] = self.total[:, here] + self.came[at.n_tp, :, here].astype(F32)

            return carry

        lax.fori_loop(0, self.tiles, some, 0)

    def finish(self):
        at = self.at

        def some(i, carry):
            j, c = i // self.tiles, lax.rem(i, self.tiles)
            pl.when(j > at.t)(lambda: self.copy(j, c, 0).wait_send())
            pl.when(j < at.t)(lambda: self.copy(j, c, 1).wait_send())
            return carry

        lax.fori_loop(0, at.n_tp * self.tiles, some, 0)


class Spread:
    def __init__(self, at, sums, near, relay, boxes, sems, local_sems):
        self.at, self.sums, self.near, self.relay, self.boxes = at, sums, near, relay, boxes
        self.sems, self.local_sems = sems, local_sems
        self.half = at.n_fsdp // 2
        self.by_relay = at.n_fsdp == 8
        self.direct = [1, 2] if self.by_relay else list(range(1, self.half))
        self.rows = sums.shape[1] // 2

    def part(self, i, part):
        return self.sums.at[i, pl.ds(part * self.rows, self.rows)]

    def relay_copy(self, part):
        return send(
            self.part(3, part), self.relay.at[part],
            self.sems.at[0, 3 + part], self.sems.at[1, 3 + part], self.at.near(1 + part),
        )

    def near_copy(self, i):
        return send(
            self.sums.at[i], self.near.at[i], self.sems.at[0, i], self.sems.at[1, i], self.at.near(i)
        )

    def start(self):
        if self.by_relay:
            for part in range(2):
                self.relay_copy(part).start()
        else:
            for i in self.direct:
                self.near_copy(i).start()

    def relayed(self):
        for part in range(2):
            self.relay_copy(part).wait_send()
            self.relay_copy(part).wait_recv()

    def add(self, here=False):
        if not self.by_relay:
            return
        for part, i in ((0, 2), (1, 1)):
            if not here:
                self.relay_copy(part).wait_recv()
            takes = [
                pltpu.make_async_copy(self.part(i, part), self.boxes.at[0], self.local_sems.at[0]),
                pltpu.make_async_copy(self.relay.at[part], self.boxes.at[1], self.local_sems.at[1]),
            ]
            for take in takes:
                take.start()
            for take in takes:
                take.wait()
            self.boxes[0] = (self.boxes[0].astype(F32) + self.boxes[1].astype(F32)).astype(BF16)
            keep = pltpu.make_async_copy(self.boxes.at[0], self.part(i, part), self.local_sems.at[0])
            keep.start()
            keep.wait()
            self.near_copy(i).start()

    def arrived(self):
        for i in self.direct:
            self.near_copy(i).wait_recv()

    def finish(self, relays=True):
        if self.by_relay and relays:
            for part in range(2):
                self.relay_copy(part).wait_send()
        for i in self.direct:
            self.near_copy(i).wait_send()


def middle_kernel(
    sizes,
    two, cot_all, wgu_all, wd_all,
    gn2, branch, sum_gu, sum_d, sib_gu, sib_d, relay_gu, relay_d,
    hidden, x, cots, wgu_v, wd_v, ggu, acts, came, going, stage_gu, stage_d, in_gu, in_d,
    line_send, line_recv, fold_send, fold_recv, sib_send, sib_recv, cot_sems, relay_sems, local_sems,
):
    n_fsdp, n_tp = sizes
    half = n_fsdp // 2
    bits = half.bit_length() - 1
    at = Places(n_fsdp, n_tp)
    slab, model = two.shape
    part_rows = model // n_fsdp
    at.greet()
    line = Line(at, two, x, line_send, line_recv)
    line.start()
    loads = [
        pltpu.make_async_copy(two, x.at[at.t], local_sems.at[0]),
        pltpu.make_async_copy(wgu_all, wgu_v, local_sems.at[1]),
        pltpu.make_async_copy(wd_all, wd_v, local_sems.at[2]),
    ]
    for load in loads:
        load.start()

    def cot_copy(j):
        return pltpu.make_async_copy(cot_all.at[j], cots.at[j], cot_sems.at[0, j])

    def cot_last(slot, way):
        return send(
            cot_all.at[slot], cots.at[slot], cot_sems.at[1, slot], cot_sems.at[2, slot], at.along(at.t + 1 - 2 * way)
        )

    for j in range(n_tp):
        pl.when((at.t - j < n_tp - 1) & (j - at.t < n_tp - 1))(cot_copy(j).start)
    for load in loads:
        load.wait()
    for j in range(n_tp):
        pl.when((at.t - j < n_tp - 1) & (j - at.t < n_tp - 1))(cot_copy(j).wait)
    fold = Fold(at, gn2, going, came, min(512, model), fold_send, fold_recv)

    def unit(slot):
        here = pl.ds(pl.multiple_of(slot * slab, slab), slab)
        acts[0] = dot(x[slot], wgu_v[0], NN)
        acts[1] = dot(x[slot], wgu_v[1], NN)
        acts[2] = dot(cots[slot], wd_v[...], NT)
        step = 16

        def some(i, carry):
            local_rows = pl.ds(pl.multiple_of(i * step, step), step)
            rows = pl.ds(pl.multiple_of(slot * slab + i * step, step), step)
            gate, up, grad = acts[0, local_rows, :], acts[1, local_rows, :], acts[2, local_rows, :]
            low = jax.nn.sigmoid(gate)
            act = gate * low
            hidden[rows, :] = (act * up).astype(BF16)
            ggu[0, rows, :] = (grad * up * low * (1.0 + gate * (1.0 - low))).astype(BF16)
            ggu[1, rows, :] = (grad * act).astype(BF16)
            return carry

        lax.fori_loop(0, slab // step, some, 0)

        def tiles(c, carry):
            rows = fold.lanes(c)
            fold.put(
                slot,
                c,
                dot(ggu[0, here, :], wgu_v[0, rows, :], NT) + dot(ggu[1, here, :], wgu_v[1, rows, :], NT),
            )
            return carry

        lax.fori_loop(0, fold.tiles, tiles, 0)

        def branch_copy(c):
            return pltpu.make_async_copy(
                stage_gu.at[c // 2 % 2, c % 2, pl.ds(0, slab), pl.ds(0, fold.tile)],
                branch.at[slot, :, fold.lanes(c)],
                local_sems.at[4 + c % 4],
            )

        for c in range(fold.tiles):
            if c >= 4:
                branch_copy(c - 4).wait()
            stage_gu[c // 2 % 2, c % 2, 0:slab, 0 : fold.tile] = dot(
                hidden[here, :], wd_v[:, c * fold.tile : (c + 1) * fold.tile], NN
            ).astype(BF16)
            branch_copy(c).start()
        for c in range(max(0, fold.tiles - 4), fold.tiles):
            branch_copy(c).wait()

    def each_from(first, last, work):
        def some(i, carry):
            s = (i + 1) // 2
            slot = at.t + s * (2 * lax.rem(i, 2) - 1)
            pl.when((slot >= 0) & (slot < n_tp))(lambda: work(slot))
            return carry

        lax.fori_loop(max(0, 2 * first - 1), 2 * last - 1, some, 0)

    for s in range(n_tp):
        if s:
            line.step(s)
        if s == 1:
            pl.when(at.t == n_tp - 2)(lambda: cot_last(0, 0).start())
            pl.when(at.t == 1)(lambda: cot_last(n_tp - 1, 1).start())
        if s == n_tp - 1:
            pl.when(at.t == n_tp - 1)(lambda: cot_last(0, 0).wait_recv())
            pl.when(at.t == 0)(lambda: cot_last(n_tp - 1, 1).wait_recv())
        each_from(s, s + 1, unit)

    for key in range(1, n_tp - 2):
        for c in range(fold.tiles):
            fold.forward(key, c)

    def block(f, take):
        columns = pl.ds(pl.multiple_of(f * part_rows, part_rows), part_rows)
        for part in range(2):
            rows = x[:, :, columns].reshape(n_tp * slab, part_rows)
            take(part, dot(rows, ggu[part], TN))
        grads = cots[:, :, columns].reshape(n_tp * slab, part_rows)
        take(2, dot(hidden[...], grads, TN))

    spreads = [
        Spread(at, sum_gu, None, relay_gu, None, relay_sems.at[0], None),
        Spread(at, sum_d, None, relay_d, None, relay_sems.at[1], None),
    ]
    by_relay = spreads[0].by_relay

    def order(n):
        return lax.rem(n + half - 1, half) if by_relay else n

    def sib_copies(n):
        i, slot = order(n), lax.rem(n, 2)
        return [
            send(stage_gu.at[slot], sib_gu.at[i], sib_send.at[0, i], sib_recv.at[0, i], at.sibling()),
            send(stage_d.at[slot], sib_d.at[i], sib_send.at[1, i], sib_recv.at[1, i], at.sibling()),
        ]

    def keep_copies(n):
        i, slot = order(n), lax.rem(n, 2)
        return [
            pltpu.make_async_copy(stage_gu.at[slot], sum_gu.at[i], local_sems.at[4 + slot]),
            pltpu.make_async_copy(stage_d.at[slot], sum_d.at[i], local_sems.at[6 + slot]),
        ]

    def others(n, carry):
        pl.when(n < fold.tiles)(lambda: fold.forward(n_tp - 2, n))

        @pl.when(n >= 2)
        def _():
            for copy in sib_copies(n - 2):
                copy.wait_send()

        def take(part, values):
            if part < 2:
                stage_gu[lax.rem(n, 2), part] = values.astype(BF16)
            else:
                stage_d[lax.rem(n, 2)] = values.astype(BF16)

        block(xor_any(at.chip, order(n), bits) * 2 + 1 - at.core, take)
        for copy in sib_copies(n):
            copy.start()
        return carry

    lax.fori_loop(0, half, others, 0)
    for n in range(half - 2, half):
        for copy in sib_copies(jnp.int32(n)):
            copy.wait_send()

    def mine(n, carry):
        for copy in sib_copies(n):
            copy.wait_recv()
        takes = [
            pltpu.make_async_copy(sib_gu.at[order(n)], in_gu, local_sems.at[8]),
            pltpu.make_async_copy(sib_d.at[order(n)], in_d, local_sems.at[9]),
        ]
        for take in takes:
            take.start()

        @pl.when(n >= 2)
        def _():
            for copy in keep_copies(n - 2):
                copy.wait()

        if by_relay:

            @pl.when(n == 2)
            def _():
                for spread in spreads:
                    spread.start()

        def take(part, values):
            if part == 0:
                for copy in takes:
                    copy.wait()
            if part < 2:
                stage_gu[lax.rem(n, 2), part] = (values + in_gu[part].astype(F32)).astype(BF16)
            else:
                stage_d[lax.rem(n, 2)] = (values + in_d[...].astype(F32)).astype(BF16)

        block(xor_any(at.chip, order(n), bits) * 2 + at.core, take)
        for copy in keep_copies(n):
            copy.start()
        return carry

    lax.fori_loop(0, half, mine, 0)
    for c in range(fold.tiles):
        fold.forward(n_tp - 1, c)
    fold.end()
    for i in range(half - 2, half):
        for copy in keep_copies(jnp.int32(i)):
            copy.wait()
    line.finish()
    pl.when(at.t == n_tp - 2)(lambda: cot_last(0, 0).wait_send())
    pl.when(at.t == 1)(lambda: cot_last(n_tp - 1, 1).wait_send())
    fold.finish()
    if by_relay:
        for spread in spreads:
            spread.relayed()


def middle(sizes, two, cot_all, wgu_all, wd_all):
    n_fsdp, n_tp = sizes
    half = n_fsdp // 2
    slab, model = two.shape
    hidden = wd_all.shape[0]
    part_rows = model // n_fsdp
    tile = min(512, model)
    hbm = pl.BlockSpec(memory_space=pl.ANY)
    vmem = pl.BlockSpec(memory_space=pltpu.VMEM)
    shape = jax.ShapeDtypeStruct
    outs = [
        (shape((slab, model), F32), vmem),
        (shape((n_tp, slab, model), BF16), hbm),
        (shape((half, 2, part_rows, hidden), BF16), hbm),
        (shape((half, hidden, part_rows), BF16), hbm),
        (shape((half, 2, part_rows, hidden), BF16), hbm),
        (shape((half, hidden, part_rows), BF16), hbm),
        (shape((2, 1, part_rows, hidden), BF16), hbm),
        (shape((2, hidden // 2, part_rows), BF16), hbm),
    ]
    dma = pltpu.SemaphoreType.DMA
    return pl.pallas_call(
        functools.partial(middle_kernel, sizes),
        in_specs=[hbm] * 4,
        out_specs=[spec for _, spec in outs],
        out_shape=[out for out, _ in outs],
        scratch_shapes=[
            pltpu.VMEM((n_tp * slab, hidden), BF16),
            pltpu.VMEM((n_tp, slab, model), BF16),
            pltpu.VMEM((n_tp, slab, model), BF16),
            pltpu.VMEM((2, model, hidden), BF16),
            pltpu.VMEM((hidden, model), BF16),
            pltpu.VMEM((2, n_tp * slab, hidden), BF16),
            pltpu.VMEM((3, slab, hidden), F32),
            pltpu.VMEM((n_tp + 1, slab, model), BF16),
            pltpu.VMEM((n_tp, slab, model), BF16),
            pltpu.VMEM((2, 2, part_rows, hidden), BF16),
            pltpu.VMEM((2, hidden, part_rows), BF16),
            pltpu.VMEM((2, part_rows, hidden), BF16),
            pltpu.VMEM((hidden, part_rows), BF16),
            dma((2, n_tp)), dma((n_tp,)), dma((n_tp, model // tile)), dma((n_tp + 1, model // tile)),
            dma((2, half)), dma((2, half)), dma((3, n_tp)), dma((2, 2, half + 1)), dma((10,)),
        ],
        compiler_params=pltpu.CompilerParams(
            collective_id=3, has_side_effects=True, vmem_limit_bytes=62 * 2**20
        ),
        cost_estimate=pl.CostEstimate(flops=10**11, bytes_accessed=10**8, transcendentals=0),
    )(two, cot_all, wgu_all, wd_all)


class Pair:
    def __init__(self, at, stage, sib, sums, inbox, sems, local_sems):
        self.at, self.stage, self.sib, self.sums, self.inbox = at, stage, sib, sums, inbox
        self.sems, self.local_sems = sems, local_sems

    def sib_copy(self, i):
        return send(
            self.stage.at[lax.rem(i, 2)], self.sib.at[i], self.sems.at[0, i], self.sems.at[1, i], self.at.sibling()
        )

    def keep_copy(self, i):
        return pltpu.make_async_copy(
            self.stage.at[lax.rem(i, 2)], self.sums.at[i], self.local_sems.at[lax.rem(i, 2)]
        )

    def give(self, i, values):
        pl.when(i >= 2)(lambda: self.sib_copy(i - 2).wait_send())
        self.stage[lax.rem(i, 2)] = values().astype(BF16)
        self.sib_copy(i).start()

    def given(self, half):
        for i in range(half - 2, half):
            self.sib_copy(jnp.int32(i)).wait_send()

    def keep(self, i, values):
        self.sib_copy(i).wait_recv()
        take = pltpu.make_async_copy(self.sib.at[i], self.inbox, self.local_sems.at[2])
        take.start()
        pl.when(i >= 2)(lambda: self.keep_copy(i - 2).wait())
        own = values()
        take.wait()
        self.stage[lax.rem(i, 2)] = (own + self.inbox[...].astype(F32)).astype(BF16)
        self.keep_copy(i).start()

    def kept(self, half):
        for i in range(half - 2, half):
            self.keep_copy(jnp.int32(i)).wait()


def norm_back(values, incoming, gain_row):
    average = jnp.mean(values, axis=-1, keepdims=True)
    centred = values - average
    scale = lax.rsqrt(jnp.mean(centred * centred, axis=-1, keepdims=True) + NORM_EPS)
    unit = centred * scale
    grads = incoming * gain_row
    inner = jnp.mean(grads * unit, axis=-1, keepdims=True)
    back = scale * (grads - jnp.mean(grads, axis=-1, keepdims=True) - unit * inner)
    return back, jnp.sum(incoming * unit, axis=0, keepdims=True), jnp.sum(incoming, axis=0, keepdims=True)


def attend_back(widest, q_in, k_in, v_in, g_in, cos, s_low, s_high, starts, g_out, bias, kt, dk, dv, first_lane):
    seq_len, width = q_in.shape
    rows = min(256, seq_len)
    lanes = pl.ds(pl.multiple_of(first_lane, LANES), LANES)
    kt[...] = k_in[:, lanes].astype(F32).T.astype(BF16)
    dk[...] = jnp.zeros_like(dk)
    dv[...] = jnp.zeros_like(dv)

    def put(part, here, values):
        columns = pl.ds(pl.multiple_of(part * width + first_lane, LANES), LANES)
        low = values.astype(BF16)
        g_out[here, columns] = low
        return jnp.sum(low.astype(F32), axis=0, keepdims=True)

    total_q = jnp.zeros((1, LANES), F32)
    for block in range(seq_len // rows):
        here = slice(block * rows, (block + 1) * rows)
        first, last = key_range(block, rows, widest)
        query_rows = (q_in[here, lanes].astype(F32) * HEAD**-0.5).astype(BF16)
        grad_rows = g_in[here, lanes]
        query_cols = query_rows.astype(F32).T.astype(BF16)
        grad_cols = grad_rows.astype(F32).T.astype(BF16)
        head_down = lax.broadcasted_iota(jnp.int32, query_cols.shape, 0) // HEAD
        head_along = lax.broadcasted_iota(jnp.int32, query_rows.shape, 1) // HEAD
        none_down, none_along = jnp.zeros_like(query_cols), jnp.zeros_like(query_rows)
        parts = []
        for head in range(LANES // HEAD):
            weights, total = seen_weights(
                k_in[first:last, lanes],
                jnp.where(head_down == head, query_cols, none_down),
                starts[:, here],
                first,
                block * rows,
            )
            probs = weights * (1.0 / total)
            grad_probs = dot(
                v_in[first:last, lanes], jnp.where(head_down == head, grad_cols, none_down), NN
            )
            inner = jnp.sum(probs * grad_probs, axis=0, keepdims=True)
            grad_scores = (probs * (grad_probs - inner)).astype(BF16)
            dk[first:last, :] += dot(
                grad_scores, jnp.where(head_along == head, query_rows, none_along), NN
            )
            dv[first:last, :] += dot(
                probs.astype(BF16), jnp.where(head_along == head, grad_rows, none_along), NN
            )
            parts.append(dot(kt[head * HEAD : (head + 1) * HEAD, first:last], grad_scores, NN))
        grad_queries = jnp.concatenate(parts, axis=0).T * HEAD**-0.5
        total_q = total_q + put(
            0, here, turn(grad_queries, cos[here, :], -s_low[here, :], -s_high[here, :])
        )
    everywhere = slice(0, seq_len)
    bias[4:5, lanes] = total_q
    bias[5:6, lanes] = put(1, everywhere, turn(dk[...], cos[...], -s_low[...], -s_high[...]))
    bias[6:7, lanes] = put(2, everywhere, dv[...])


def back_kernel(
    sizes, widest,
    gn2, resid, tok, cot, att_own, wo_all, wq_all, q_in, k_in, v_in, one, sum_gu_in, sum_d_in,
    relay_gu, relay_d, rows_in, cos, s_low, s_high, starts,
    grad_tok, small_out, near_gu, near_d, own_gu, own_d, sum_q, near_q, sib_q, relay_q,
    sum_o, near_o, sib_o, relay_o, zo,
    gres, res_v, tok_v, cot_v, att_v, gattn, wo_v, wq_v, q_v, k_v, v_v, gp, gatt, ghead, came, going,
    kt, dk, dv, stage_o, inbox_o, stage_q, inbox_q, box_gu, box_d, box_o, box_q, zo_stage, zo_box,
    norm_sums, bias, tiles, land_z, land_near, land_sib,
    swap_send, swap_recv, fold_send, fold_recv, pair_o_sems, pair_q_sems, gu_sems, d_sems, o_sems, q_sems,
    zo_sems, small_sems, local_sems, pair_o_local, pair_q_local,
):
    n_fsdp, n_tp = sizes
    half = n_fsdp // 2
    bits = half.bit_length() - 1
    at = Places(n_fsdp, n_tp)
    slab, model = tok.shape
    seq_len, width = q_in.shape
    part_rows = model // n_fsdp
    pairs = width // LANES
    loads = [
        pltpu.make_async_copy(src, dst, local_sems.at[i])
        for i, (src, dst) in enumerate(
            [
                (gn2, gres), (resid, res_v), (cot, cot_v), (wo_all, wo_v), (tok, tok_v), (att_own, att_v),
                (q_in, q_v), (k_in, k_v), (v_in, v_v), (wq_all, wq_v),
            ]
        )
    ]
    for load in loads:
        load.start()
    at.greet()
    spread_gu = Spread(at, own_gu, near_gu, relay_gu, box_gu, gu_sems, local_sems.at[pl.ds(13, 2)])
    spread_d = Spread(at, own_d, near_d, relay_d, box_d, d_sems, local_sems.at[pl.ds(13, 2)])
    spread_o = Spread(at, sum_o, near_o, relay_o, box_o, o_sems, local_sems.at[pl.ds(13, 2)])
    spread_q = Spread(at, sum_q, near_q, relay_q, box_q, q_sems, local_sems.at[pl.ds(13, 2)])
    if not spread_gu.by_relay:
        spread_gu.start()
        spread_d.start()
    norm_sums[...] = jnp.zeros_like(norm_sums)
    bias[...] = jnp.zeros_like(bias)
    for load in loads[:4]:
        load.wait()

    step = 16

    def second(i, carry):
        here = pl.ds(pl.multiple_of(i * step, step), step)
        back, gain, shift = norm_back(res_v[here, :], gres[here, :], rows_in[1:2, :])
        total = cot_v[here, :].astype(F32) + back
        gres[here, :] = total
        gattn[here, :] = total.astype(BF16)
        norm_sums[1:2, :] = norm_sums[1:2, :] + gain
        norm_sums[3:4, :] = norm_sums[3:4, :] + shift
        return carry

    lax.fori_loop(0, slab // step, second, 0)

    def swap_copy(i, k):
        lanes = pl.ds(pl.multiple_of(i * LANES, LANES), LANES)
        other = lax.rem(at.t + k, n_tp)
        return send(
            ghead.at[other, :, lanes],
            gatt.at[pl.ds(pl.multiple_of(at.t * slab, slab), slab), lanes],
            swap_send.at[i, k], swap_recv.at[i, k], at.along(other),
        )

    def give_heads(i, carry):
        lanes = pl.ds(pl.multiple_of(i * LANES, LANES), LANES)

        def to(k, carry):
            other = lax.rem(at.t + k, n_tp)
            rows = pl.ds(pl.multiple_of(other * width + i * LANES, LANES), LANES)
            ghead[other, :, lanes] = dot(gattn[...], wo_v[rows, :], NT).astype(BF16)
            pl.when(k > 0)(lambda: swap_copy(i, k).start())
            return carry

        lax.fori_loop(0, n_tp, to, 0)
        gatt[pl.ds(pl.multiple_of(at.t * slab, slab), slab), lanes] = ghead[at.t, :, lanes]
        return carry

    lax.fori_loop(0, pairs, give_heads, 0)

    spread_gu.add(here=True)
    spread_d.add(here=True)

    loads[5].wait()
    pair_o = Pair(at, stage_o, sib_o, sum_o, inbox_o, pair_o_sems, pair_o_local)
    pair_q = Pair(at, stage_q, sib_q, sum_q, inbox_q, pair_q_sems, pair_q_local)

    def piece(f):
        return pl.ds(pl.multiple_of(f * part_rows, part_rows), part_rows)

    def owner(i, core):
        return xor_any(at.chip, i, bits) * 2 + core

    def give_o(i, carry):
        pair_o.give(i, lambda: dot(att_v[...], gattn[:, piece(owner(i, 1 - at.core))], TN))
        return carry

    lax.fori_loop(0, half, give_o, 0)
    for load in loads[6:9]:
        load.wait()
    load_one = pltpu.make_async_copy(one, wo_v.at[pl.ds(0, seq_len), :], local_sems.at[12])
    load_one.start()

    def some_heads(i, carry):
        for k in range(1, n_tp):
            source = lax.rem(at.t + n_tp - k, n_tp)
            lanes = pl.ds(pl.multiple_of(i * LANES, LANES), LANES)
            came_rows = gatt.at[pl.ds(pl.multiple_of(source * slab, slab), slab), lanes]
            send(came_rows, came_rows, swap_send.at[i, k], swap_recv.at[i, k], at.along(source)).wait_recv()
        attend_back(
            widest, q_v, k_v, v_v, gatt, cos, s_low, s_high, starts, gp, bias, kt, dk, dv, i * LANES
        )

        def keep_o(n, carry):
            pair_o.keep(n, lambda: dot(att_v[...], gattn[:, piece(owner(n, at.core))], TN))
            return carry

        lax.fori_loop(i * half // pairs, (i + 1) * half // pairs, keep_o, 0)
        return carry

    pair_o.given(half)
    lax.fori_loop(0, pairs, some_heads, 0)
    pair_o.kept(half)
    spread_o.start()

    loads[9].wait()
    fold = Fold(at, grad_tok, going, came, min(512, model), fold_send, fold_recv)

    def term(slot):
        rows = gp[pl.ds(pl.multiple_of(slot * slab, slab), slab), :]

        def some(c, carry):
            fold.put(slot, c, dot(rows, wq_v[fold.lanes(c), :], NT))
            return carry

        lax.fori_loop(0, fold.tiles, some, 0)

    def far_first(i, carry):
        s = (2 * n_tp - 1 - i) // 2
        slot = at.t + s * (2 * lax.rem(i, 2) - 1)
        pl.when((slot >= 0) & (slot < n_tp))(lambda: term(slot))
        return carry

    lax.fori_loop(0, 2 * n_tp - 1, far_first, 0)

    spread_o.add()
    load_one.wait()

    def give_q(i, carry):
        pair_q.give(i, lambda: dot(wo_v[0:seq_len, piece(owner(i, 1 - at.core))], gp[...], TN))
        return carry

    lax.fori_loop(0, half, give_q, 0)
    pair_q.given(half)

    def keep_q(i, carry):
        pair_q.keep(i, lambda: dot(wo_v[0:seq_len, piece(owner(i, at.core))], gp[...], TN))
        return carry

    lax.fori_loop(0, half, keep_q, 0)
    pair_q.kept(half)
    spread_q.start()
    for c in range(fold.tiles):
        fold.forward(n_tp - 1, c)
    spread_q.add()
    for key in range(n_tp - 2, 0, -1):
        for c in range(fold.tiles):
            fold.forward(key, c)

    each = model // n_tp
    spread_o.arrived()

    def zo_copy(k):
        other = lax.rem(at.t + k, n_tp)
        return send(zo_stage.at[other], zo.at[at.t], zo_sems.at[0, k], zo_sems.at[1, k], at.along(other))

    def group(k, carry):
        other = lax.rem(at.t + k, n_tp)
        rows = pl.ds(pl.multiple_of(other * each, each), each)
        takes = [
            pltpu.make_async_copy(
                (sum_o if i == 0 else near_o).at[i, rows, :], zo_box.at[n], local_sems.at[16 + n]
            )
            for n, i in enumerate([0] + spread_o.direct)
        ]
        for take in takes:
            take.start()
        total = jnp.zeros(zo_box.shape[1:], F32)
        for n, take in enumerate(takes):
            take.wait()
            total = total + zo_box[n].astype(F32)
        zo_stage[other] = total.astype(BF16)
        return carry

    lax.fori_loop(0, n_tp, group, 0)
    own_zo = pltpu.make_async_copy(zo_stage.at[at.t], zo.at[at.t], local_sems.at[15])
    own_zo.start()

    fold.end()
    for k in range(1, n_tp):
        zo_copy(k).start()
    loads[4].wait()

    def first(i, carry):
        here = pl.ds(pl.multiple_of(i * step, step), step)
        back, gain, shift = norm_back(tok_v[here, :].astype(F32), grad_tok[here, :], rows_in[0:1, :])
        grad_tok[here, :] = gres[here, :] + back
        norm_sums[0:1, :] = norm_sums[0:1, :] + gain
        norm_sums[2:3, :] = norm_sums[2:3, :] + shift
        return carry

    lax.fori_loop(0, slab // step, first, 0)

    lanes_each = model // (n_fsdp * n_tp)
    kept = lax.broadcasted_iota(jnp.int32, (8, LANES), 1) < lanes_each

    def tile_of(ref, index):
        start = index * lanes_each
        tile = ref[:, start // LANES * LANES : start // LANES * LANES + LANES]
        return jnp.where(kept, pltpu.roll(tile, (LANES - start % LANES) % LANES, 1), 0.0)

    for f in range(n_fsdp):
        for t in range(n_tp):
            tiles[t, f] = tile_of(norm_sums, f * n_tp + t)
    for f in range(n_fsdp):
        tiles[at.t, f] = tiles[at.t, f] + tile_of(bias, f)

    def z_copy(k):
        other = lax.rem(at.t + k, n_tp)
        return send(
            tiles.at[other], land_z.at[k], small_sems.at[0, half + k], small_sems.at[1, half + k], at.along(other)
        )

    for k in range(1, n_tp):
        z_copy(k).start()
    total = tiles[at.t]
    for k in range(1, n_tp):
        z_copy(k).wait_recv()
        total = total + land_z[k]
    land_z[0] = total

    def chip_copy(k):
        return send(
            land_z.at[0, pl.ds(xor(at.chip, k) * 2, 2)], land_near.at[k],
            small_sems.at[0, k], small_sems.at[1, k], at.near(k),
        )

    for k in range(1, half):
        chip_copy(k).start()
    total = land_z[0, pl.ds(at.chip * 2, 2)]
    for k in range(1, half):
        chip_copy(k).wait_recv()
        total = total + land_near[k]
    land_near[0] = total
    to_sib = send(
        land_near.at[0, 1 - at.core], land_sib, small_sems.at[0, 0], small_sems.at[1, 0], at.sibling()
    )
    to_sib.start()
    to_sib.wait_recv()
    small_out[...] = land_near[0, at.core] + land_sib[...]

    to_sib.wait_send()
    for k in range(1, half):
        chip_copy(k).wait_send()
    for k in range(1, n_tp):
        z_copy(k).wait_send()
        zo_copy(k).wait_send()
        source = lax.rem(at.t + n_tp - k, n_tp)
        send(zo.at[source], zo.at[source], zo_sems.at[0, k], zo_sems.at[1, k], at.along(source)).wait_recv()
    own_zo.wait()

    def swapped(i, carry):
        for k in range(1, n_tp):
            swap_copy(i, k).wait_send()
        return carry

    lax.fori_loop(0, pairs, swapped, 0)
    fold.finish()
    for spread in (spread_gu, spread_d, spread_q):
        spread.arrived()
    for spread in (spread_gu, spread_d):
        spread.finish(relays=False)
    for spread in (spread_q, spread_o):
        spread.finish()


def back(sizes, widest, gn2, resid, tok, cot, att_own, wo_all, wq_all, q_in, k_in, v_in, one, sum_gu, sum_d, relay_gu, relay_d, rows_in, tables, starts):
    n_fsdp, n_tp = sizes
    half = n_fsdp // 2
    slab, model = tok.shape
    seq_len, width = q_in.shape
    hidden = sum_d.shape[1]
    part_rows = model // n_fsdp
    pairs = width // LANES
    each = model // n_tp
    tile = min(512, model)
    hbm = pl.BlockSpec(memory_space=pl.ANY)
    vmem = pl.BlockSpec(memory_space=pltpu.VMEM)
    shape = jax.ShapeDtypeStruct
    piece_q, piece_o = (part_rows, 3 * width), (model, part_rows)
    piece_gu, piece_d = sum_gu.shape[1:], sum_d.shape[1:]
    halved = lambda piece: (piece[0] // 2,) + tuple(piece[1:])
    outs = [
        (shape((slab, model), F32), vmem),
        (shape((8, LANES), F32), vmem),
        (shape(sum_gu.shape, BF16), hbm),
        (shape(sum_d.shape, BF16), hbm),
        (shape(sum_gu.shape, BF16), hbm),
        (shape(sum_d.shape, BF16), hbm),
        (shape((half,) + piece_q, BF16), hbm),
        (shape((half,) + piece_q, BF16), hbm),
        (shape((half,) + piece_q, BF16), hbm),
        (shape((2,) + halved(piece_q), BF16), hbm),
        (shape((half,) + piece_o, BF16), hbm),
        (shape((half,) + piece_o, BF16), hbm),
        (shape((half,) + piece_o, BF16), hbm),
        (shape((2,) + halved(piece_o), BF16), hbm),
        (shape((n_tp, each, part_rows), BF16), hbm),
    ]
    dma = pltpu.SemaphoreType.DMA
    return pl.pallas_call(
        functools.partial(back_kernel, sizes, widest),
        in_specs=[hbm] * 15 + [vmem] * 5,
        out_specs=[spec for _, spec in outs],
        out_shape=[out for out, _ in outs],
        scratch_shapes=[
            pltpu.VMEM((slab, model), F32),
            pltpu.VMEM((slab, model), F32),
            pltpu.VMEM((slab, model), BF16),
            pltpu.VMEM((slab, model), BF16),
            pltpu.VMEM((slab, model), BF16),
            pltpu.VMEM((slab, model), BF16),
            pltpu.VMEM((model, model), BF16),
            pltpu.VMEM((model, 3 * width), BF16),
            pltpu.VMEM((seq_len, width), BF16),
            pltpu.VMEM((seq_len, width), BF16),
            pltpu.VMEM((seq_len, width), BF16),
            pltpu.VMEM((seq_len, 3 * width), BF16),
            pltpu.VMEM((seq_len, width), BF16),
            pltpu.VMEM((n_tp, slab, width), BF16),
            pltpu.VMEM((n_tp + 1, slab, model), BF16),
            pltpu.VMEM((n_tp, slab, model), BF16),
            pltpu.VMEM((LANES, seq_len), BF16),
            pltpu.VMEM((seq_len, LANES), F32),
            pltpu.VMEM((seq_len, LANES), F32),
            pltpu.VMEM((2,) + piece_o, BF16),
            pltpu.VMEM(piece_o, BF16),
            pltpu.VMEM((2,) + piece_q, BF16),
            pltpu.VMEM(piece_q, BF16),
            pltpu.VMEM((2,) + halved(piece_gu), BF16),
            pltpu.VMEM((2,) + halved(piece_d), BF16),
            pltpu.VMEM((2,) + halved(piece_o), BF16),
            pltpu.VMEM((2,) + halved(piece_q), BF16),
            pltpu.VMEM((n_tp, each, part_rows), BF16),
            pltpu.VMEM((half, each, part_rows), BF16),
            pltpu.VMEM((8, model), F32),
            pltpu.VMEM((8, width), F32),
            pltpu.VMEM((n_tp, n_fsdp, 8, LANES), F32),
            pltpu.VMEM((n_tp, n_fsdp, 8, LANES), F32),
            pltpu.VMEM((half, 2, 8, LANES), F32),
            pltpu.VMEM((8, LANES), F32),
            dma((pairs, n_tp)), dma((pairs, n_tp)),
            dma((n_tp, model // tile)), dma((n_tp + 1, model // tile)),
            dma((2, half)), dma((2, half)),
            dma((2, half + 1)), dma((2, half + 1)), dma((2, half + 1)), dma((2, half + 1)),
            dma((2, n_tp)), dma((2, half + n_tp)), dma((16 + half,)), dma((3,)), dma((3,)),
        ],
        input_output_aliases={11: 4, 12: 5},
        compiler_params=pltpu.CompilerParams(
            collective_id=2, has_side_effects=True, vmem_limit_bytes=62 * 2**20
        ),
        cost_estimate=pl.CostEstimate(flops=10**11, bytes_accessed=10**8, transcendentals=0),
    )(
        gn2, resid, tok, cot, att_own, wo_all, wq_all, q_in, k_in, v_in, one, sum_gu, sum_d,
        relay_gu, relay_d, rows_in, *tables, starts,
    )


def reduce_rows(values):
    return lax.psum_scatter(values.astype(BF16), "tp", scatter_dimension=0, tiled=True).astype(F32)


def local(tokens, lengths, ln_gains, ln_shifts, w_qkv, b_qkv, w_out, w_gate_up, w_down, cotangent):
    n_fsdp, n_tp = lax.axis_size("fsdp"), lax.axis_size("tp")
    sizes = (n_fsdp, n_tp)
    at_tp = lax.axis_index("tp")
    slab_rows, model_width = tokens.shape
    seq_len = slab_rows * n_tp
    small = ln_gains.shape[1]
    local_width = w_qkv.shape[2]
    hidden_width = w_gate_up.shape[2]
    part_rows = w_qkv.shape[0]

    length_row = lengths[0]
    doc_ends = jnp.cumsum(length_row)
    ids = jnp.arange(seq_len, dtype=jnp.int32)
    passed = (doc_ends[None, :] <= ids[:, None]).astype(jnp.int32)
    starts = jnp.sum(passed * length_row[None, :], axis=1)
    places = (ids - starts).astype(F32)
    lane = jnp.arange(LANES, dtype=jnp.int32) % HEAD
    frequency = 10000.0 ** (-2.0 * (lane % (ROT // 2)).astype(F32) / ROT)
    angles = places[:, None] * frequency[None, :]
    cosine = jnp.where(lane[None] < ROT, jnp.cos(angles), 1.0)
    sine = jnp.sin(angles)
    sine_low = jnp.where(lane[None] < ROT // 2, -sine, 0.0)
    sine_high = jnp.where((lane[None] >= ROT // 2) & (lane[None] < ROT), sine, 0.0)
    tables = (cosine, sine_low, sine_high)
    starts_row = starts.reshape(1, seq_len).astype(jnp.int32)
    widest = seq_len // 2

    tile = jnp.concatenate([ln_gains, ln_shifts, b_qkv.astype(F32), jnp.zeros((1, small), F32)], 0)
    tile = jnp.pad(tile, ((0, 0), (0, LANES - small)))
    (
        full_one, queries, key_vals, value_rows, residual, normed_two, norm_rows_all, attended_own,
        grad_branch, qkv_all, out_all, gu_all, down_all,
    ) = front(
        sizes, widest, tokens, cotangent, w_qkv.reshape(part_rows, 3 * local_width), w_out,
        w_gate_up.transpose(1, 0, 2), w_down, tile, tables, starts_row,
    )
    full_one = full_one.reshape(seq_len, model_width)

    grad_normed_two, branch_terms, sum_gu, sum_down, _, _, relay_gu, relay_down = middle(
        sizes, normed_two, grad_branch, gu_all, down_all
    )
    (
        grad_tokens, shares, near_gu, near_down, own_gu, own_down, sum_qkv, near_qkv, _, _, _, _, _, _,
        out_parts,
    ) = back(
        sizes, widest, grad_normed_two, residual, tokens, cotangent, attended_own, out_all, qkv_all,
        queries, key_vals, value_rows, full_one, sum_gu, sum_down, relay_gu, relay_down,
        norm_rows_all, tables, starts_row,
    )
    branch = reduce_rows(branch_terms.reshape(seq_len, model_width))
    result = (residual + branch).astype(BF16)
    direct = [1, 2] if n_fsdp == 8 else list(range(1, n_fsdp // 2))

    def total(sums, near):
        return sum([near[i].astype(F32) for i in direct], sums[0].astype(F32))

    shares = shares[:, :small]
    return (
        result,
        grad_tokens,
        shares[0:2],
        shares[2:4],
        total(sum_qkv, near_qkv).reshape(part_rows, 3, local_width),
        shares[4:7],
        jnp.sum(out_parts.astype(F32), axis=0),
        total(own_gu, near_gu).transpose(1, 0, 2),
        total(own_down, near_down),
    )


def solution(mesh):
    placed = (
        P(("fsdp", "tp"), None),
        P("fsdp", None),
        P(None, ("fsdp", "tp")),
        P(None, ("fsdp", "tp")),
        P("fsdp", None, "tp"),
        P(None, ("tp", "fsdp")),
        P("tp", "fsdp"),
        P("fsdp", None, "tp"),
        P("tp", "fsdp"),
        P(("fsdp", "tp"), None),
    )
    return jax.shard_map(
        local,
        mesh=mesh,
        in_specs=placed,
        out_specs=(
            P(("fsdp", "tp"), None),
            P(("fsdp", "tp"), None),
            P(None, ("fsdp", "tp")),
            P(None, ("fsdp", "tp")),
            P("fsdp", None, "tp"),
            P(None, ("tp", "fsdp")),
            P("tp", "fsdp"),
            P("fsdp", None, "tp"),
            P("tp", "fsdp"),
        ),
        check_vma=False,
    )
```

```python
import functools

import jax
import jax.numpy as jnp
from jax import lax
from jax.experimental import pallas as pl
from jax.experimental.pallas import tpu as pltpu
from jax.sharding import PartitionSpec as P

HEAD = 64
ROT = 16
NORM_EPS = 1e-05
LANES = 128
MESH = pl.DeviceIdType.MESH
NN = (((1,), (0,)), ((), ()))
NT = (((1,), (1,)), ((), ()))
TN = (((0,), (0,)), ((), ()))
F32 = jnp.float32
BF16 = jnp.bfloat16


def dot(left, right, dims):
    return lax.dot_general(left, right, dims, preferred_element_type=F32)


def turn(values, cosine, sine_low, sine_high):
    return (
        values * cosine
        + pltpu.roll(values, LANES - ROT // 2, 1) * sine_low
        + pltpu.roll(values, ROT // 2, 1) * sine_high
    )


def key_range(block, rows, widest):
    first = max(0, block * rows - widest)
    return first, (block + 1) * rows


def seen_weights(key_rows, query_cols, starts_row, first_key, first_query):
    scores = dot(key_rows, query_cols, NN)
    key_ids = first_key + lax.broadcasted_iota(jnp.int32, scores.shape, 0)
    query_ids = first_query + lax.broadcasted_iota(jnp.int32, scores.shape, 1)
    seen = (key_ids <= query_ids) & (key_ids >= starts_row)
    scores = jnp.where(seen, scores, -1e30)
    top = jnp.max(scores, axis=0, keepdims=True)
    weights = jnp.exp(scores - top)
    return weights, jnp.sum(weights, axis=0, keepdims=True)


def xor(value, mask):
    bit = 1
    while bit <= mask:
        if mask & bit:
            value = value + bit * (1 - 2 * lax.rem(value // bit, 2))
        bit *= 2
    return value


class Places:
    def __init__(self, n_fsdp, n_tp):
        self.n_fsdp, self.n_tp = n_fsdp, n_tp
        self.f, self.t = lax.axis_index("fsdp"), lax.axis_index("tp")
        self.chip, self.core = self.f // 2, lax.rem(self.f, 2)

    def near_f(self, k):
        return xor(self.chip, k) * 2 + self.core

    def near(self, k):
        return (self.near_f(k), self.t)

    def sibling(self):
        return (self.chip * 2 + 1 - self.core, self.t)

    def along(self, t):
        return (self.f, t)

    def greet(self):
        barrier = pltpu.get_barrier_semaphore()
        partners = [self.near(k) for k in range(1, self.n_fsdp // 2)] + [self.sibling()]
        partners += [self.along(lax.rem(self.t + k, self.n_tp)) for k in range(1, self.n_tp)]
        for partner in partners:
            pl.semaphore_signal(barrier, inc=1, device_id=partner, device_id_type=MESH)
        pl.semaphore_wait(barrier, len(partners))


def send(src, dst, send_sem, recv_sem, device):
    return pltpu.make_async_remote_copy(
        src_ref=src,
        dst_ref=dst,
        send_sem=send_sem,
        recv_sem=recv_sem,
        device_id=device,
        device_id_type=MESH,
    )


class Line:
    def __init__(self, at, own, slots, send_sems, recv_sems):
        self.at, self.own, self.slots = at, own, slots
        self.send_sems, self.recv_sems = send_sems, recv_sems

    def copy(self, slot, way, first):
        at = self.at
        return send(
            self.own if first else self.slots.at[slot],
            self.slots.at[slot],
            self.send_sems.at[way, slot],
            self.recv_sems.at[slot],
            at.along(at.t + 1 - 2 * way),
        )

    def start(self):
        at = self.at
        pl.when(at.t < at.n_tp - 1)(lambda: self.copy(at.t, 0, True).start())
        pl.when(at.t > 0)(lambda: self.copy(at.t, 1, True).start())

    def start_inner(self):
        at = self.at
        pl.when(at.t < at.n_tp - 2)(lambda: self.copy(at.t, 0, True).start())
        pl.when(at.t > 1)(lambda: self.copy(at.t, 1, True).start())

    def start_outer(self):
        at = self.at
        pl.when(at.t == at.n_tp - 2)(lambda: self.copy(at.t, 0, True).start())
        pl.when(at.t == 1)(lambda: self.copy(at.t, 1, True).start())

    def step(self, s, on=True):
        at = self.at

        @pl.when(at.t >= s)
        def _():
            self.copy(at.t - s, 0, False).wait_recv()
            if on:
                pl.when(at.t < at.n_tp - 1)(lambda: self.copy(at.t - s, 0, False).start())

        @pl.when(at.t + s < at.n_tp)
        def _():
            self.copy(at.t + s, 1, False).wait_recv()
            if on:
                pl.when(at.t > 0)(lambda: self.copy(at.t + s, 1, False).start())

    def finish(self, last=None):
        at = self.at
        for s in range(at.n_tp if last is None else last):
            pl.when((at.t >= s) & (at.t < at.n_tp - 1))(
                lambda s=s: self.copy(at.t - s, 0, s == 0).wait_send()
            )
            pl.when((at.t + s < at.n_tp) & (at.t > 0))(
                lambda s=s: self.copy(at.t + s, 1, s == 0).wait_send()
            )


class Shards:
    def __init__(self, at, own, whole, by_rows, near_sems, sib_sems, index):
        self.at, self.own, self.whole, self.by_rows = at, own, whole, by_rows
        self.near_sems, self.sib_sems, self.index = near_sems, sib_sems, index
        self.half = at.n_fsdp // 2
        self.relay = at.n_fsdp == 8
        self.direct = [1, 2] if self.relay else list(range(1, self.half))

    def slot(self, f, part=None):
        if self.by_rows:
            rows = self.whole.shape[-2] // self.at.n_fsdp
            first = f * rows
            if part is not None:
                rows = rows // 2
                first = first + part * rows
            here = pl.ds(pl.multiple_of(first, rows), rows)
            return self.whole.at[:, here, :] if len(self.whole.shape) == 3 else self.whole.at[here, :]
        width = self.whole.shape[1] // self.at.n_fsdp
        columns = pl.ds(pl.multiple_of(f * width, LANES), width)
        if part is None:
            return self.whole.at[:, columns]
        rows = self.whole.shape[0] // 2
        return self.whole.at[pl.ds(part * rows, rows), columns]

    def near_copy(self, k):
        return send(
            self.own,
            self.slot(self.at.f),
            self.near_sems.at[self.index, 0, k],
            self.near_sems.at[self.index, 1, k],
            self.at.near(k),
        )

    def start(self):
        for k in self.direct:
            self.near_copy(k).start()
        self.sib_copy(0).start()

    def arrived(self, k):
        slot = self.slot(self.at.near_f(k))
        send(
            slot,
            slot,
            self.near_sems.at[self.index, 0, k],
            self.near_sems.at[self.index, 1, k],
            self.at.near(k),
        ).wait_recv()

    def relay_copy(self, part):
        source, target = (1, 2) if part == 0 else (2, 1)
        slot = self.slot(self.at.near_f(source), part)
        return send(
            slot,
            slot,
            self.near_sems.at[self.index, 0, 3 + part],
            self.near_sems.at[self.index, 1, 3 + part],
            self.at.near(target),
        )

    def sib_copy(self, k):
        f = self.at.near_f(k)
        return send(
            self.own if k == 0 else self.slot(f),
            self.slot(f),
            self.sib_sems.at[self.index, 0, k],
            self.sib_sems.at[self.index, 1, k],
            self.at.sibling(),
        )

    def pass_on(self):
        for k in self.direct:
            self.arrived(k)
            if self.relay:
                self.relay_copy(k - 1).start()
        for k in self.direct:
            self.sib_copy(k).start()

    def pass_last(self):
        if self.relay:
            for part in range(2):
                slot = self.slot(self.at.near_f(3), part)
                send(
                    slot,
                    slot,
                    self.near_sems.at[self.index, 0, 3 + part],
                    self.near_sems.at[self.index, 1, 3 + part],
                    self.at.near(2 - part),
                ).wait_recv()
            self.sib_copy(3).start()

    def complete(self):
        for k in range(self.half):
            f = xor(self.at.chip, k) * 2 + 1 - self.at.core
            slot = self.slot(f)
            send(
                slot,
                slot,
                self.sib_sems.at[self.index, 0, k],
                self.sib_sems.at[self.index, 1, k],
                self.at.sibling(),
            ).wait_recv()

    def finish(self):
        for k in self.direct:
            self.near_copy(k).wait_send()
        if self.relay:
            for part in range(2):
                self.relay_copy(part).wait_send()
        for k in range(self.half):
            self.sib_copy(k).wait_send()


def norm_rows(values, gain_row, shift_row):
    average = jnp.mean(values, axis=-1, keepdims=True)
    centred = values - average
    variance = jnp.mean(centred * centred, axis=-1, keepdims=True)
    return centred * lax.rsqrt(variance + NORM_EPS) * gain_row + shift_row


def front_kernel(
    sizes, widest,
    tok, cot, wq, wo, wgu, wd, tile, turns, starts,
    one, q_out, k_out, v_out, resid, two, rows_out, att_out, cot_all, wq_all, wo_all, wgu_all, wd_all,
    cos, s_low, s_high,
    toks, wq_v, wo_v, att, heads, vt, small, bias,
    tok_send, tok_recv, cot_send, cot_recv, near_sems, sib_sems, wz_sems, small_sems,
    swap_send, swap_recv, local_sems,
):
    n_fsdp, n_tp = sizes
    half = n_fsdp // 2
    at = Places(n_fsdp, n_tp)
    slab, model = tok.shape
    width = q_out.shape[1]
    each = wo.shape[0]
    at.greet()

    line = Line(at, tok, toks, tok_send, tok_recv)
    line.start()
    grads = Line(at, cot, cot_all, cot_send, cot_recv)
    weights = [
        Shards(at, wq, wq_all, True, near_sems, sib_sems, 0),
        None,
        Shards(at, wgu, wgu_all, True, near_sems, sib_sems, 2),
        Shards(at, wd, wd_all, False, near_sems, sib_sems, 3),
    ]
    weights[1] = Shards(at, None, wo_all, False, near_sems, sib_sems, 1)
    weights[1].own = weights[1].slot(at.f)
    weights[0].start()

    own_columns = pl.ds(pl.multiple_of(at.f * (model // n_fsdp), LANES), model // n_fsdp)

    def wo_rows(t):
        return wo_all.at[pl.ds(pl.multiple_of(t * each, each), each), own_columns]

    def wo_copy(k):
        return send(wo, wo_rows(at.t), wz_sems.at[0, k], wz_sems.at[1, k], at.along(lax.rem(at.t + k, n_tp)))

    for k in range(1, n_tp):
        wo_copy(k).start()
    own_copies = [
        pltpu.make_async_copy(tok, toks.at[at.t], local_sems.at[0]),
        pltpu.make_async_copy(wq, weights[0].slot(at.f), local_sems.at[1]),
        pltpu.make_async_copy(wo, wo_rows(at.t), local_sems.at[2]),
        pltpu.make_async_copy(wgu, weights[2].slot(at.f), local_sems.at[3]),
        pltpu.make_async_copy(wd, weights[3].slot(at.f), local_sems.at[4]),
        pltpu.make_async_copy(cot, cot_all.at[at.t], local_sems.at[5]),
    ]
    for copy in own_copies:
        copy.start()

    eight = ROT // 2
    cosine, sine = turns[0:eight, :], turns[eight : 2 * eight, :]
    none = jnp.zeros_like(sine)
    flat = jnp.zeros((HEAD - ROT, turns.shape[1]), F32)
    cos[...] = jnp.concatenate([cosine, cosine, flat + 1.0] * 2, axis=0).T
    s_low[...] = jnp.concatenate([-sine, none, flat] * 2, axis=0).T
    s_high[...] = jnp.concatenate([none, sine, flat] * 2, axis=0).T

    small[at.t, at.f] = tile[...]
    mine = small.at[at.t, at.f]
    to_sib = send(mine, mine, small_sems.at[0, 0], small_sems.at[1, 0], at.sibling())
    to_sib.start()
    to_sib.wait()
    pair = small.at[at.t, pl.ds(at.chip * 2, 2)]
    to_near = [
        send(pair, pair, small_sems.at[0, k], small_sems.at[1, k], at.near(k)) for k in range(1, half)
    ]
    for copy in to_near:
        copy.start()
    for k in range(1, half):
        to_near[k - 1].wait_send()
        came = small.at[at.t, pl.ds(xor(at.chip, k) * 2, 2)]
        send(came, came, small_sems.at[0, k], small_sems.at[1, k], at.near(k)).wait_recv()
    plane = small.at[at.t]
    to_line = [
        send(
            plane, plane, small_sems.at[0, half + k], small_sems.at[1, half + k],
            at.along(lax.rem(at.t + k, n_tp)),
        )
        for k in range(1, n_tp)
    ]
    for copy in to_line:
        copy.start()
    for k in range(1, n_tp):
        to_line[k - 1].wait_send()
        came = small.at[lax.rem(at.t + n_tp - k, n_tp)]
        send(
            came, came, small_sems.at[0, half + k], small_sems.at[1, half + k],
            at.along(lax.rem(at.t + k, n_tp)),
        ).wait_recv()
    lanes_each = model // (n_fsdp * n_tp)
    group = LANES // lanes_each
    for i in range(model // LANES):
        total = jnp.zeros((8, LANES), F32)
        for j in range(group):
            linear = i * group + j
            total = total + pltpu.roll(small[linear % n_tp, linear // n_tp], j * lanes_each, 1)
        rows_out[:, i * LANES : (i + 1) * LANES] = total
    for i in range(width // LANES):
        total = jnp.zeros((8, LANES), F32)
        for j in range(group):
            total = total + pltpu.roll(small[at.t, i * group + j], j * lanes_each, 1)
        bias[:, i * LANES : (i + 1) * LANES] = total
    own_copies[0].wait()

    def normalise(slot):
        step = 32

        def some(i, carry):
            here = pl.ds(pl.multiple_of(i * step, step), step)
            one[slot, here, :] = norm_rows(
                toks[slot, here, :].astype(F32), rows_out[0:1, :], rows_out[2:3, :]
            ).astype(BF16)
            return carry

        lax.fori_loop(0, slab // step, some, 0)

    wide = 256

    def project(slot):
        here = pl.ds(pl.multiple_of(slot * slab, slab), slab)
        for part, out in enumerate((q_out, k_out, v_out)):

            def some(i, carry, part=part, out=out):
                values = dot(
                    one[slot], wq_v[:, pl.ds(pl.multiple_of(part * width + i * wide, wide), wide)], NN
                )
                for j in range(wide // LANES):
                    lanes = pl.ds(pl.multiple_of(i * wide + j * LANES, LANES), LANES)
                    piece = values[:, j * LANES : (j + 1) * LANES] + bias[4 + part : 5 + part, lanes]
                    if part < 2:
                        piece = turn(piece, cos[here, :], s_low[here, :], s_high[here, :])
                    out[here, lanes] = piece.astype(BF16)
                return carry

            lax.fori_loop(0, width // wide, some, 0)

    def each_from(first, last, work):
        def some(i, carry):
            s = (i + 1) // 2
            slot = at.t + s * (2 * lax.rem(i, 2) - 1)
            pl.when((slot >= 0) & (slot < n_tp))(lambda: work(slot))
            return carry

        lax.fori_loop(max(0, 2 * first - 1), 2 * last - 1, some, 0)

    normalise(at.t)
    for s in range(1, n_tp - 1):
        line.step(s)
        if s == 1:
            weights[0].pass_on()
            own_copies[2].wait()
            for k in range(1, n_tp):
                wo_copy(k).wait_send()
                came = wo_rows(lax.rem(at.t + n_tp - k, n_tp))
                send(came, came, wz_sems.at[0, k], wz_sems.at[1, k], at.along(at.t)).wait_recv()
            weights[1].start()
        if s == 2:
            weights[0].pass_last()
            weights[2].start()
            grads.start_inner()
        each_from(s, s + 1, normalise)
    own_copies[1].wait()
    weights[0].complete()
    load = pltpu.make_async_copy(wq_all, wq_v, local_sems.at[6])
    load.start()
    load.wait()
    each_from(0, n_tp - 1, project)
    weights[1].pass_on()
    weights[3].start()
    line.step(n_tp - 1)
    grads.start_outer()
    each_from(n_tp - 1, n_tp, normalise)
    each_from(n_tp - 1, n_tp, project)

    def swap_copy(i, k):
        lanes = pl.ds(pl.multiple_of(i * LANES, LANES), LANES)
        columns = pl.ds(pl.multiple_of(at.t * width + i * LANES, LANES), LANES)
        other = lax.rem(at.t + k, n_tp)
        return send(
            heads.at[other, :, lanes], att.at[:, columns],
            swap_send.at[i, k], swap_recv.at[i, k], at.along(other),
        )

    def some_heads(i, carry):
        lanes = pl.ds(pl.multiple_of(i * LANES, LANES), LANES)
        attend(widest, q_out, k_out, v_out, starts, heads, vt, lanes, slab)
        for k in range(1, n_tp):
            swap_copy(i, k).start()
        columns = pl.ds(pl.multiple_of(at.t * width + i * LANES, LANES), LANES)
        att[:, columns] = heads[at.t, :, lanes]
        pl.when(i == width // LANES // 2 - 1)(weights[1].pass_last)
        return carry

    lax.fori_loop(0, width // LANES, some_heads, 0)
    weights[2].pass_on()
    weights[1].complete()
    load = pltpu.make_async_copy(wo_all, wo_v, local_sems.at[7])
    load.start()

    def took_heads(i, carry):
        for k in range(1, n_tp):
            swap_copy(i, k).wait_send()
            source = lax.rem(at.t + n_tp - k, n_tp)
            came = att.at[:, pl.ds(pl.multiple_of(source * width + i * LANES, LANES), LANES)]
            send(came, came, swap_send.at[i, k], swap_recv.at[i, k], at.along(source)).wait_recv()
        return carry

    lax.fori_loop(0, width // LANES, took_heads, 0)
    grads.step(1)
    keep = pltpu.make_async_copy(att, att_out, local_sems.at[8])
    keep.start()
    load.wait()

    def out_columns(i, carry):
        here = pl.ds(pl.multiple_of(i * wide, wide), wide)
        resid[:, here] = toks[at.t, :, here].astype(F32) + dot(att[...], wo_v[:, here], NN)
        return carry

    lax.fori_loop(0, model // wide, out_columns, 0)
    weights[3].pass_on()

    def second_norm(i, carry):
        here = pl.ds(pl.multiple_of(i * 32, 32), 32)
        two[here, :] = norm_rows(resid[here, :], rows_out[1:2, :], rows_out[3:4, :]).astype(BF16)
        return carry

    lax.fori_loop(0, slab // 32, second_norm, 0)

    weights[2].pass_last()
    weights[3].pass_last()
    for s in range(2, n_tp - 1):
        grads.step(s, on=s < n_tp - 2)
    for copy in own_copies[3:]:
        copy.wait()
    weights[2].complete()
    weights[3].complete()
    keep.wait()
    line.finish()
    grads.finish(n_tp - 2)
    for weight in weights:
        weight.finish()


def attend(widest, q_in, k_in, v_in, starts, heads, vt, lanes, slab):
    seq_len = q_in.shape[0]
    rows = min(256, seq_len)
    vt[...] = v_in[:, lanes].astype(F32).T.astype(BF16)
    for block in range(seq_len // rows):
        here = slice(block * rows, (block + 1) * rows)
        first, last = key_range(block, rows, widest)
        query_cols = (q_in[here, lanes].astype(F32) * HEAD**-0.5).T.astype(BF16)
        head_of = lax.broadcasted_iota(jnp.int32, query_cols.shape, 0) // HEAD
        parts = []
        for head in range(LANES // HEAD):
            own_cols = jnp.where(head_of == head, query_cols, jnp.zeros_like(query_cols))
            weights, total = seen_weights(
                k_in[first:last, lanes], own_cols, starts[:, here], first, block * rows
            )
            part = dot(vt[head * HEAD : (head + 1) * HEAD, first:last], weights.astype(BF16), NN)
            parts.append(part / total)
        found = jnp.concatenate(parts, axis=0).T.astype(BF16)
        for j in range(max(1, rows // slab)):
            count = min(slab, rows)
            row = block * rows + j * count
            heads[row // slab, row % slab : row % slab + count, lanes] = found[
                j * count : (j + 1) * count, :
            ]


def front(sizes, widest, tok, cot, wq, wo, wgu, wd, tile, turns, starts):
    n_fsdp, n_tp = sizes
    half = n_fsdp // 2
    slab, model = tok.shape
    seq_len = slab * n_tp
    width = wq.shape[1] // 3
    hidden = wd.shape[0]
    hbm = pl.BlockSpec(memory_space=pl.ANY)
    vmem = pl.BlockSpec(memory_space=pltpu.VMEM)
    shape = jax.ShapeDtypeStruct
    outs = [
        (shape((n_tp, slab, model), BF16), vmem),
        (shape((seq_len, width), BF16), vmem),
        (shape((seq_len, width), BF16), vmem),
        (shape((seq_len, width), BF16), vmem),
        (shape((slab, model), F32), vmem),
        (shape((slab, model), BF16), vmem),
        (shape((8, model), F32), vmem),
        (shape((slab, model), BF16), hbm),
        (shape((n_tp, slab, model), BF16), hbm),
        (shape((model, 3 * width), BF16), hbm),
        (shape((model, model), BF16), hbm),
        (shape((2, model, hidden), BF16), hbm),
        (shape((hidden, model), BF16), hbm),
    ] + [(shape((seq_len, LANES), F32), vmem)] * 3
    dma = pltpu.SemaphoreType.DMA
    pairs = width // LANES
    return pl.pallas_call(
        functools.partial(front_kernel, sizes, widest),
        in_specs=[vmem] * 9,
        out_specs=[spec for _, spec in outs],
        out_shape=[out for out, _ in outs],
        scratch_shapes=[
            pltpu.VMEM((n_tp, slab, model), BF16),
            pltpu.VMEM((model, 3 * width), BF16),
            pltpu.VMEM((model, model), BF16),
            pltpu.VMEM((slab, model), BF16),
            pltpu.VMEM((n_tp, slab, width), BF16),
            pltpu.VMEM((LANES, seq_len), BF16),
            pltpu.VMEM((n_tp, n_fsdp, 8, LANES), F32),
            pltpu.VMEM((8, width), F32),
            dma((2, n_tp)), dma((n_tp,)), dma((2, n_tp)), dma((n_tp,)),
            dma((4, 2, half + 1)), dma((4, 2, half)), dma((2, n_tp)), dma((2, half + n_tp)),
            dma((pairs, n_tp)), dma((pairs, n_tp)), dma((9,)),
        ],
        compiler_params=pltpu.CompilerParams(
            collective_id=1, has_side_effects=True, vmem_limit_bytes=60 * 2**20
        ),
        cost_estimate=pl.CostEstimate(flops=10**11, bytes_accessed=10**8, transcendentals=0),
    )(tok, cot, wq, wo, wgu, wd, tile, turns, starts)


def xor_any(value, mask, bits):
    total = 0
    for b in range(bits):
        both = lax.rem(value // 2**b, 2) + lax.rem(mask // 2**b, 2)
        total = total + lax.rem(both, 2) * 2**b
    return total


class Fold:
    def __init__(self, at, total, going, came, tile, send_sems, recv_sems):
        self.at, self.total, self.going, self.came, self.tile = at, total, going, came, tile
        self.send_sems, self.recv_sems = send_sems, recv_sems
        self.tiles = total.shape[1] // tile

    def lanes(self, c):
        return pl.ds(pl.multiple_of(c * self.tile, self.tile), self.tile)

    def copy(self, j, c, way):
        at = self.at
        slot = j if way == 0 else j + (at.n_tp - j) * lax.max(0, j - at.t + 2)
        return send(
            self.going.at[j, :, self.lanes(c)],
            self.came.at[slot, :, self.lanes(c)],
            self.send_sems.at[j, c],
            self.recv_sems.at[slot, c],
            at.along(at.t + 1 - 2 * way),
        )

    def put(self, j, c, values):
        at = self.at

        @pl.when(j == at.t)
        def _():
            self.total[:, self.lanes(c)] = values

        @pl.when(j != at.t)
        def _():
            self.going[j, :, self.lanes(c)] = values.astype(BF16)

        pl.when((j > at.t) & (at.t == 0))(lambda: self.copy(j, c, 0).start())
        pl.when((j < at.t) & (at.t == at.n_tp - 1))(lambda: self.copy(j, c, 1).start())

    def arrived(self, slot, c):
        tile = self.came.at[slot, :, self.lanes(c)]
        send(
            tile, tile, self.send_sems.at[0, c], self.recv_sems.at[slot, c], self.at.along(self.at.t)
        ).wait_recv()

    def forward(self, key, c):
        at = self.at

        def some(j, way):
            self.arrived(j, c)
            here = self.lanes(c)
            self.going[j, :, here] = (
                self.going[j, :, here].astype(F32) + self.came[j, :, here].astype(F32)
            ).astype(BF16)
            self.copy(j, c, way).start()

        pl.when((key > at.t) & (at.t > 0))(lambda: some(key, 0))
        down = at.n_tp - 1 - key
        pl.when((down < at.t) & (at.t < at.n_tp - 1))(lambda: some(down, 1))

    def end(self):
        at = self.at

        def some(c, carry):
            here = self.lanes(c)

            @pl.when(at.t > 0)
            def _():
                self.arrived(at.t, c)
                self.total[:, here] = self.total[:, here] + self.came[at.t, :, here].astype(F32)

            @pl.when(at.t < at.n_tp - 1)
            def _():
                self.arrived(at.n_tp, c)
                self.total[:, here] = self.total[:, here] + self.came[at.n_tp, :, here].astype(F32)

            return carry

        lax.fori_loop(0, self.tiles, some, 0)

    def finish(self):
        at = self.at

        def some(i, carry):
            j, c = i // self.tiles, lax.rem(i, self.tiles)
            pl.when(j > at.t)(lambda: self.copy(j, c, 0).wait_send())
            pl.when(j < at.t)(lambda: self.copy(j, c, 1).wait_send())
            return carry

        lax.fori_loop(0, at.n_tp * self.tiles, some, 0)


class Spread:
    def __init__(self, at, sums, near, relay, boxes, sems, local_sems):
        self.at, self.sums, self.near, self.relay, self.boxes = at, sums, near, relay, boxes
        self.sems, self.local_sems = sems, local_sems
        self.half = at.n_fsdp // 2
        self.by_relay = at.n_fsdp == 8
        self.direct = [1, 2] if self.by_relay else list(range(1, self.half))
        self.rows = sums.shape[1] // 2

    def part(self, i, part):
        return self.sums.at[i, pl.ds(part * self.rows, self.rows)]

    def relay_copy(self, part):
        return send(
            self.part(3, part), self.relay.at[part],
            self.sems.at[0, 3 + part], self.sems.at[1, 3 + part], self.at.near(1 + part),
        )

    def near_copy(self, i):
        return send(
            self.sums.at[i], self.near.at[i], self.sems.at[0, i], self.sems.at[1, i], self.at.near(i)
        )

    def start(self):
        if self.by_relay:
            for part in range(2):
                self.relay_copy(part).start()
        else:
            for i in self.direct:
                self.near_copy(i).start()

    def relayed(self):
        for part in range(2):
            self.relay_copy(part).wait_send()
            self.relay_copy(part).wait_recv()

    def add(self, here=False):
        if not self.by_relay:
            return
        for part, i in ((0, 2), (1, 1)):
            if not here:
                self.relay_copy(part).wait_recv()
            takes = [
                pltpu.make_async_copy(self.part(i, part), self.boxes.at[0], self.local_sems.at[0]),
                pltpu.make_async_copy(self.relay.at[part], self.boxes.at[1], self.local_sems.at[1]),
            ]
            for take in takes:
                take.start()
            for take in takes:
                take.wait()
            self.boxes[0] = (self.boxes[0].astype(F32) + self.boxes[1].astype(F32)).astype(BF16)
            keep = pltpu.make_async_copy(self.boxes.at[0], self.part(i, part), self.local_sems.at[0])
            keep.start()
            keep.wait()
            self.near_copy(i).start()

    def arrived(self):
        for i in self.direct:
            self.near_copy(i).wait_recv()

    def finish(self, relays=True):
        if self.by_relay and relays:
            for part in range(2):
                self.relay_copy(part).wait_send()
        for i in self.direct:
            self.near_copy(i).wait_send()


def middle_kernel(
    sizes,
    two, cot_all, wgu_all, wd_all,
    gn2, branch, sum_gu, sum_d, sib_gu, sib_d, relay_gu, relay_d,
    hidden, x, cots, wgu_v, wd_v, ggu, acts, came, going, stage_gu, stage_d, in_gu, in_d,
    line_send, line_recv, fold_send, fold_recv, sib_send, sib_recv, cot_sems, relay_sems, local_sems,
):
    n_fsdp, n_tp = sizes
    half = n_fsdp // 2
    bits = half.bit_length() - 1
    at = Places(n_fsdp, n_tp)
    slab, model = two.shape
    part_rows = model // n_fsdp
    at.greet()
    line = Line(at, two, x, line_send, line_recv)
    line.start()
    loads = [
        pltpu.make_async_copy(two, x.at[at.t], local_sems.at[0]),
        pltpu.make_async_copy(wgu_all, wgu_v, local_sems.at[1]),
        pltpu.make_async_copy(wd_all, wd_v, local_sems.at[2]),
    ]
    for load in loads:
        load.start()

    def cot_copy(j):
        return pltpu.make_async_copy(cot_all.at[j], cots.at[j], cot_sems.at[0, j])

    def cot_last(slot, way):
        return send(
            cot_all.at[slot], cots.at[slot], cot_sems.at[1, slot], cot_sems.at[2, slot], at.along(at.t + 1 - 2 * way)
        )

    for j in range(n_tp):
        pl.when((at.t - j < n_tp - 1) & (j - at.t < n_tp - 1))(cot_copy(j).start)
    for load in loads:
        load.wait()
    for j in range(n_tp):
        pl.when((at.t - j < n_tp - 1) & (j - at.t < n_tp - 1))(cot_copy(j).wait)
    fold = Fold(at, gn2, going, came, min(512, model), fold_send, fold_recv)

    def unit(slot):
        here = pl.ds(pl.multiple_of(slot * slab, slab), slab)
        acts[0] = dot(x[slot], wgu_v[0], NN)
        acts[1] = dot(x[slot], wgu_v[1], NN)
        acts[2] = dot(cots[slot], wd_v[...], NT)
        step = 16

        def some(i, carry):
            local_rows = pl.ds(pl.multiple_of(i * step, step), step)
            rows = pl.ds(pl.multiple_of(slot * slab + i * step, step), step)
            gate, up, grad = acts[0, local_rows, :], acts[1, local_rows, :], acts[2, local_rows, :]
            low = jax.nn.sigmoid(gate)
            act = gate * low
            hidden[rows, :] = (act * up).astype(BF16)
            ggu[0, rows, :] = (grad * up * low * (1.0 + gate * (1.0 - low))).astype(BF16)
            ggu[1, rows, :] = (grad * act).astype(BF16)
            return carry

        lax.fori_loop(0, slab // step, some, 0)

        def tiles(c, carry):
            rows = fold.lanes(c)
            fold.put(
                slot,
                c,
                dot(ggu[0, here, :], wgu_v[0, rows, :], NT) + dot(ggu[1, here, :], wgu_v[1, rows, :], NT),
            )
            return carry

        lax.fori_loop(0, fold.tiles, tiles, 0)

        def branch_copy(c):
            return pltpu.make_async_copy(
                stage_gu.at[c // 2 % 2, c % 2, pl.ds(0, slab), pl.ds(0, fold.tile)],
                branch.at[slot, :, fold.lanes(c)],
                local_sems.at[4 + c % 4],
            )

        for c in range(fold.tiles):
            if c >= 4:
                branch_copy(c - 4).wait()
            stage_gu[c // 2 % 2, c % 2, 0:slab, 0 : fold.tile] = dot(
                hidden[here, :], wd_v[:, c * fold.tile : (c + 1) * fold.tile], NN
            ).astype(BF16)
            branch_copy(c).start()
        for c in range(max(0, fold.tiles - 4), fold.tiles):
            branch_copy(c).wait()

    def each_from(first, last, work):
        def some(i, carry):
            s = (i + 1) // 2
            slot = at.t + s * (2 * lax.rem(i, 2) - 1)
            pl.when((slot >= 0) & (slot < n_tp))(lambda: work(slot))
            return carry

        lax.fori_loop(max(0, 2 * first - 1), 2 * last - 1, some, 0)

    for s in range(n_tp):
        if s:
            line.step(s)
        if s == 1:
            pl.when(at.t == n_tp - 2)(lambda: cot_last(0, 0).start())
            pl.when(at.t == 1)(lambda: cot_last(n_tp - 1, 1).start())
        if s == n_tp - 1:
            pl.when(at.t == n_tp - 1)(lambda: cot_last(0, 0).wait_recv())
            pl.when(at.t == 0)(lambda: cot_last(n_tp - 1, 1).wait_recv())
        each_from(s, s + 1, unit)

    for key in range(1, n_tp - 2):
        for c in range(fold.tiles):
            fold.forward(key, c)

    def block(f, take):
        columns = pl.ds(pl.multiple_of(f * part_rows, part_rows), part_rows)
        for part in range(2):
            rows = x[:, :, columns].reshape(n_tp * slab, part_rows)
            take(part, dot(rows, ggu[part], TN))
        grads = cots[:, :, columns].reshape(n_tp * slab, part_rows)
        take(2, dot(hidden[...], grads, TN))

    spreads = [
        Spread(at, sum_gu, None, relay_gu, None, relay_sems.at[0], None),
        Spread(at, sum_d, None, relay_d, None, relay_sems.at[1], None),
    ]
    by_relay = spreads[0].by_relay

    def order(n):
        return lax.rem(n + half - 1, half) if by_relay else n

    def sib_copies(n):
        i, slot = order(n), lax.rem(n, 2)
        return [
            send(stage_gu.at[slot], sib_gu.at[i], sib_send.at[0, i], sib_recv.at[0, i], at.sibling()),
            send(stage_d.at[slot], sib_d.at[i], sib_send.at[1, i], sib_recv.at[1, i], at.sibling()),
        ]

    def keep_copies(n):
        i, slot = order(n), lax.rem(n, 2)
        return [
            pltpu.make_async_copy(stage_gu.at[slot], sum_gu.at[i], local_sems.at[4 + slot]),
            pltpu.make_async_copy(stage_d.at[slot], sum_d.at[i], local_sems.at[6 + slot]),
        ]

    def others(n, carry):
        pl.when(n < fold.tiles)(lambda: fold.forward(n_tp - 2, n))

        @pl.when(n >= 2)
        def _():
            for copy in sib_copies(n - 2):
                copy.wait_send()

        def take(part, values):
            if part < 2:
                stage_gu[lax.rem(n, 2), part] = values.astype(BF16)
            else:
                stage_d[lax.rem(n, 2)] = values.astype(BF16)

        block(xor_any(at.chip, order(n), bits) * 2 + 1 - at.core, take)
        for copy in sib_copies(n):
            copy.start()
        return carry

    lax.fori_loop(0, half, others, 0)
    for n in range(half - 2, half):
        for copy in sib_copies(jnp.int32(n)):
            copy.wait_send()

    def mine(n, carry):
        for copy in sib_copies(n):
            copy.wait_recv()
        takes = [
            pltpu.make_async_copy(sib_gu.at[order(n)], in_gu, local_sems.at[8]),
            pltpu.make_async_copy(sib_d.at[order(n)], in_d, local_sems.at[9]),
        ]
        for take in takes:
            take.start()

        @pl.when(n >= 2)
        def _():
            for copy in keep_copies(n - 2):
                copy.wait()

        if by_relay:

            @pl.when(n == 2)
            def _():
                for spread in spreads:
                    spread.start()

        def take(part, values):
            if part == 0:
                for copy in takes:
                    copy.wait()
            if part < 2:
                stage_gu[lax.rem(n, 2), part] = (values + in_gu[part].astype(F32)).astype(BF16)
            else:
                stage_d[lax.rem(n, 2)] = (values + in_d[...].astype(F32)).astype(BF16)

        block(xor_any(at.chip, order(n), bits) * 2 + at.core, take)
        for copy in keep_copies(n):
            copy.start()
        return carry

    lax.fori_loop(0, half, mine, 0)
    for c in range(fold.tiles):
        fold.forward(n_tp - 1, c)
    fold.end()
    for i in range(half - 2, half):
        for copy in keep_copies(jnp.int32(i)):
            copy.wait()
    line.finish()
    pl.when(at.t == n_tp - 2)(lambda: cot_last(0, 0).wait_send())
    pl.when(at.t == 1)(lambda: cot_last(n_tp - 1, 1).wait_send())
    fold.finish()
    if by_relay:
        for spread in spreads:
            spread.relayed()


def middle(sizes, two, cot_all, wgu_all, wd_all):
    n_fsdp, n_tp = sizes
    half = n_fsdp // 2
    slab, model = two.shape
    hidden = wd_all.shape[0]
    part_rows = model // n_fsdp
    tile = min(512, model)
    hbm = pl.BlockSpec(memory_space=pl.ANY)
    vmem = pl.BlockSpec(memory_space=pltpu.VMEM)
    shape = jax.ShapeDtypeStruct
    outs = [
        (shape((slab, model), F32), vmem),
        (shape((n_tp, slab, model), BF16), hbm),
        (shape((half, 2, part_rows, hidden), BF16), hbm),
        (shape((half, hidden, part_rows), BF16), hbm),
        (shape((half, 2, part_rows, hidden), BF16), hbm),
        (shape((half, hidden, part_rows), BF16), hbm),
        (shape((2, 1, part_rows, hidden), BF16), hbm),
        (shape((2, hidden // 2, part_rows), BF16), hbm),
    ]
    dma = pltpu.SemaphoreType.DMA
    return pl.pallas_call(
        functools.partial(middle_kernel, sizes),
        in_specs=[hbm] * 4,
        out_specs=[spec for _, spec in outs],
        out_shape=[out for out, _ in outs],
        scratch_shapes=[
            pltpu.VMEM((n_tp * slab, hidden), BF16),
            pltpu.VMEM((n_tp, slab, model), BF16),
            pltpu.VMEM((n_tp, slab, model), BF16),
            pltpu.VMEM((2, model, hidden), BF16),
            pltpu.VMEM((hidden, model), BF16),
            pltpu.VMEM((2, n_tp * slab, hidden), BF16),
            pltpu.VMEM((3, slab, hidden), F32),
            pltpu.VMEM((n_tp + 1, slab, model), BF16),
            pltpu.VMEM((n_tp, slab, model), BF16),
            pltpu.VMEM((2, 2, part_rows, hidden), BF16),
            pltpu.VMEM((2, hidden, part_rows), BF16),
            pltpu.VMEM((2, part_rows, hidden), BF16),
            pltpu.VMEM((hidden, part_rows), BF16),
            dma((2, n_tp)), dma((n_tp,)), dma((n_tp, model // tile)), dma((n_tp + 1, model // tile)),
            dma((2, half)), dma((2, half)), dma((3, n_tp)), dma((2, 2, half + 1)), dma((10,)),
        ],
        compiler_params=pltpu.CompilerParams(
            collective_id=3, has_side_effects=True, vmem_limit_bytes=62 * 2**20
        ),
        cost_estimate=pl.CostEstimate(flops=10**11, bytes_accessed=10**8, transcendentals=0),
    )(two, cot_all, wgu_all, wd_all)


class Pair:
    def __init__(self, at, stage, sib, sums, inbox, sems, local_sems):
        self.at, self.stage, self.sib, self.sums, self.inbox = at, stage, sib, sums, inbox
        self.sems, self.local_sems = sems, local_sems

    def sib_copy(self, i):
        return send(
            self.stage.at[lax.rem(i, 2)], self.sib.at[i], self.sems.at[0, i], self.sems.at[1, i], self.at.sibling()
        )

    def keep_copy(self, i):
        return pltpu.make_async_copy(
            self.stage.at[lax.rem(i, 2)], self.sums.at[i], self.local_sems.at[lax.rem(i, 2)]
        )

    def give(self, i, values):
        pl.when(i >= 2)(lambda: self.sib_copy(i - 2).wait_send())
        self.stage[lax.rem(i, 2)] = values().astype(BF16)
        self.sib_copy(i).start()

    def given(self, half):
        for i in range(half - 2, half):
            self.sib_copy(jnp.int32(i)).wait_send()

    def keep(self, i, values):
        self.sib_copy(i).wait_recv()
        take = pltpu.make_async_copy(self.sib.at[i], self.inbox, self.local_sems.at[2])
        take.start()
        pl.when(i >= 2)(lambda: self.keep_copy(i - 2).wait())
        own = values()
        take.wait()
        self.stage[lax.rem(i, 2)] = (own + self.inbox[...].astype(F32)).astype(BF16)
        self.keep_copy(i).start()

    def kept(self, half):
        for i in range(half - 2, half):
            self.keep_copy(jnp.int32(i)).wait()


def norm_back(values, incoming, gain_row):
    average = jnp.mean(values, axis=-1, keepdims=True)
    centred = values - average
    scale = lax.rsqrt(jnp.mean(centred * centred, axis=-1, keepdims=True) + NORM_EPS)
    unit = centred * scale
    grads = incoming * gain_row
    inner = jnp.mean(grads * unit, axis=-1, keepdims=True)
    back = scale * (grads - jnp.mean(grads, axis=-1, keepdims=True) - unit * inner)
    return back, jnp.sum(incoming * unit, axis=0, keepdims=True), jnp.sum(incoming, axis=0, keepdims=True)


def attend_back(widest, q_in, k_in, v_in, g_in, cos, s_low, s_high, starts, g_out, bias, kt, dk, dv, first_lane):
    seq_len, width = q_in.shape
    rows = min(256, seq_len)
    lanes = pl.ds(pl.multiple_of(first_lane, LANES), LANES)
    kt[...] = k_in[:, lanes].astype(F32).T.astype(BF16)
    dk[...] = jnp.zeros_like(dk)
    dv[...] = jnp.zeros_like(dv)

    def put(part, here, values):
        columns = pl.ds(pl.multiple_of(part * width + first_lane, LANES), LANES)
        low = values.astype(BF16)
        g_out[here, columns] = low
        return jnp.sum(low.astype(F32), axis=0, keepdims=True)

    total_q = jnp.zeros((1, LANES), F32)
    for block in range(seq_len // rows):
        here = slice(block * rows, (block + 1) * rows)
        first, last = key_range(block, rows, widest)
        query_rows = (q_in[here, lanes].astype(F32) * HEAD**-0.5).astype(BF16)
        grad_rows = g_in[here, lanes]
        query_cols = query_rows.astype(F32).T.astype(BF16)
        grad_cols = grad_rows.astype(F32).T.astype(BF16)
        head_down = lax.broadcasted_iota(jnp.int32, query_cols.shape, 0) // HEAD
        head_along = lax.broadcasted_iota(jnp.int32, query_rows.shape, 1) // HEAD
        none_down, none_along = jnp.zeros_like(query_cols), jnp.zeros_like(query_rows)
        parts = []
        for head in range(LANES // HEAD):
            weights, total = seen_weights(
                k_in[first:last, lanes],
                jnp.where(head_down == head, query_cols, none_down),
                starts[:, here],
                first,
                block * rows,
            )
            probs = weights * (1.0 / total)
            grad_probs = dot(
                v_in[first:last, lanes], jnp.where(head_down == head, grad_cols, none_down), NN
            )
            inner = jnp.sum(probs * grad_probs, axis=0, keepdims=True)
            grad_scores = (probs * (grad_probs - inner)).astype(BF16)
            dk[first:last, :] += dot(
                grad_scores, jnp.where(head_along == head, query_rows, none_along), NN
            )
            dv[first:last, :] += dot(
                probs.astype(BF16), jnp.where(head_along == head, grad_rows, none_along), NN
            )
            parts.append(dot(kt[head * HEAD : (head + 1) * HEAD, first:last], grad_scores, NN))
        grad_queries = jnp.concatenate(parts, axis=0).T * HEAD**-0.5
        total_q = total_q + put(
            0, here, turn(grad_queries, cos[here, :], -s_low[here, :], -s_high[here, :])
        )
    everywhere = slice(0, seq_len)
    bias[4:5, lanes] = total_q
    bias[5:6, lanes] = put(1, everywhere, turn(dk[...], cos[...], -s_low[...], -s_high[...]))
    bias[6:7, lanes] = put(2, everywhere, dv[...])


def back_kernel(
    sizes, widest,
    gn2, resid, tok, cot, att_own, wo_all, wq_all, q_in, k_in, v_in, one, sum_gu_in, sum_d_in,
    relay_gu, relay_d, rows_in, cos, s_low, s_high, starts,
    grad_tok, small_out, near_gu, near_d, own_gu, own_d, sum_q, near_q, sib_q, relay_q,
    sum_o, near_o, sib_o, relay_o, zo,
    gres, res_v, tok_v, cot_v, att_v, gattn, wo_v, wq_v, q_v, k_v, v_v, gp, gatt, ghead, came, going,
    kt, dk, dv, stage_o, inbox_o, stage_q, inbox_q, box_gu, box_d, box_o, box_q, zo_stage, zo_box,
    norm_sums, bias, tiles, land_z, land_near, land_sib,
    swap_send, swap_recv, fold_send, fold_recv, pair_o_sems, pair_q_sems, gu_sems, d_sems, o_sems, q_sems,
    zo_sems, small_sems, local_sems, pair_o_local, pair_q_local,
):
    n_fsdp, n_tp = sizes
    half = n_fsdp // 2
    bits = half.bit_length() - 1
    at = Places(n_fsdp, n_tp)
    slab, model = tok.shape
    seq_len, width = q_in.shape
    part_rows = model // n_fsdp
    pairs = width // LANES
    loads = [
        pltpu.make_async_copy(src, dst, local_sems.at[i])
        for i, (src, dst) in enumerate(
            [
                (gn2, gres), (resid, res_v), (cot, cot_v), (wo_all, wo_v), (tok, tok_v), (att_own, att_v),
                (q_in, q_v), (k_in, k_v), (v_in, v_v), (wq_all, wq_v),
            ]
        )
    ]
    for load in loads:
        load.start()
    at.greet()
    spread_gu = Spread(at, own_gu, near_gu, relay_gu, box_gu, gu_sems, local_sems.at[pl.ds(13, 2)])
    spread_d = Spread(at, own_d, near_d, relay_d, box_d, d_sems, local_sems.at[pl.ds(13, 2)])
    spread_o = Spread(at, sum_o, near_o, relay_o, box_o, o_sems, local_sems.at[pl.ds(13, 2)])
    spread_q = Spread(at, sum_q, near_q, relay_q, box_q, q_sems, local_sems.at[pl.ds(13, 2)])
    if not spread_gu.by_relay:
        spread_gu.start()
        spread_d.start()
    norm_sums[...] = jnp.zeros_like(norm_sums)
    bias[...] = jnp.zeros_like(bias)
    for load in loads[:4]:
        load.wait()

    step = 16

    def second(i, carry):
        here = pl.ds(pl.multiple_of(i * step, step), step)
        back, gain, shift = norm_back(res_v[here, :], gres[here, :], rows_in[1:2, :])
        total = cot_v[here, :].astype(F32) + back
        gres[here, :] = total
        gattn[here, :] = total.astype(BF16)
        norm_sums[1:2, :] = norm_sums[1:2, :] + gain
        norm_sums[3:4, :] = norm_sums[3:4, :] + shift
        return carry

    lax.fori_loop(0, slab // step, second, 0)

    def swap_copy(i, k):
        lanes = pl.ds(pl.multiple_of(i * LANES, LANES), LANES)
        other = lax.rem(at.t + k, n_tp)
        return send(
            ghead.at[other, :, lanes],
            gatt.at[pl.ds(pl.multiple_of(at.t * slab, slab), slab), lanes],
            swap_send.at[i, k], swap_recv.at[i, k], at.along(other),
        )

    def give_heads(i, carry):
        lanes = pl.ds(pl.multiple_of(i * LANES, LANES), LANES)

        def to(k, carry):
            other = lax.rem(at.t + k, n_tp)
            rows = pl.ds(pl.multiple_of(other * width + i * LANES, LANES), LANES)
            ghead[other, :, lanes] = dot(gattn[...], wo_v[rows, :], NT).astype(BF16)
            pl.when(k > 0)(lambda: swap_copy(i, k).start())
            return carry

        lax.fori_loop(0, n_tp, to, 0)
        gatt[pl.ds(pl.multiple_of(at.t * slab, slab), slab), lanes] = ghead[at.t, :, lanes]
        return carry

    lax.fori_loop(0, pairs, give_heads, 0)

    spread_gu.add(here=True)
    spread_d.add(here=True)

    loads[5].wait()
    pair_o = Pair(at, stage_o, sib_o, sum_o, inbox_o, pair_o_sems, pair_o_local)
    pair_q = Pair(at, stage_q, sib_q, sum_q, inbox_q, pair_q_sems, pair_q_local)

    def piece(f):
        return pl.ds(pl.multiple_of(f * part_rows, part_rows), part_rows)

    def owner(i, core):
        return xor_any(at.chip, i, bits) * 2 + core

    def give_o(i, carry):
        pair_o.give(i, lambda: dot(att_v[...], gattn[:, piece(owner(i, 1 - at.core))], TN))
        return carry

    lax.fori_loop(0, half, give_o, 0)
    for load in loads[6:9]:
        load.wait()
    load_one = pltpu.make_async_copy(one, wo_v.at[pl.ds(0, seq_len), :], local_sems.at[12])
    load_one.start()

    def some_heads(i, carry):
        for k in range(1, n_tp):
            source = lax.rem(at.t + n_tp - k, n_tp)
            lanes = pl.ds(pl.multiple_of(i * LANES, LANES), LANES)
            came_rows = gatt.at[pl.ds(pl.multiple_of(source * slab, slab), slab), lanes]
            send(came_rows, came_rows, swap_send.at[i, k], swap_recv.at[i, k], at.along(source)).wait_recv()
        attend_back(
            widest, q_v, k_v, v_v, gatt, cos, s_low, s_high, starts, gp, bias, kt, dk, dv, i * LANES
        )

        def keep_o(n, carry):
            pair_o.keep(n, lambda: dot(att_v[...], gattn[:, piece(owner(n, at.core))], TN))
            return carry

        lax.fori_loop(i * half // pairs, (i + 1) * half // pairs, keep_o, 0)
        return carry

    pair_o.given(half)
    lax.fori_loop(0, pairs, some_heads, 0)
    pair_o.kept(half)
    spread_o.start()

    loads[9].wait()
    fold = Fold(at, grad_tok, going, came, min(512, model), fold_send, fold_recv)

    def term(slot):
        rows = gp[pl.ds(pl.multiple_of(slot * slab, slab), slab), :]

        def some(c, carry):
            fold.put(slot, c, dot(rows, wq_v[fold.lanes(c), :], NT))
            return carry

        lax.fori_loop(0, fold.tiles, some, 0)

    def far_first(i, carry):
        s = (2 * n_tp - 1 - i) // 2
        slot = at.t + s * (2 * lax.rem(i, 2) - 1)
        pl.when((slot >= 0) & (slot < n_tp))(lambda: term(slot))
        return carry

    lax.fori_loop(0, 2 * n_tp - 1, far_first, 0)

    load_one.wait()

    def give_q(i, carry):
        pair_q.give(i, lambda: dot(wo_v[0:seq_len, piece(owner(i, 1 - at.core))], gp[...], TN))
        return carry

    def keep_q(i, carry):
        pair_q.keep(i, lambda: dot(wo_v[0:seq_len, piece(owner(i, at.core))], gp[...], TN))
        return carry

    for c in range(fold.tiles):
        fold.forward(n_tp - 1, c)
        lax.fori_loop(half * c // fold.tiles, half * (c + 1) // fold.tiles, give_q, 0)
        if c == 1:
            spread_o.add()
    pair_q.given(half)
    for c in range(fold.tiles):
        fold.forward(n_tp - 2, c)
        lax.fori_loop(half * c // fold.tiles, half * (c + 1) // fold.tiles, keep_q, 0)
    pair_q.kept(half)
    spread_q.start()
    for key in range(n_tp - 3, 0, -1):
        for c in range(fold.tiles):
            fold.forward(key, c)

    each = model // n_tp
    spread_o.arrived()

    def zo_copy(k):
        other = lax.rem(at.t + k, n_tp)
        return send(zo_stage.at[other], zo.at[at.t], zo_sems.at[0, k], zo_sems.at[1, k], at.along(other))

    def group(k, carry):
        other = lax.rem(at.t + k, n_tp)
        rows = pl.ds(pl.multiple_of(other * each, each), each)
        takes = [
            pltpu.make_async_copy(
                (sum_o if i == 0 else near_o).at[i, rows, :], zo_box.at[n], local_sems.at[16 + n]
            )
            for n, i in enumerate([0] + spread_o.direct)
        ]
        for take in takes:
            take.start()
        total = jnp.zeros(zo_box.shape[1:], F32)
        for n, take in enumerate(takes):
            take.wait()
            total = total + zo_box[n].astype(F32)
        zo_stage[other] = total.astype(BF16)
        return carry

    lax.fori_loop(0, n_tp, group, 0)
    own_zo = pltpu.make_async_copy(zo_stage.at[at.t], zo.at[at.t], local_sems.at[15])
    own_zo.start()

    for k in range(1, n_tp):
        zo_copy(k).start()
    spread_q.add()

    fold.end()
    loads[4].wait()

    def first(i, carry):
        here = pl.ds(pl.multiple_of(i * step, step), step)
        back, gain, shift = norm_back(tok_v[here, :].astype(F32), grad_tok[here, :], rows_in[0:1, :])
        grad_tok[here, :] = gres[here, :] + back
        norm_sums[0:1, :] = norm_sums[0:1, :] + gain
        norm_sums[2:3, :] = norm_sums[2:3, :] + shift
        return carry

    lax.fori_loop(0, slab // step, first, 0)

    lanes_each = model // (n_fsdp * n_tp)
    kept = lax.broadcasted_iota(jnp.int32, (8, LANES), 1) < lanes_each

    def tile_of(ref, index):
        start = index * lanes_each
        tile = ref[:, start // LANES * LANES : start // LANES * LANES + LANES]
        return jnp.where(kept, pltpu.roll(tile, (LANES - start % LANES) % LANES, 1), 0.0)

    for f in range(n_fsdp):
        for t in range(n_tp):
            tiles[t, f] = tile_of(norm_sums, f * n_tp + t)
    for f in range(n_fsdp):
        tiles[at.t, f] = tiles[at.t, f] + tile_of(bias, f)

    def z_copy(k):
        other = lax.rem(at.t + k, n_tp)
        return send(
            tiles.at[other], land_z.at[k], small_sems.at[0, half + k], small_sems.at[1, half + k], at.along(other)
        )

    for k in range(1, n_tp):
        z_copy(k).start()
    total = tiles[at.t]
    for k in range(1, n_tp):
        z_copy(k).wait_recv()
        total = total + land_z[k]
    land_z[0] = total

    def chip_copy(k):
        return send(
            land_z.at[0, pl.ds(xor(at.chip, k) * 2, 2)], land_near.at[k],
            small_sems.at[0, k], small_sems.at[1, k], at.near(k),
        )

    for k in range(1, half):
        chip_copy(k).start()
    total = land_z[0, pl.ds(at.chip * 2, 2)]
    for k in range(1, half):
        chip_copy(k).wait_recv()
        total = total + land_near[k]
    land_near[0] = total
    to_sib = send(
        land_near.at[0, 1 - at.core], land_sib, small_sems.at[0, 0], small_sems.at[1, 0], at.sibling()
    )
    to_sib.start()
    to_sib.wait_recv()
    small_out[...] = land_near[0, at.core] + land_sib[...]

    to_sib.wait_send()
    for k in range(1, half):
        chip_copy(k).wait_send()
    for k in range(1, n_tp):
        z_copy(k).wait_send()
        zo_copy(k).wait_send()
        source = lax.rem(at.t + n_tp - k, n_tp)
        send(zo.at[source], zo.at[source], zo_sems.at[0, k], zo_sems.at[1, k], at.along(source)).wait_recv()
    own_zo.wait()

    def swapped(i, carry):
        for k in range(1, n_tp):
            swap_copy(i, k).wait_send()
        return carry

    lax.fori_loop(0, pairs, swapped, 0)
    fold.finish()
    for spread in (spread_gu, spread_d, spread_q):
        spread.arrived()
    for spread in (spread_gu, spread_d):
        spread.finish(relays=False)
    for spread in (spread_q, spread_o):
        spread.finish()


def back(sizes, widest, gn2, resid, tok, cot, att_own, wo_all, wq_all, q_in, k_in, v_in, one, sum_gu, sum_d, relay_gu, relay_d, rows_in, tables, starts):
    n_fsdp, n_tp = sizes
    half = n_fsdp // 2
    slab, model = tok.shape
    seq_len, width = q_in.shape
    hidden = sum_d.shape[1]
    part_rows = model // n_fsdp
    pairs = width // LANES
    each = model // n_tp
    tile = min(512, model)
    hbm = pl.BlockSpec(memory_space=pl.ANY)
    vmem = pl.BlockSpec(memory_space=pltpu.VMEM)
    shape = jax.ShapeDtypeStruct
    piece_q, piece_o = (part_rows, 3 * width), (model, part_rows)
    piece_gu, piece_d = sum_gu.shape[1:], sum_d.shape[1:]
    halved = lambda piece: (piece[0] // 2,) + tuple(piece[1:])
    outs = [
        (shape((slab, model), F32), vmem),
        (shape((8, LANES), F32), vmem),
        (shape(sum_gu.shape, BF16), hbm),
        (shape(sum_d.shape, BF16), hbm),
        (shape(sum_gu.shape, BF16), hbm),
        (shape(sum_d.shape, BF16), hbm),
        (shape((half,) + piece_q, BF16), hbm),
        (shape((half,) + piece_q, BF16), hbm),
        (shape((half,) + piece_q, BF16), hbm),
        (shape((2,) + halved(piece_q), BF16), hbm),
        (shape((half,) + piece_o, BF16), hbm),
        (shape((half,) + piece_o, BF16), hbm),
        (shape((half,) + piece_o, BF16), hbm),
        (shape((2,) + halved(piece_o), BF16), hbm),
        (shape((n_tp, each, part_rows), BF16), hbm),
    ]
    dma = pltpu.SemaphoreType.DMA
    return pl.pallas_call(
        functools.partial(back_kernel, sizes, widest),
        in_specs=[hbm] * 15 + [vmem] * 5,
        out_specs=[spec for _, spec in outs],
        out_shape=[out for out, _ in outs],
        scratch_shapes=[
            pltpu.VMEM((slab, model), F32),
            pltpu.VMEM((slab, model), F32),
            pltpu.VMEM((slab, model), BF16),
            pltpu.VMEM((slab, model), BF16),
            pltpu.VMEM((slab, model), BF16),
            pltpu.VMEM((slab, model), BF16),
            pltpu.VMEM((model, model), BF16),
            pltpu.VMEM((model, 3 * width), BF16),
            pltpu.VMEM((seq_len, width), BF16),
            pltpu.VMEM((seq_len, width), BF16),
            pltpu.VMEM((seq_len, width), BF16),
            pltpu.VMEM((seq_len, 3 * width), BF16),
            pltpu.VMEM((seq_len, width), BF16),
            pltpu.VMEM((n_tp, slab, width), BF16),
            pltpu.VMEM((n_tp + 1, slab, model), BF16),
            pltpu.VMEM((n_tp, slab, model), BF16),
            pltpu.VMEM((LANES, seq_len), BF16),
            pltpu.VMEM((seq_len, LANES), F32),
            pltpu.VMEM((seq_len, LANES), F32),
            pltpu.VMEM((2,) + piece_o, BF16),
            pltpu.VMEM(piece_o, BF16),
            pltpu.VMEM((2,) + piece_q, BF16),
            pltpu.VMEM(piece_q, BF16),
            pltpu.VMEM((2,) + halved(piece_gu), BF16),
            pltpu.VMEM((2,) + halved(piece_d), BF16),
            pltpu.VMEM((2,) + halved(piece_o), BF16),
            pltpu.VMEM((2,) + halved(piece_q), BF16),
            pltpu.VMEM((n_tp, each, part_rows), BF16),
            pltpu.VMEM((half, each, part_rows), BF16),
            pltpu.VMEM((8, model), F32),
            pltpu.VMEM((8, width), F32),
            pltpu.VMEM((n_tp, n_fsdp, 8, LANES), F32),
            pltpu.VMEM((n_tp, n_fsdp, 8, LANES), F32),
            pltpu.VMEM((half, 2, 8, LANES), F32),
            pltpu.VMEM((8, LANES), F32),
            dma((pairs, n_tp)), dma((pairs, n_tp)),
            dma((n_tp, model // tile)), dma((n_tp + 1, model // tile)),
            dma((2, half)), dma((2, half)),
            dma((2, half + 1)), dma((2, half + 1)), dma((2, half + 1)), dma((2, half + 1)),
            dma((2, n_tp)), dma((2, half + n_tp)), dma((16 + half,)), dma((3,)), dma((3,)),
        ],
        input_output_aliases={11: 4, 12: 5},
        compiler_params=pltpu.CompilerParams(
            collective_id=2, has_side_effects=True, vmem_limit_bytes=62 * 2**20
        ),
        cost_estimate=pl.CostEstimate(flops=10**11, bytes_accessed=10**8, transcendentals=0),
    )(
        gn2, resid, tok, cot, att_own, wo_all, wq_all, q_in, k_in, v_in, one, sum_gu, sum_d,
        relay_gu, relay_d, rows_in, *tables, starts,
    )


def reduce_rows(values):
    return lax.psum_scatter(values.astype(BF16), "tp", scatter_dimension=0, tiled=True).astype(F32)


def local(tokens, lengths, ln_gains, ln_shifts, w_qkv, b_qkv, w_out, w_gate_up, w_down, cotangent):
    n_fsdp, n_tp = lax.axis_size("fsdp"), lax.axis_size("tp")
    sizes = (n_fsdp, n_tp)
    at_tp = lax.axis_index("tp")
    slab_rows, model_width = tokens.shape
    seq_len = slab_rows * n_tp
    small = ln_gains.shape[1]
    local_width = w_qkv.shape[2]
    hidden_width = w_gate_up.shape[2]
    part_rows = w_qkv.shape[0]

    length_row = lengths[0]
    doc_ends = jnp.cumsum(length_row)
    ids = jnp.arange(seq_len, dtype=jnp.int32)
    passed = (doc_ends[None, :] <= ids[:, None]).astype(jnp.int32)
    starts = jnp.sum(passed * length_row[None, :], axis=1)
    places = (ids - starts).astype(F32)
    frequency = 10000.0 ** (-2.0 * jnp.arange(ROT // 2, dtype=F32) / ROT)
    angles = frequency[:, None] * places[None, :]
    turns = jnp.concatenate([jnp.cos(angles), jnp.sin(angles)], axis=0)
    starts_row = starts.reshape(1, seq_len).astype(jnp.int32)
    widest = seq_len // 2

    tile = jnp.concatenate([ln_gains, ln_shifts, b_qkv.astype(F32), jnp.zeros((1, small), F32)], 0)
    tile = jnp.pad(tile, ((0, 0), (0, LANES - small)))
    (
        full_one, queries, key_vals, value_rows, residual, normed_two, norm_rows_all, attended_own,
        grad_branch, qkv_all, out_all, gu_all, down_all, *tables,
    ) = front(
        sizes, widest, tokens, cotangent, w_qkv.reshape(part_rows, 3 * local_width), w_out,
        w_gate_up.transpose(1, 0, 2), w_down, tile, turns, starts_row,
    )
    full_one = full_one.reshape(seq_len, model_width)

    grad_normed_two, branch_terms, sum_gu, sum_down, _, _, relay_gu, relay_down = middle(
        sizes, normed_two, grad_branch, gu_all, down_all
    )
    (
        grad_tokens, shares, near_gu, near_down, own_gu, own_down, sum_qkv, near_qkv, _, _, _, _, _, _,
        out_parts,
    ) = back(
        sizes, widest, grad_normed_two, residual, tokens, cotangent, attended_own, out_all, qkv_all,
        queries, key_vals, value_rows, full_one, sum_gu, sum_down, relay_gu, relay_down,
        norm_rows_all, tables, starts_row,
    )
    branch = reduce_rows(branch_terms.reshape(seq_len, model_width))
    result = (residual + branch).astype(BF16)
    direct = [1, 2] if n_fsdp == 8 else list(range(1, n_fsdp // 2))

    def total(sums, near):
        return sum([near[i].astype(F32) for i in direct], sums[0].astype(F32))

    shares = shares[:, :small]
    return (
        result,
        grad_tokens,
        shares[0:2],
        shares[2:4],
        total(sum_qkv, near_qkv).reshape(part_rows, 3, local_width),
        shares[4:7],
        jnp.sum(out_parts.astype(F32), axis=0),
        jnp.stack([total(own_gu[:, part], near_gu[:, part]) for part in range(2)], axis=1),
        total(own_down, near_down),
    )


def solution(mesh):
    placed = (
        P(("fsdp", "tp"), None),
        P("fsdp", None),
        P(None, ("fsdp", "tp")),
        P(None, ("fsdp", "tp")),
        P("fsdp", None, "tp"),
        P(None, ("tp", "fsdp")),
        P("tp", "fsdp"),
        P("fsdp", None, "tp"),
        P("tp", "fsdp"),
        P(("fsdp", "tp"), None),
    )
    return jax.shard_map(
        local,
        mesh=mesh,
        in_specs=placed,
        out_specs=(
            P(("fsdp", "tp"), None),
            P(("fsdp", "tp"), None),
            P(None, ("fsdp", "tp")),
            P(None, ("fsdp", "tp")),
            P("fsdp", None, "tp"),
            P(None, ("tp", "fsdp")),
            P("tp", "fsdp"),
            P("fsdp", None, "tp"),
            P("tp", "fsdp"),
        ),
        check_vma=False,
    )
```

```python
import functools

import jax
import jax.numpy as jnp
from jax import lax
from jax.experimental import pallas as pl
from jax.experimental.pallas import tpu as pltpu
from jax.sharding import PartitionSpec as P

HEAD = 64
ROT = 16
NORM_EPS = 1e-05
LANES = 128
MESH = pl.DeviceIdType.MESH
NN = (((1,), (0,)), ((), ()))
NT = (((1,), (1,)), ((), ()))
TN = (((0,), (0,)), ((), ()))
F32 = jnp.float32
BF16 = jnp.bfloat16


def dot(left, right, dims):
    return lax.dot_general(left, right, dims, preferred_element_type=F32)


def turn(values, cosine, sine_low, sine_high):
    return (
        values * cosine
        + pltpu.roll(values, LANES - ROT // 2, 1) * sine_low
        + pltpu.roll(values, ROT // 2, 1) * sine_high
    )


def key_range(block, rows, widest):
    first = max(0, block * rows - widest)
    return first, (block + 1) * rows


def seen_weights(key_rows, query_cols, starts_row, first_key, first_query):
    scores = dot(key_rows, query_cols, NN)
    key_ids = first_key + lax.broadcasted_iota(jnp.int32, scores.shape, 0)
    query_ids = first_query + lax.broadcasted_iota(jnp.int32, scores.shape, 1)
    seen = (key_ids <= query_ids) & (key_ids >= starts_row)
    scores = jnp.where(seen, scores, -1e30)
    top = jnp.max(scores, axis=0, keepdims=True)
    weights = jnp.exp(scores - top)
    return weights, jnp.sum(weights, axis=0, keepdims=True)


def xor(value, mask):
    bit = 1
    while bit <= mask:
        if mask & bit:
            value = value + bit * (1 - 2 * lax.rem(value // bit, 2))
        bit *= 2
    return value


class Places:
    def __init__(self, n_fsdp, n_tp):
        self.n_fsdp, self.n_tp = n_fsdp, n_tp
        self.f, self.t = lax.axis_index("fsdp"), lax.axis_index("tp")
        self.chip, self.core = self.f // 2, lax.rem(self.f, 2)

    def near_f(self, k):
        return xor(self.chip, k) * 2 + self.core

    def near(self, k):
        return (self.near_f(k), self.t)

    def sibling(self):
        return (self.chip * 2 + 1 - self.core, self.t)

    def along(self, t):
        return (self.f, t)

    def greet(self):
        barrier = pltpu.get_barrier_semaphore()
        partners = [self.near(k) for k in range(1, self.n_fsdp // 2)] + [self.sibling()]
        partners += [self.along(lax.rem(self.t + k, self.n_tp)) for k in range(1, self.n_tp)]
        for partner in partners:
            pl.semaphore_signal(barrier, inc=1, device_id=partner, device_id_type=MESH)
        pl.semaphore_wait(barrier, len(partners))


def send(src, dst, send_sem, recv_sem, device):
    return pltpu.make_async_remote_copy(
        src_ref=src,
        dst_ref=dst,
        send_sem=send_sem,
        recv_sem=recv_sem,
        device_id=device,
        device_id_type=MESH,
    )


class Line:
    def __init__(self, at, own, slots, send_sems, recv_sems):
        self.at, self.own, self.slots = at, own, slots
        self.send_sems, self.recv_sems = send_sems, recv_sems

    def copy(self, slot, way, first):
        at = self.at
        return send(
            self.own if first else self.slots.at[slot],
            self.slots.at[slot],
            self.send_sems.at[way, slot],
            self.recv_sems.at[slot],
            at.along(at.t + 1 - 2 * way),
        )

    def start(self):
        at = self.at
        pl.when(at.t < at.n_tp - 1)(lambda: self.copy(at.t, 0, True).start())
        pl.when(at.t > 0)(lambda: self.copy(at.t, 1, True).start())

    def start_inner(self):
        at = self.at
        pl.when(at.t < at.n_tp - 2)(lambda: self.copy(at.t, 0, True).start())
        pl.when(at.t > 1)(lambda: self.copy(at.t, 1, True).start())

    def start_outer(self):
        at = self.at
        pl.when(at.t == at.n_tp - 2)(lambda: self.copy(at.t, 0, True).start())
        pl.when(at.t == 1)(lambda: self.copy(at.t, 1, True).start())

    def step(self, s, on=True):
        at = self.at

        @pl.when(at.t >= s)
        def _():
            self.copy(at.t - s, 0, False).wait_recv()
            if on:
                pl.when(at.t < at.n_tp - 1)(lambda: self.copy(at.t - s, 0, False).start())

        @pl.when(at.t + s < at.n_tp)
        def _():
            self.copy(at.t + s, 1, False).wait_recv()
            if on:
                pl.when(at.t > 0)(lambda: self.copy(at.t + s, 1, False).start())

    def finish(self, last=None):
        at = self.at
        for s in range(at.n_tp if last is None else last):
            pl.when((at.t >= s) & (at.t < at.n_tp - 1))(
                lambda s=s: self.copy(at.t - s, 0, s == 0).wait_send()
            )
            pl.when((at.t + s < at.n_tp) & (at.t > 0))(
                lambda s=s: self.copy(at.t + s, 1, s == 0).wait_send()
            )


class Shards:
    def __init__(self, at, own, whole, by_rows, near_sems, sib_sems, index):
        self.at, self.own, self.whole, self.by_rows = at, own, whole, by_rows
        self.near_sems, self.sib_sems, self.index = near_sems, sib_sems, index
        self.half = at.n_fsdp // 2
        self.relay = at.n_fsdp == 8
        self.direct = [1, 2] if self.relay else list(range(1, self.half))

    def slot(self, f, part=None):
        if self.by_rows:
            rows = self.whole.shape[-2] // self.at.n_fsdp
            first = f * rows
            if part is not None:
                rows = rows // 2
                first = first + part * rows
            here = pl.ds(pl.multiple_of(first, rows), rows)
            return self.whole.at[:, here, :] if len(self.whole.shape) == 3 else self.whole.at[here, :]
        width = self.whole.shape[1] // self.at.n_fsdp
        columns = pl.ds(pl.multiple_of(f * width, LANES), width)
        if part is None:
            return self.whole.at[:, columns]
        rows = self.whole.shape[0] // 2
        return self.whole.at[pl.ds(part * rows, rows), columns]

    def near_copy(self, k):
        return send(
            self.own,
            self.slot(self.at.f),
            self.near_sems.at[self.index, 0, k],
            self.near_sems.at[self.index, 1, k],
            self.at.near(k),
        )

    def start(self):
        for k in self.direct:
            self.near_copy(k).start()
        self.sib_copy(0).start()

    def arrived(self, k):
        slot = self.slot(self.at.near_f(k))
        send(
            slot,
            slot,
            self.near_sems.at[self.index, 0, k],
            self.near_sems.at[self.index, 1, k],
            self.at.near(k),
        ).wait_recv()

    def relay_copy(self, part):
        source, target = (1, 2) if part == 0 else (2, 1)
        slot = self.slot(self.at.near_f(source), part)
        return send(
            slot,
            slot,
            self.near_sems.at[self.index, 0, 3 + part],
            self.near_sems.at[self.index, 1, 3 + part],
            self.at.near(target),
        )

    def sib_copy(self, k):
        f = self.at.near_f(k)
        return send(
            self.own if k == 0 else self.slot(f),
            self.slot(f),
            self.sib_sems.at[self.index, 0, k],
            self.sib_sems.at[self.index, 1, k],
            self.at.sibling(),
        )

    def pass_on(self):
        for k in self.direct:
            self.arrived(k)
            if self.relay:
                self.relay_copy(k - 1).start()
        for k in self.direct:
            self.sib_copy(k).start()

    def pass_last(self):
        if self.relay:
            for part in range(2):
                slot = self.slot(self.at.near_f(3), part)
                send(
                    slot,
                    slot,
                    self.near_sems.at[self.index, 0, 3 + part],
                    self.near_sems.at[self.index, 1, 3 + part],
                    self.at.near(2 - part),
                ).wait_recv()
            self.sib_copy(3).start()

    def complete(self):
        for k in range(self.half):
            f = xor(self.at.chip, k) * 2 + 1 - self.at.core
            slot = self.slot(f)
            send(
                slot,
                slot,
                self.sib_sems.at[self.index, 0, k],
                self.sib_sems.at[self.index, 1, k],
                self.at.sibling(),
            ).wait_recv()

    def finish(self):
        for k in self.direct:
            self.near_copy(k).wait_send()
        if self.relay:
            for part in range(2):
                self.relay_copy(part).wait_send()
        for k in range(self.half):
            self.sib_copy(k).wait_send()


def norm_rows(values, gain_row, shift_row):
    average = jnp.mean(values, axis=-1, keepdims=True)
    centred = values - average
    variance = jnp.mean(centred * centred, axis=-1, keepdims=True)
    return centred * lax.rsqrt(variance + NORM_EPS) * gain_row + shift_row


def front_kernel(
    sizes, widest,
    tok, cot, wq, wo, wgu, wd, tile, turns, starts,
    one, q_out, k_out, v_out, resid, two, rows_out, att_out, cot_all, wq_all, wo_all, wgu_all, wd_all,
    cos, s_low, s_high,
    toks, wq_v, wo_v, att, heads, vt, small, bias,
    tok_send, tok_recv, cot_send, cot_recv, near_sems, sib_sems, wz_sems, small_sems,
    swap_send, swap_recv, local_sems,
):
    n_fsdp, n_tp = sizes
    half = n_fsdp // 2
    at = Places(n_fsdp, n_tp)
    slab, model = tok.shape
    width = q_out.shape[1]
    each = wo.shape[0]
    at.greet()

    line = Line(at, tok, toks, tok_send, tok_recv)
    line.start()
    grads = Line(at, cot, cot_all, cot_send, cot_recv)
    weights = [
        Shards(at, wq, wq_all, True, near_sems, sib_sems, 0),
        None,
        Shards(at, wgu, wgu_all, True, near_sems, sib_sems, 2),
        Shards(at, wd, wd_all, False, near_sems, sib_sems, 3),
    ]
    weights[1] = Shards(at, None, wo_all, False, near_sems, sib_sems, 1)
    weights[1].own = weights[1].slot(at.f)
    weights[0].start()

    own_columns = pl.ds(pl.multiple_of(at.f * (model // n_fsdp), LANES), model // n_fsdp)

    def wo_rows(t):
        return wo_all.at[pl.ds(pl.multiple_of(t * each, each), each), own_columns]

    def wo_copy(k):
        return send(wo, wo_rows(at.t), wz_sems.at[0, k], wz_sems.at[1, k], at.along(lax.rem(at.t + k, n_tp)))

    for k in range(1, n_tp):
        wo_copy(k).start()
    own_copies = [
        pltpu.make_async_copy(tok, toks.at[at.t], local_sems.at[0]),
        pltpu.make_async_copy(wq, weights[0].slot(at.f), local_sems.at[1]),
        pltpu.make_async_copy(wo, wo_rows(at.t), local_sems.at[2]),
        pltpu.make_async_copy(wgu, weights[2].slot(at.f), local_sems.at[3]),
        pltpu.make_async_copy(wd, weights[3].slot(at.f), local_sems.at[4]),
        pltpu.make_async_copy(cot, cot_all.at[at.t], local_sems.at[5]),
    ]
    for copy in own_copies:
        copy.start()

    eight = ROT // 2
    cosine, sine = turns[0:eight, :], turns[eight : 2 * eight, :]
    none = jnp.zeros_like(sine)
    flat = jnp.zeros((HEAD - ROT, turns.shape[1]), F32)
    cos[...] = jnp.concatenate([cosine, cosine, flat + 1.0] * 2, axis=0).T
    s_low[...] = jnp.concatenate([-sine, none, flat] * 2, axis=0).T
    s_high[...] = jnp.concatenate([none, sine, flat] * 2, axis=0).T

    small[at.t, at.f] = tile[...]
    mine = small.at[at.t, at.f]
    to_sib = send(mine, mine, small_sems.at[0, 0], small_sems.at[1, 0], at.sibling())
    to_sib.start()
    to_sib.wait()
    pair = small.at[at.t, pl.ds(at.chip * 2, 2)]
    to_near = [
        send(pair, pair, small_sems.at[0, k], small_sems.at[1, k], at.near(k)) for k in range(1, half)
    ]
    for copy in to_near:
        copy.start()
    for k in range(1, half):
        to_near[k - 1].wait_send()
        came = small.at[at.t, pl.ds(xor(at.chip, k) * 2, 2)]
        send(came, came, small_sems.at[0, k], small_sems.at[1, k], at.near(k)).wait_recv()
    plane = small.at[at.t]
    to_line = [
        send(
            plane, plane, small_sems.at[0, half + k], small_sems.at[1, half + k],
            at.along(lax.rem(at.t + k, n_tp)),
        )
        for k in range(1, n_tp)
    ]
    for copy in to_line:
        copy.start()
    for k in range(1, n_tp):
        to_line[k - 1].wait_send()
        came = small.at[lax.rem(at.t + n_tp - k, n_tp)]
        send(
            came, came, small_sems.at[0, half + k], small_sems.at[1, half + k],
            at.along(lax.rem(at.t + k, n_tp)),
        ).wait_recv()
    lanes_each = model // (n_fsdp * n_tp)
    group = LANES // lanes_each
    for i in range(model // LANES):
        total = jnp.zeros((8, LANES), F32)
        for j in range(group):
            linear = i * group + j
            total = total + pltpu.roll(small[linear % n_tp, linear // n_tp], j * lanes_each, 1)
        rows_out[:, i * LANES : (i + 1) * LANES] = total
    for i in range(width // LANES):
        total = jnp.zeros((8, LANES), F32)
        for j in range(group):
            total = total + pltpu.roll(small[at.t, i * group + j], j * lanes_each, 1)
        bias[:, i * LANES : (i + 1) * LANES] = total
    own_copies[0].wait()

    def normalise(slot):
        step = 32

        def some(i, carry):
            here = pl.ds(pl.multiple_of(i * step, step), step)
            one[slot, here, :] = norm_rows(
                toks[slot, here, :].astype(F32), rows_out[0:1, :], rows_out[2:3, :]
            ).astype(BF16)
            return carry

        lax.fori_loop(0, slab // step, some, 0)

    wide = 256

    def project(slot):
        here = pl.ds(pl.multiple_of(slot * slab, slab), slab)
        for part, out in enumerate((q_out, k_out, v_out)):

            def some(i, carry, part=part, out=out):
                values = dot(
                    one[slot], wq_v[:, pl.ds(pl.multiple_of(part * width + i * wide, wide), wide)], NN
                )
                for j in range(wide // LANES):
                    lanes = pl.ds(pl.multiple_of(i * wide + j * LANES, LANES), LANES)
                    piece = values[:, j * LANES : (j + 1) * LANES] + bias[4 + part : 5 + part, lanes]
                    if part < 2:
                        piece = turn(piece, cos[here, :], s_low[here, :], s_high[here, :])
                    out[here, lanes] = piece.astype(BF16)
                return carry

            lax.fori_loop(0, width // wide, some, 0)

    def each_from(first, last, work):
        def some(i, carry):
            s = (i + 1) // 2
            slot = at.t + s * (2 * lax.rem(i, 2) - 1)
            pl.when((slot >= 0) & (slot < n_tp))(lambda: work(slot))
            return carry

        lax.fori_loop(max(0, 2 * first - 1), 2 * last - 1, some, 0)

    normalise(at.t)
    for s in range(1, n_tp - 1):
        line.step(s)
        if s == 1:
            weights[0].pass_on()
            own_copies[2].wait()
            for k in range(1, n_tp):
                wo_copy(k).wait_send()
                came = wo_rows(lax.rem(at.t + n_tp - k, n_tp))
                send(came, came, wz_sems.at[0, k], wz_sems.at[1, k], at.along(at.t)).wait_recv()
            weights[1].start()
        if s == 2:
            weights[0].pass_last()
            weights[2].start()
            grads.start_inner()
        each_from(s, s + 1, normalise)
    own_copies[1].wait()
    weights[0].complete()
    load = pltpu.make_async_copy(wq_all, wq_v, local_sems.at[6])
    load.start()
    load.wait()
    each_from(0, n_tp - 1, project)
    weights[1].pass_on()
    weights[3].start()
    line.step(n_tp - 1)
    grads.start_outer()
    each_from(n_tp - 1, n_tp, normalise)
    each_from(n_tp - 1, n_tp, project)

    def swap_copy(i, k):
        lanes = pl.ds(pl.multiple_of(i * LANES, LANES), LANES)
        columns = pl.ds(pl.multiple_of(at.t * width + i * LANES, LANES), LANES)
        other = lax.rem(at.t + k, n_tp)
        return send(
            heads.at[other, :, lanes], att.at[:, columns],
            swap_send.at[i, k], swap_recv.at[i, k], at.along(other),
        )

    def some_heads(i, carry):
        lanes = pl.ds(pl.multiple_of(i * LANES, LANES), LANES)
        attend(widest, q_out, k_out, v_out, starts, heads, vt, lanes, slab)
        for k in range(1, n_tp):
            swap_copy(i, k).start()
        columns = pl.ds(pl.multiple_of(at.t * width + i * LANES, LANES), LANES)
        att[:, columns] = heads[at.t, :, lanes]
        pl.when(i == width // LANES // 2 - 1)(weights[1].pass_last)
        return carry

    lax.fori_loop(0, width // LANES, some_heads, 0)
    weights[2].pass_on()
    weights[1].complete()
    load = pltpu.make_async_copy(wo_all, wo_v, local_sems.at[7])
    load.start()

    def took_heads(i, carry):
        for k in range(1, n_tp):
            swap_copy(i, k).wait_send()
            source = lax.rem(at.t + n_tp - k, n_tp)
            came = att.at[:, pl.ds(pl.multiple_of(source * width + i * LANES, LANES), LANES)]
            send(came, came, swap_send.at[i, k], swap_recv.at[i, k], at.along(source)).wait_recv()
        return carry

    lax.fori_loop(0, width // LANES, took_heads, 0)
    grads.step(1)
    keep = pltpu.make_async_copy(att, att_out, local_sems.at[8])
    keep.start()
    load.wait()

    def out_columns(i, carry):
        here = pl.ds(pl.multiple_of(i * wide, wide), wide)
        resid[:, here] = toks[at.t, :, here].astype(F32) + dot(att[...], wo_v[:, here], NN)
        return carry

    lax.fori_loop(0, model // wide, out_columns, 0)
    weights[3].pass_on()

    def second_norm(i, carry):
        here = pl.ds(pl.multiple_of(i * 32, 32), 32)
        two[here, :] = norm_rows(resid[here, :], rows_out[1:2, :], rows_out[3:4, :]).astype(BF16)
        return carry

    lax.fori_loop(0, slab // 32, second_norm, 0)

    weights[2].pass_last()
    weights[3].pass_last()
    for s in range(2, n_tp - 1):
        grads.step(s, on=s < n_tp - 2)
    for copy in own_copies[3:]:
        copy.wait()
    weights[2].complete()
    weights[3].complete()
    keep.wait()
    line.finish()
    grads.finish(n_tp - 2)
    for weight in weights:
        weight.finish()


def attend(widest, q_in, k_in, v_in, starts, heads, vt, lanes, slab):
    seq_len = q_in.shape[0]
    rows = min(256, seq_len)
    vt[...] = v_in[:, lanes].astype(F32).T.astype(BF16)
    for block in range(seq_len // rows):
        here = slice(block * rows, (block + 1) * rows)
        first, last = key_range(block, rows, widest)
        query_cols = (q_in[here, lanes].astype(F32) * HEAD**-0.5).T.astype(BF16)
        head_of = lax.broadcasted_iota(jnp.int32, query_cols.shape, 0) // HEAD
        parts = []
        for head in range(LANES // HEAD):
            own_cols = jnp.where(head_of == head, query_cols, jnp.zeros_like(query_cols))
            weights, total = seen_weights(
                k_in[first:last, lanes], own_cols, starts[:, here], first, block * rows
            )
            part = dot(vt[head * HEAD : (head + 1) * HEAD, first:last], weights.astype(BF16), NN)
            parts.append(part / total)
        found = jnp.concatenate(parts, axis=0).T.astype(BF16)
        for j in range(max(1, rows // slab)):
            count = min(slab, rows)
            row = block * rows + j * count
            heads[row // slab, row % slab : row % slab + count, lanes] = found[
                j * count : (j + 1) * count, :
            ]


def front(sizes, widest, tok, cot, wq, wo, wgu, wd, tile, turns, starts):
    n_fsdp, n_tp = sizes
    half = n_fsdp // 2
    slab, model = tok.shape
    seq_len = slab * n_tp
    width = wq.shape[1] // 3
    hidden = wd.shape[0]
    hbm = pl.BlockSpec(memory_space=pl.ANY)
    vmem = pl.BlockSpec(memory_space=pltpu.VMEM)
    shape = jax.ShapeDtypeStruct
    outs = [
        (shape((n_tp, slab, model), BF16), vmem),
        (shape((seq_len, width), BF16), vmem),
        (shape((seq_len, width), BF16), vmem),
        (shape((seq_len, width), BF16), vmem),
        (shape((slab, model), F32), vmem),
        (shape((slab, model), BF16), vmem),
        (shape((8, model), F32), vmem),
        (shape((slab, model), BF16), hbm),
        (shape((n_tp, slab, model), BF16), hbm),
        (shape((model, 3 * width), BF16), hbm),
        (shape((model, model), BF16), hbm),
        (shape((2, model, hidden), BF16), hbm),
        (shape((hidden, model), BF16), hbm),
    ] + [(shape((seq_len, LANES), F32), vmem)] * 3
    dma = pltpu.SemaphoreType.DMA
    pairs = width // LANES
    return pl.pallas_call(
        functools.partial(front_kernel, sizes, widest),
        in_specs=[vmem] * 9,
        out_specs=[spec for _, spec in outs],
        out_shape=[out for out, _ in outs],
        scratch_shapes=[
            pltpu.VMEM((n_tp, slab, model), BF16),
            pltpu.VMEM((model, 3 * width), BF16),
            pltpu.VMEM((model, model), BF16),
            pltpu.VMEM((slab, model), BF16),
            pltpu.VMEM((n_tp, slab, width), BF16),
            pltpu.VMEM((LANES, seq_len), BF16),
            pltpu.VMEM((n_tp, n_fsdp, 8, LANES), F32),
            pltpu.VMEM((8, width), F32),
            dma((2, n_tp)), dma((n_tp,)), dma((2, n_tp)), dma((n_tp,)),
            dma((4, 2, half + 1)), dma((4, 2, half)), dma((2, n_tp)), dma((2, half + n_tp)),
            dma((pairs, n_tp)), dma((pairs, n_tp)), dma((9,)),
        ],
        compiler_params=pltpu.CompilerParams(
            collective_id=1, has_side_effects=True, vmem_limit_bytes=60 * 2**20
        ),
        cost_estimate=pl.CostEstimate(flops=10**11, bytes_accessed=10**8, transcendentals=0),
    )(tok, cot, wq, wo, wgu, wd, tile, turns, starts)


def xor_any(value, mask, bits):
    total = 0
    for b in range(bits):
        both = lax.rem(value // 2**b, 2) + lax.rem(mask // 2**b, 2)
        total = total + lax.rem(both, 2) * 2**b
    return total


class Fold:
    def __init__(self, at, total, going, came, tile, send_sems, recv_sems):
        self.at, self.total, self.going, self.came, self.tile = at, total, going, came, tile
        self.send_sems, self.recv_sems = send_sems, recv_sems
        self.tiles = total.shape[1] // tile

    def lanes(self, c):
        return pl.ds(pl.multiple_of(c * self.tile, self.tile), self.tile)

    def copy(self, j, c, way):
        at = self.at
        slot = j if way == 0 else j + (at.n_tp - j) * lax.max(0, j - at.t + 2)
        return send(
            self.going.at[j, :, self.lanes(c)],
            self.came.at[slot, :, self.lanes(c)],
            self.send_sems.at[j, c],
            self.recv_sems.at[slot, c],
            at.along(at.t + 1 - 2 * way),
        )

    def put(self, j, c, values):
        at = self.at

        @pl.when(j == at.t)
        def _():
            self.total[:, self.lanes(c)] = values

        @pl.when(j != at.t)
        def _():
            self.going[j, :, self.lanes(c)] = values.astype(BF16)

        pl.when((j > at.t) & (at.t == 0))(lambda: self.copy(j, c, 0).start())
        pl.when((j < at.t) & (at.t == at.n_tp - 1))(lambda: self.copy(j, c, 1).start())

    def arrived(self, slot, c):
        tile = self.came.at[slot, :, self.lanes(c)]
        send(
            tile, tile, self.send_sems.at[0, c], self.recv_sems.at[slot, c], self.at.along(self.at.t)
        ).wait_recv()

    def forward(self, key, c):
        at = self.at

        def some(j, way):
            self.arrived(j, c)
            here = self.lanes(c)
            self.going[j, :, here] = (
                self.going[j, :, here].astype(F32) + self.came[j, :, here].astype(F32)
            ).astype(BF16)
            self.copy(j, c, way).start()

        pl.when((key > at.t) & (at.t > 0))(lambda: some(key, 0))
        down = at.n_tp - 1 - key
        pl.when((down < at.t) & (at.t < at.n_tp - 1))(lambda: some(down, 1))

    def end(self):
        at = self.at

        def some(c, carry):
            here = self.lanes(c)

            @pl.when(at.t > 0)
            def _():
                self.arrived(at.t, c)
                self.total[:, here] = self.total[:, here] + self.came[at.t, :, here].astype(F32)

            @pl.when(at.t < at.n_tp - 1)
            def _():
                self.arrived(at.n_tp, c)
                self.total[:, here] = self.total[:, here] + self.came[at.n_tp, :, here].astype(F32)

            return carry

        lax.fori_loop(0, self.tiles, some, 0)

    def finish(self):
        at = self.at

        def some(i, carry):
            j, c = i // self.tiles, lax.rem(i, self.tiles)
            pl.when(j > at.t)(lambda: self.copy(j, c, 0).wait_send())
            pl.when(j < at.t)(lambda: self.copy(j, c, 1).wait_send())
            return carry

        lax.fori_loop(0, at.n_tp * self.tiles, some, 0)


class Spread:
    def __init__(self, at, sums, near, relay, boxes, sems, local_sems):
        self.at, self.sums, self.near, self.relay, self.boxes = at, sums, near, relay, boxes
        self.sems, self.local_sems = sems, local_sems
        self.half = at.n_fsdp // 2
        self.by_relay = at.n_fsdp == 8
        self.direct = [1, 2] if self.by_relay else list(range(1, self.half))
        self.rows = sums.shape[1] // 2

    def part(self, i, part):
        return self.sums.at[i, pl.ds(part * self.rows, self.rows)]

    def relay_copy(self, part):
        return send(
            self.part(3, part), self.relay.at[part],
            self.sems.at[0, 3 + part], self.sems.at[1, 3 + part], self.at.near(1 + part),
        )

    def near_copy(self, i):
        return send(
            self.sums.at[i], self.near.at[i], self.sems.at[0, i], self.sems.at[1, i], self.at.near(i)
        )

    def start(self):
        if self.by_relay:
            for part in range(2):
                self.relay_copy(part).start()
        else:
            for i in self.direct:
                self.near_copy(i).start()

    def relayed(self):
        for part in range(2):
            self.relay_copy(part).wait_send()
            self.relay_copy(part).wait_recv()

    def add(self, here=False):
        if not self.by_relay:
            return
        for part, i in ((0, 2), (1, 1)):
            if not here:
                self.relay_copy(part).wait_recv()
            takes = [
                pltpu.make_async_copy(self.part(i, part), self.boxes.at[0], self.local_sems.at[0]),
                pltpu.make_async_copy(self.relay.at[part], self.boxes.at[1], self.local_sems.at[1]),
            ]
            for take in takes:
                take.start()
            for take in takes:
                take.wait()
            self.boxes[0] = (self.boxes[0].astype(F32) + self.boxes[1].astype(F32)).astype(BF16)
            keep = pltpu.make_async_copy(self.boxes.at[0], self.part(i, part), self.local_sems.at[0])
            keep.start()
            keep.wait()
            self.near_copy(i).start()

    def arrived(self):
        for i in self.direct:
            self.near_copy(i).wait_recv()

    def finish(self, relays=True):
        if self.by_relay and relays:
            for part in range(2):
                self.relay_copy(part).wait_send()
        for i in self.direct:
            self.near_copy(i).wait_send()


def middle_kernel(
    sizes,
    two, cot_all, wgu_all, wd_all,
    gn2, branch, sum_gu, sum_d, sib_gu, sib_d, relay_gu, relay_d,
    hidden, x, cots, wgu_v, wd_v, ggu, acts, came, going, stage_gu, stage_d, in_gu, in_d,
    line_send, line_recv, fold_send, fold_recv, sib_send, sib_recv, cot_sems, relay_sems, local_sems,
):
    n_fsdp, n_tp = sizes
    half = n_fsdp // 2
    bits = half.bit_length() - 1
    at = Places(n_fsdp, n_tp)
    slab, model = two.shape
    part_rows = model // n_fsdp
    at.greet()
    line = Line(at, two, x, line_send, line_recv)
    line.start()
    loads = [
        pltpu.make_async_copy(two, x.at[at.t], local_sems.at[0]),
        pltpu.make_async_copy(wgu_all, wgu_v, local_sems.at[1]),
        pltpu.make_async_copy(wd_all, wd_v, local_sems.at[2]),
    ]
    for load in loads:
        load.start()

    def cot_copy(j):
        return pltpu.make_async_copy(cot_all.at[j], cots.at[j], cot_sems.at[0, j])

    def cot_last(slot, way):
        return send(
            cot_all.at[slot], cots.at[slot], cot_sems.at[1, slot], cot_sems.at[2, slot], at.along(at.t + 1 - 2 * way)
        )

    for j in range(n_tp):
        pl.when((at.t - j < n_tp - 1) & (j - at.t < n_tp - 1))(cot_copy(j).start)
    for load in loads:
        load.wait()
    for j in range(n_tp):
        pl.when((at.t - j < n_tp - 1) & (j - at.t < n_tp - 1))(cot_copy(j).wait)
    fold = Fold(at, gn2, going, came, min(512, model), fold_send, fold_recv)

    def unit(slot):
        here = pl.ds(pl.multiple_of(slot * slab, slab), slab)
        acts[0] = dot(x[slot], wgu_v[0], NN)
        acts[1] = dot(x[slot], wgu_v[1], NN)
        acts[2] = dot(cots[slot], wd_v[...], NT)
        step = 16

        def some(i, carry):
            local_rows = pl.ds(pl.multiple_of(i * step, step), step)
            rows = pl.ds(pl.multiple_of(slot * slab + i * step, step), step)
            gate, up, grad = acts[0, local_rows, :], acts[1, local_rows, :], acts[2, local_rows, :]
            low = jax.nn.sigmoid(gate)
            act = gate * low
            hidden[rows, :] = (act * up).astype(BF16)
            ggu[0, rows, :] = (grad * up * low * (1.0 + gate * (1.0 - low))).astype(BF16)
            ggu[1, rows, :] = (grad * act).astype(BF16)
            return carry

        lax.fori_loop(0, slab // step, some, 0)

        def tiles(c, carry):
            rows = fold.lanes(c)
            fold.put(
                slot,
                c,
                dot(ggu[0, here, :], wgu_v[0, rows, :], NT) + dot(ggu[1, here, :], wgu_v[1, rows, :], NT),
            )
            return carry

        lax.fori_loop(0, fold.tiles, tiles, 0)

        def branch_copy(c):
            return pltpu.make_async_copy(
                stage_gu.at[c // 2 % 2, c % 2, pl.ds(0, slab), pl.ds(0, fold.tile)],
                branch.at[slot, :, fold.lanes(c)],
                local_sems.at[4 + c % 4],
            )

        for c in range(fold.tiles):
            if c >= 4:
                branch_copy(c - 4).wait()
            stage_gu[c // 2 % 2, c % 2, 0:slab, 0 : fold.tile] = dot(
                hidden[here, :], wd_v[:, c * fold.tile : (c + 1) * fold.tile], NN
            ).astype(BF16)
            branch_copy(c).start()
        for c in range(max(0, fold.tiles - 4), fold.tiles):
            branch_copy(c).wait()

    def each_from(first, last, work):
        def some(i, carry):
            s = (i + 1) // 2
            slot = at.t + s * (2 * lax.rem(i, 2) - 1)
            pl.when((slot >= 0) & (slot < n_tp))(lambda: work(slot))
            return carry

        lax.fori_loop(max(0, 2 * first - 1), 2 * last - 1, some, 0)

    for s in range(n_tp):
        if s:
            line.step(s)
        if s == 1:
            pl.when(at.t == n_tp - 2)(lambda: cot_last(0, 0).start())
            pl.when(at.t == 1)(lambda: cot_last(n_tp - 1, 1).start())
        if s == n_tp - 1:
            pl.when(at.t == n_tp - 1)(lambda: cot_last(0, 0).wait_recv())
            pl.when(at.t == 0)(lambda: cot_last(n_tp - 1, 1).wait_recv())
        each_from(s, s + 1, unit)

    for key in range(1, n_tp - 2):
        for c in range(fold.tiles):
            fold.forward(key, c)

    def block(f, take):
        columns = pl.ds(pl.multiple_of(f * part_rows, part_rows), part_rows)
        for part in range(2):
            rows = x[:, :, columns].reshape(n_tp * slab, part_rows)
            take(part, dot(rows, ggu[part], TN))
        grads = cots[:, :, columns].reshape(n_tp * slab, part_rows)
        take(2, dot(hidden[...], grads, TN))

    spreads = [
        Spread(at, sum_gu, None, relay_gu, None, relay_sems.at[0], None),
        Spread(at, sum_d, None, relay_d, None, relay_sems.at[1], None),
    ]
    by_relay = spreads[0].by_relay

    def order(n):
        return lax.rem(n + half - 1, half) if by_relay else n

    def sib_copies(n):
        i, slot = order(n), lax.rem(n, 2)
        return [
            send(stage_gu.at[slot], sib_gu.at[i], sib_send.at[0, i], sib_recv.at[0, i], at.sibling()),
            send(stage_d.at[slot], sib_d.at[i], sib_send.at[1, i], sib_recv.at[1, i], at.sibling()),
        ]

    def keep_copies(n):
        i, slot = order(n), lax.rem(n, 2)
        return [
            pltpu.make_async_copy(stage_gu.at[slot], sum_gu.at[i], local_sems.at[4 + slot]),
            pltpu.make_async_copy(stage_d.at[slot], sum_d.at[i], local_sems.at[6 + slot]),
        ]

    def others(n, carry):
        pl.when(n < fold.tiles)(lambda: fold.forward(n_tp - 2, n))

        @pl.when(n >= 2)
        def _():
            for copy in sib_copies(n - 2):
                copy.wait_send()

        def take(part, values):
            if part < 2:
                stage_gu[lax.rem(n, 2), part] = values.astype(BF16)
            else:
                stage_d[lax.rem(n, 2)] = values.astype(BF16)

        block(xor_any(at.chip, order(n), bits) * 2 + 1 - at.core, take)
        for copy in sib_copies(n):
            copy.start()
        return carry

    lax.fori_loop(0, half, others, 0)
    for n in range(half - 2, half):
        for copy in sib_copies(jnp.int32(n)):
            copy.wait_send()

    def mine(n, carry):
        for copy in sib_copies(n):
            copy.wait_recv()
        takes = [
            pltpu.make_async_copy(sib_gu.at[order(n)], in_gu, local_sems.at[8]),
            pltpu.make_async_copy(sib_d.at[order(n)], in_d, local_sems.at[9]),
        ]
        for take in takes:
            take.start()

        @pl.when(n >= 2)
        def _():
            for copy in keep_copies(n - 2):
                copy.wait()

        if by_relay:

            @pl.when(n == 2)
            def _():
                for spread in spreads:
                    spread.start()

        def take(part, values):
            if part == 0:
                for copy in takes:
                    copy.wait()
            if part < 2:
                stage_gu[lax.rem(n, 2), part] = (values + in_gu[part].astype(F32)).astype(BF16)
            else:
                stage_d[lax.rem(n, 2)] = (values + in_d[...].astype(F32)).astype(BF16)

        block(xor_any(at.chip, order(n), bits) * 2 + at.core, take)
        for copy in keep_copies(n):
            copy.start()
        return carry

    lax.fori_loop(0, half, mine, 0)
    for c in range(fold.tiles):
        fold.forward(n_tp - 1, c)
    fold.end()
    for i in range(half - 2, half):
        for copy in keep_copies(jnp.int32(i)):
            copy.wait()
    line.finish()
    pl.when(at.t == n_tp - 2)(lambda: cot_last(0, 0).wait_send())
    pl.when(at.t == 1)(lambda: cot_last(n_tp - 1, 1).wait_send())
    fold.finish()
    if by_relay:
        for spread in spreads:
            spread.relayed()


def middle(sizes, two, cot_all, wgu_all, wd_all):
    n_fsdp, n_tp = sizes
    half = n_fsdp // 2
    slab, model = two.shape
    hidden = wd_all.shape[0]
    part_rows = model // n_fsdp
    tile = min(512, model)
    hbm = pl.BlockSpec(memory_space=pl.ANY)
    vmem = pl.BlockSpec(memory_space=pltpu.VMEM)
    shape = jax.ShapeDtypeStruct
    outs = [
        (shape((slab, model), F32), vmem),
        (shape((n_tp, slab, model), BF16), hbm),
        (shape((half, 2, part_rows, hidden), BF16), hbm),
        (shape((half, hidden, part_rows), BF16), hbm),
        (shape((half, 2, part_rows, hidden), BF16), hbm),
        (shape((half, hidden, part_rows), BF16), hbm),
        (shape((2, 1, part_rows, hidden), BF16), hbm),
        (shape((2, hidden // 2, part_rows), BF16), hbm),
    ]
    dma = pltpu.SemaphoreType.DMA
    return pl.pallas_call(
        functools.partial(middle_kernel, sizes),
        in_specs=[hbm] * 4,
        out_specs=[spec for _, spec in outs],
        out_shape=[out for out, _ in outs],
        scratch_shapes=[
            pltpu.VMEM((n_tp * slab, hidden), BF16),
            pltpu.VMEM((n_tp, slab, model), BF16),
            pltpu.VMEM((n_tp, slab, model), BF16),
            pltpu.VMEM((2, model, hidden), BF16),
            pltpu.VMEM((hidden, model), BF16),
            pltpu.VMEM((2, n_tp * slab, hidden), BF16),
            pltpu.VMEM((3, slab, hidden), F32),
            pltpu.VMEM((n_tp + 1, slab, model), BF16),
            pltpu.VMEM((n_tp, slab, model), BF16),
            pltpu.VMEM((2, 2, part_rows, hidden), BF16),
            pltpu.VMEM((2, hidden, part_rows), BF16),
            pltpu.VMEM((2, part_rows, hidden), BF16),
            pltpu.VMEM((hidden, part_rows), BF16),
            dma((2, n_tp)), dma((n_tp,)), dma((n_tp, model // tile)), dma((n_tp + 1, model // tile)),
            dma((2, half)), dma((2, half)), dma((3, n_tp)), dma((2, 2, half + 1)), dma((10,)),
        ],
        compiler_params=pltpu.CompilerParams(
            collective_id=3, has_side_effects=True, vmem_limit_bytes=62 * 2**20
        ),
        cost_estimate=pl.CostEstimate(flops=10**11, bytes_accessed=10**8, transcendentals=0),
    )(two, cot_all, wgu_all, wd_all)


class Pair:
    def __init__(self, at, stage, sib, sums, inbox, sems, local_sems):
        self.at, self.stage, self.sib, self.sums, self.inbox = at, stage, sib, sums, inbox
        self.sems, self.local_sems = sems, local_sems

    def sib_copy(self, i):
        return send(
            self.stage.at[lax.rem(i, 2)], self.sib.at[i], self.sems.at[0, i], self.sems.at[1, i], self.at.sibling()
        )

    def keep_copy(self, i):
        return pltpu.make_async_copy(
            self.stage.at[lax.rem(i, 2)], self.sums.at[i], self.local_sems.at[lax.rem(i, 2)]
        )

    def give(self, i, values):
        pl.when(i >= 2)(lambda: self.sib_copy(i - 2).wait_send())
        self.stage[lax.rem(i, 2)] = values().astype(BF16)
        self.sib_copy(i).start()

    def given(self, half):
        for i in range(half - 2, half):
            self.sib_copy(jnp.int32(i)).wait_send()

    def keep(self, i, values):
        self.sib_copy(i).wait_recv()
        take = pltpu.make_async_copy(self.sib.at[i], self.inbox, self.local_sems.at[2])
        take.start()
        pl.when(i >= 2)(lambda: self.keep_copy(i - 2).wait())
        own = values()
        take.wait()
        self.stage[lax.rem(i, 2)] = (own + self.inbox[...].astype(F32)).astype(BF16)
        self.keep_copy(i).start()

    def kept(self, half):
        for i in range(half - 2, half):
            self.keep_copy(jnp.int32(i)).wait()


def norm_back(values, incoming, gain_row):
    average = jnp.mean(values, axis=-1, keepdims=True)
    centred = values - average
    scale = lax.rsqrt(jnp.mean(centred * centred, axis=-1, keepdims=True) + NORM_EPS)
    unit = centred * scale
    grads = incoming * gain_row
    inner = jnp.mean(grads * unit, axis=-1, keepdims=True)
    back = scale * (grads - jnp.mean(grads, axis=-1, keepdims=True) - unit * inner)
    return back, jnp.sum(incoming * unit, axis=0, keepdims=True), jnp.sum(incoming, axis=0, keepdims=True)


def attend_back(widest, q_in, k_in, v_in, g_in, cos, s_low, s_high, starts, g_out, bias, kt, dk, dv, first_lane):
    seq_len, width = q_in.shape
    rows = min(256, seq_len)
    lanes = pl.ds(pl.multiple_of(first_lane, LANES), LANES)
    kt[...] = k_in[:, lanes].astype(F32).T.astype(BF16)
    dk[...] = jnp.zeros_like(dk)
    dv[...] = jnp.zeros_like(dv)

    def put(part, here, values):
        columns = pl.ds(pl.multiple_of(part * width + first_lane, LANES), LANES)
        low = values.astype(BF16)
        g_out[here, columns] = low
        return jnp.sum(low.astype(F32), axis=0, keepdims=True)

    total_q = jnp.zeros((1, LANES), F32)
    for block in range(seq_len // rows):
        here = slice(block * rows, (block + 1) * rows)
        first, last = key_range(block, rows, widest)
        query_rows = (q_in[here, lanes].astype(F32) * HEAD**-0.5).astype(BF16)
        grad_rows = g_in[here, lanes]
        query_cols = query_rows.astype(F32).T.astype(BF16)
        grad_cols = grad_rows.astype(F32).T.astype(BF16)
        head_down = lax.broadcasted_iota(jnp.int32, query_cols.shape, 0) // HEAD
        head_along = lax.broadcasted_iota(jnp.int32, query_rows.shape, 1) // HEAD
        none_down, none_along = jnp.zeros_like(query_cols), jnp.zeros_like(query_rows)
        parts = []
        for head in range(LANES // HEAD):
            weights, total = seen_weights(
                k_in[first:last, lanes],
                jnp.where(head_down == head, query_cols, none_down),
                starts[:, here],
                first,
                block * rows,
            )
            probs = weights * (1.0 / total)
            grad_probs = dot(
                v_in[first:last, lanes], jnp.where(head_down == head, grad_cols, none_down), NN
            )
            inner = jnp.sum(probs * grad_probs, axis=0, keepdims=True)
            grad_scores = (probs * (grad_probs - inner)).astype(BF16)
            dk[first:last, :] += dot(
                grad_scores, jnp.where(head_along == head, query_rows, none_along), NN
            )
            dv[first:last, :] += dot(
                probs.astype(BF16), jnp.where(head_along == head, grad_rows, none_along), NN
            )
            parts.append(dot(kt[head * HEAD : (head + 1) * HEAD, first:last], grad_scores, NN))
        grad_queries = jnp.concatenate(parts, axis=0).T * HEAD**-0.5
        total_q = total_q + put(
            0, here, turn(grad_queries, cos[here, :], -s_low[here, :], -s_high[here, :])
        )
    everywhere = slice(0, seq_len)
    bias[4:5, lanes] = total_q
    bias[5:6, lanes] = put(1, everywhere, turn(dk[...], cos[...], -s_low[...], -s_high[...]))
    bias[6:7, lanes] = put(2, everywhere, dv[...])


def back_kernel(
    sizes, widest,
    gn2, resid, tok, cot, att_own, wo_all, wq_all, q_in, k_in, v_in, one, sum_gu_in, sum_d_in,
    relay_gu, relay_d, rows_in, cos, s_low, s_high, starts,
    grad_tok, small_out, near_gu, near_d, own_gu, own_d, sum_q, near_q, sib_q, relay_q,
    sum_o, near_o, sib_o, relay_o, zo,
    gres, res_v, tok_v, cot_v, att_v, gattn, wo_v, wq_v, q_v, k_v, v_v, gp, gatt, ghead, came, going,
    kt, dk, dv, stage_o, inbox_o, stage_q, inbox_q, box_gu, box_d, box_o, box_q, zo_stage, zo_box,
    norm_sums, bias, tiles, land_z, land_near, land_sib,
    swap_send, swap_recv, fold_send, fold_recv, pair_o_sems, pair_q_sems, gu_sems, d_sems, o_sems, q_sems,
    zo_sems, small_sems, local_sems, pair_o_local, pair_q_local,
):
    n_fsdp, n_tp = sizes
    half = n_fsdp // 2
    bits = half.bit_length() - 1
    at = Places(n_fsdp, n_tp)
    slab, model = tok.shape
    seq_len, width = q_in.shape
    part_rows = model // n_fsdp
    pairs = width // LANES
    loads = [
        pltpu.make_async_copy(src, dst, local_sems.at[i])
        for i, (src, dst) in enumerate(
            [
                (gn2, gres), (resid, res_v), (cot, cot_v), (wo_all, wo_v), (tok, tok_v), (att_own, att_v),
                (q_in, q_v), (k_in, k_v), (v_in, v_v), (wq_all, wq_v),
            ]
        )
    ]
    for load in loads:
        load.start()
    at.greet()
    spread_gu = Spread(at, own_gu, near_gu, relay_gu, box_gu, gu_sems, local_sems.at[pl.ds(13, 2)])
    spread_d = Spread(at, own_d, near_d, relay_d, box_d, d_sems, local_sems.at[pl.ds(13, 2)])
    spread_o = Spread(at, sum_o, near_o, relay_o, box_o, o_sems, local_sems.at[pl.ds(13, 2)])
    spread_q = Spread(at, sum_q, near_q, relay_q, box_q, q_sems, local_sems.at[pl.ds(13, 2)])
    if not spread_gu.by_relay:
        spread_gu.start()
        spread_d.start()
    norm_sums[...] = jnp.zeros_like(norm_sums)
    bias[...] = jnp.zeros_like(bias)
    for load in loads[:4]:
        load.wait()

    step = 16

    def second(i, carry):
        here = pl.ds(pl.multiple_of(i * step, step), step)
        back, gain, shift = norm_back(res_v[here, :], gres[here, :], rows_in[1:2, :])
        total = cot_v[here, :].astype(F32) + back
        gres[here, :] = total
        gattn[here, :] = total.astype(BF16)
        norm_sums[1:2, :] = norm_sums[1:2, :] + gain
        norm_sums[3:4, :] = norm_sums[3:4, :] + shift
        return carry

    lax.fori_loop(0, slab // step, second, 0)

    def swap_copy(i, k):
        lanes = pl.ds(pl.multiple_of(i * LANES, LANES), LANES)
        other = lax.rem(at.t + k, n_tp)
        return send(
            ghead.at[other, :, lanes],
            gatt.at[pl.ds(pl.multiple_of(at.t * slab, slab), slab), lanes],
            swap_send.at[i, k], swap_recv.at[i, k], at.along(other),
        )

    def give_heads(i, carry):
        lanes = pl.ds(pl.multiple_of(i * LANES, LANES), LANES)

        def to(k, carry):
            other = lax.rem(at.t + k, n_tp)
            rows = pl.ds(pl.multiple_of(other * width + i * LANES, LANES), LANES)
            ghead[other, :, lanes] = dot(gattn[...], wo_v[rows, :], NT).astype(BF16)
            pl.when(k > 0)(lambda: swap_copy(i, k).start())
            return carry

        lax.fori_loop(0, n_tp, to, 0)
        gatt[pl.ds(pl.multiple_of(at.t * slab, slab), slab), lanes] = ghead[at.t, :, lanes]
        return carry

    lax.fori_loop(0, pairs, give_heads, 0)

    spread_gu.add(here=True)
    spread_d.add(here=True)

    loads[5].wait()
    pair_o = Pair(at, stage_o, sib_o, sum_o, inbox_o, pair_o_sems, pair_o_local)
    pair_q = Pair(at, stage_q, sib_q, sum_q, inbox_q, pair_q_sems, pair_q_local)

    def piece(f):
        return pl.ds(pl.multiple_of(f * part_rows, part_rows), part_rows)

    def owner(i, core):
        return xor_any(at.chip, i, bits) * 2 + core

    def give_o(i, carry):
        pair_o.give(i, lambda: dot(att_v[...], gattn[:, piece(owner(i, 1 - at.core))], TN))
        return carry

    lax.fori_loop(0, half, give_o, 0)
    for load in loads[6:9]:
        load.wait()
    load_one = pltpu.make_async_copy(one, wo_v.at[pl.ds(0, seq_len), :], local_sems.at[12])
    load_one.start()

    def some_heads(i, carry):
        for k in range(1, n_tp):
            source = lax.rem(at.t + n_tp - k, n_tp)
            lanes = pl.ds(pl.multiple_of(i * LANES, LANES), LANES)
            came_rows = gatt.at[pl.ds(pl.multiple_of(source * slab, slab), slab), lanes]
            send(came_rows, came_rows, swap_send.at[i, k], swap_recv.at[i, k], at.along(source)).wait_recv()
        attend_back(
            widest, q_v, k_v, v_v, gatt, cos, s_low, s_high, starts, gp, bias, kt, dk, dv, i * LANES
        )

        def keep_o(n, carry):
            pair_o.keep(n, lambda: dot(att_v[...], gattn[:, piece(owner(n, at.core))], TN))
            return carry

        lax.fori_loop(i * half // pairs, (i + 1) * half // pairs, keep_o, 0)
        return carry

    pair_o.given(half)
    lax.fori_loop(0, pairs, some_heads, 0)
    pair_o.kept(half)
    spread_o.start()

    loads[9].wait()
    fold = Fold(at, grad_tok, going, came, min(512, model), fold_send, fold_recv)

    def term(slot):
        rows = gp[pl.ds(pl.multiple_of(slot * slab, slab), slab), :]

        def some(c, carry):
            fold.put(slot, c, dot(rows, wq_v[fold.lanes(c), :], NT))
            return carry

        lax.fori_loop(0, fold.tiles, some, 0)

    def far_first(i, carry):
        s = (2 * n_tp - 1 - i) // 2
        slot = at.t + s * (2 * lax.rem(i, 2) - 1)
        pl.when((slot >= 0) & (slot < n_tp))(lambda: term(slot))
        return carry

    lax.fori_loop(0, 2 * n_tp - 1, far_first, 0)

    load_one.wait()

    def give_q(i, carry):
        pair_q.give(i, lambda: dot(wo_v[0:seq_len, piece(owner(i, 1 - at.core))], gp[...], TN))
        return carry

    def keep_q(i, carry):
        pair_q.keep(i, lambda: dot(wo_v[0:seq_len, piece(owner(i, at.core))], gp[...], TN))
        return carry

    for c in range(fold.tiles):
        fold.forward(n_tp - 1, c)
        lax.fori_loop(half * c // fold.tiles, half * (c + 1) // fold.tiles, give_q, 0)
        if c == 1:
            spread_o.add()
    pair_q.given(half)
    for c in range(fold.tiles):
        fold.forward(n_tp - 2, c)
        lax.fori_loop(half * c // fold.tiles, half * (c + 1) // fold.tiles, keep_q, 0)
    pair_q.kept(half)
    spread_q.start()
    for key in range(n_tp - 3, 0, -1):
        for c in range(fold.tiles):
            fold.forward(key, c)

    each = model // n_tp
    spread_o.arrived()

    def zo_copy(k):
        other = lax.rem(at.t + k, n_tp)
        return send(zo_stage.at[other], zo.at[at.t], zo_sems.at[0, k], zo_sems.at[1, k], at.along(other))

    def group(k, carry):
        other = lax.rem(at.t + k, n_tp)
        rows = pl.ds(pl.multiple_of(other * each, each), each)
        takes = [
            pltpu.make_async_copy(
                (sum_o if i == 0 else near_o).at[i, rows, :], zo_box.at[n], local_sems.at[16 + n]
            )
            for n, i in enumerate([0] + spread_o.direct)
        ]
        for take in takes:
            take.start()
        total = jnp.zeros(zo_box.shape[1:], F32)
        for n, take in enumerate(takes):
            take.wait()
            total = total + zo_box[n].astype(F32)
        zo_stage[other] = total.astype(BF16)
        return carry

    lax.fori_loop(0, n_tp, group, 0)
    own_zo = pltpu.make_async_copy(zo_stage.at[at.t], zo.at[at.t], local_sems.at[15])
    own_zo.start()

    for k in range(1, n_tp):
        zo_copy(k).start()
    spread_q.add()

    fold.end()
    loads[4].wait()

    def first(i, carry):
        here = pl.ds(pl.multiple_of(i * step, step), step)
        back, gain, shift = norm_back(tok_v[here, :].astype(F32), grad_tok[here, :], rows_in[0:1, :])
        grad_tok[here, :] = gres[here, :] + back
        norm_sums[0:1, :] = norm_sums[0:1, :] + gain
        norm_sums[2:3, :] = norm_sums[2:3, :] + shift
        return carry

    lax.fori_loop(0, slab // step, first, 0)

    lanes_each = model // (n_fsdp * n_tp)
    kept = lax.broadcasted_iota(jnp.int32, (8, LANES), 1) < lanes_each

    def tile_of(ref, index):
        start = index * lanes_each
        tile = ref[:, start // LANES * LANES : start // LANES * LANES + LANES]
        return jnp.where(kept, pltpu.roll(tile, (LANES - start % LANES) % LANES, 1), 0.0)

    for f in range(n_fsdp):
        for t in range(n_tp):
            tiles[t, f] = tile_of(norm_sums, f * n_tp + t)
    for f in range(n_fsdp):
        tiles[at.t, f] = tiles[at.t, f] + tile_of(bias, f)

    def z_copy(k):
        other = lax.rem(at.t + k, n_tp)
        return send(
            tiles.at[other], land_z.at[k], small_sems.at[0, half + k], small_sems.at[1, half + k], at.along(other)
        )

    for k in range(1, n_tp):
        z_copy(k).start()
    total = tiles[at.t]
    for k in range(1, n_tp):
        z_copy(k).wait_recv()
        total = total + land_z[k]
    land_z[0] = total

    def chip_copy(k):
        return send(
            land_z.at[0, pl.ds(xor(at.chip, k) * 2, 2)], land_near.at[k],
            small_sems.at[0, k], small_sems.at[1, k], at.near(k),
        )

    for k in range(1, half):
        chip_copy(k).start()
    total = land_z[0, pl.ds(at.chip * 2, 2)]
    for k in range(1, half):
        chip_copy(k).wait_recv()
        total = total + land_near[k]
    land_near[0] = total
    to_sib = send(
        land_near.at[0, 1 - at.core], land_sib, small_sems.at[0, 0], small_sems.at[1, 0], at.sibling()
    )
    to_sib.start()
    to_sib.wait_recv()
    small_out[...] = land_near[0, at.core] + land_sib[...]

    to_sib.wait_send()
    for k in range(1, half):
        chip_copy(k).wait_send()
    for k in range(1, n_tp):
        z_copy(k).wait_send()
        zo_copy(k).wait_send()
        source = lax.rem(at.t + n_tp - k, n_tp)
        send(zo.at[source], zo.at[source], zo_sems.at[0, k], zo_sems.at[1, k], at.along(source)).wait_recv()
    own_zo.wait()

    def swapped(i, carry):
        for k in range(1, n_tp):
            swap_copy(i, k).wait_send()
        return carry

    lax.fori_loop(0, pairs, swapped, 0)
    fold.finish()
    for spread in (spread_gu, spread_d, spread_q):
        spread.arrived()
    for spread in (spread_gu, spread_d):
        spread.finish(relays=False)
    for spread in (spread_q, spread_o):
        spread.finish()


def back(sizes, widest, gn2, resid, tok, cot, att_own, wo_all, wq_all, q_in, k_in, v_in, one, sum_gu, sum_d, relay_gu, relay_d, rows_in, tables, starts):
    n_fsdp, n_tp = sizes
    half = n_fsdp // 2
    slab, model = tok.shape
    seq_len, width = q_in.shape
    hidden = sum_d.shape[1]
    part_rows = model // n_fsdp
    pairs = width // LANES
    each = model // n_tp
    tile = min(512, model)
    hbm = pl.BlockSpec(memory_space=pl.ANY)
    vmem = pl.BlockSpec(memory_space=pltpu.VMEM)
    shape = jax.ShapeDtypeStruct
    piece_q, piece_o = (part_rows, 3 * width), (model, part_rows)
    piece_gu, piece_d = sum_gu.shape[1:], sum_d.shape[1:]
    halved = lambda piece: (piece[0] // 2,) + tuple(piece[1:])
    outs = [
        (shape((slab, model), F32), vmem),
        (shape((8, LANES), F32), vmem),
        (shape(sum_gu.shape, BF16), hbm),
        (shape(sum_d.shape, BF16), hbm),
        (shape(sum_gu.shape, BF16), hbm),
        (shape(sum_d.shape, BF16), hbm),
        (shape((half,) + piece_q, BF16), hbm),
        (shape((half,) + piece_q, BF16), hbm),
        (shape((half,) + piece_q, BF16), hbm),
        (shape((2,) + halved(piece_q), BF16), hbm),
        (shape((half,) + piece_o, BF16), hbm),
        (shape((half,) + piece_o, BF16), hbm),
        (shape((half,) + piece_o, BF16), hbm),
        (shape((2,) + halved(piece_o), BF16), hbm),
        (shape((n_tp, each, part_rows), BF16), hbm),
    ]
    dma = pltpu.SemaphoreType.DMA
    return pl.pallas_call(
        functools.partial(back_kernel, sizes, widest),
        in_specs=[hbm] * 15 + [vmem] * 5,
        out_specs=[spec for _, spec in outs],
        out_shape=[out for out, _ in outs],
        scratch_shapes=[
            pltpu.VMEM((slab, model), F32),
            pltpu.VMEM((slab, model), F32),
            pltpu.VMEM((slab, model), BF16),
            pltpu.VMEM((slab, model), BF16),
            pltpu.VMEM((slab, model), BF16),
            pltpu.VMEM((slab, model), BF16),
            pltpu.VMEM((model, model), BF16),
            pltpu.VMEM((model, 3 * width), BF16),
            pltpu.VMEM((seq_len, width), BF16),
            pltpu.VMEM((seq_len, width), BF16),
            pltpu.VMEM((seq_len, width), BF16),
            pltpu.VMEM((seq_len, 3 * width), BF16),
            pltpu.VMEM((seq_len, width), BF16),
            pltpu.VMEM((n_tp, slab, width), BF16),
            pltpu.VMEM((n_tp + 1, slab, model), BF16),
            pltpu.VMEM((n_tp, slab, model), BF16),
            pltpu.VMEM((LANES, seq_len), BF16),
            pltpu.VMEM((seq_len, LANES), F32),
            pltpu.VMEM((seq_len, LANES), F32),
            pltpu.VMEM((2,) + piece_o, BF16),
            pltpu.VMEM(piece_o, BF16),
            pltpu.VMEM((2,) + piece_q, BF16),
            pltpu.VMEM(piece_q, BF16),
            pltpu.VMEM((2,) + halved(piece_gu), BF16),
            pltpu.VMEM((2,) + halved(piece_d), BF16),
            pltpu.VMEM((2,) + halved(piece_o), BF16),
            pltpu.VMEM((2,) + halved(piece_q), BF16),
            pltpu.VMEM((n_tp, each, part_rows), BF16),
            pltpu.VMEM((half, each, part_rows), BF16),
            pltpu.VMEM((8, model), F32),
            pltpu.VMEM((8, width), F32),
            pltpu.VMEM((n_tp, n_fsdp, 8, LANES), F32),
            pltpu.VMEM((n_tp, n_fsdp, 8, LANES), F32),
            pltpu.VMEM((half, 2, 8, LANES), F32),
            pltpu.VMEM((8, LANES), F32),
            dma((pairs, n_tp)), dma((pairs, n_tp)),
            dma((n_tp, model // tile)), dma((n_tp + 1, model // tile)),
            dma((2, half)), dma((2, half)),
            dma((2, half + 1)), dma((2, half + 1)), dma((2, half + 1)), dma((2, half + 1)),
            dma((2, n_tp)), dma((2, half + n_tp)), dma((16 + half,)), dma((3,)), dma((3,)),
        ],
        input_output_aliases={11: 4, 12: 5},
        compiler_params=pltpu.CompilerParams(
            collective_id=2, has_side_effects=True, vmem_limit_bytes=62 * 2**20
        ),
        cost_estimate=pl.CostEstimate(flops=10**11, bytes_accessed=10**8, transcendentals=0),
    )(
        gn2, resid, tok, cot, att_own, wo_all, wq_all, q_in, k_in, v_in, one, sum_gu, sum_d,
        relay_gu, relay_d, rows_in, *tables, starts,
    )


def last_kernel(count, *refs):
    gu, down, qkv = refs[:count], refs[count : 2 * count], refs[2 * count : 3 * count]
    gu_out, down_out, qkv_out = refs[3 * count :]
    width = qkv_out.shape[2]
    for part in range(2):
        gu_out[:, part, :] = sum([ref[0, part].astype(F32) for ref in gu[1:]], gu[0][0, part].astype(F32))
    down_out[...] = sum([ref[0].astype(F32) for ref in down[1:]], down[0][0].astype(F32))
    for part in range(3):
        lanes = slice(part * width, (part + 1) * width)
        qkv_out[:, part, :] = sum(
            [ref[0, :, lanes].astype(F32) for ref in qkv[1:]], qkv[0][0, :, lanes].astype(F32)
        )


def last_sums(own_gu, near_gu, own_down, near_down, own_qkv, near_qkv, direct):
    rows, hidden, part_rows = own_gu.shape[2], own_gu.shape[3], own_down.shape[2]
    width = own_qkv.shape[2] // 3
    steps = 4
    gu = lambda k: pl.BlockSpec((1, 2, rows // steps, hidden), lambda i, k=k: (k, 0, i, 0))
    down = lambda k: pl.BlockSpec((1, hidden // steps, part_rows), lambda i, k=k: (k, i, 0))
    qkv = lambda k: pl.BlockSpec((1, rows // steps, 3 * width), lambda i, k=k: (k, i, 0))
    places = [0] + direct
    return pl.pallas_call(
        functools.partial(last_kernel, len(places)),
        grid=(steps,),
        in_specs=[make(k) for make in (gu, down, qkv) for k in places],
        out_specs=[
            pl.BlockSpec((rows // steps, 2, hidden), lambda i: (i, 0, 0)),
            pl.BlockSpec((hidden // steps, part_rows), lambda i: (i, 0)),
            pl.BlockSpec((rows // steps, 3, width), lambda i: (i, 0, 0)),
        ],
        out_shape=[
            jax.ShapeDtypeStruct((rows, 2, hidden), F32),
            jax.ShapeDtypeStruct((hidden, part_rows), F32),
            jax.ShapeDtypeStruct((rows, 3, width), F32),
        ],
        compiler_params=pltpu.CompilerParams(vmem_limit_bytes=62 * 2**20),
    )(
        *[own_gu] + [near_gu] * len(direct),
        *[own_down] + [near_down] * len(direct),
        *[own_qkv] + [near_qkv] * len(direct),
    )


def reduce_rows(values):
    return lax.psum_scatter(values.astype(BF16), "tp", scatter_dimension=0, tiled=True).astype(F32)


def local(tokens, lengths, ln_gains, ln_shifts, w_qkv, b_qkv, w_out, w_gate_up, w_down, cotangent):
    n_fsdp, n_tp = lax.axis_size("fsdp"), lax.axis_size("tp")
    sizes = (n_fsdp, n_tp)
    at_tp = lax.axis_index("tp")
    slab_rows, model_width = tokens.shape
    seq_len = slab_rows * n_tp
    small = ln_gains.shape[1]
    local_width = w_qkv.shape[2]
    hidden_width = w_gate_up.shape[2]
    part_rows = w_qkv.shape[0]

    length_row = lengths[0]
    doc_ends = jnp.cumsum(length_row)
    ids = jnp.arange(seq_len, dtype=jnp.int32)
    passed = (doc_ends[None, :] <= ids[:, None]).astype(jnp.int32)
    starts = jnp.sum(passed * length_row[None, :], axis=1)
    places = (ids - starts).astype(F32)
    frequency = 10000.0 ** (-2.0 * jnp.arange(ROT // 2, dtype=F32) / ROT)
    angles = frequency[:, None] * places[None, :]
    turns = jnp.concatenate([jnp.cos(angles), jnp.sin(angles)], axis=0)
    starts_row = starts.reshape(1, seq_len).astype(jnp.int32)
    widest = seq_len // 2

    tile = jnp.concatenate([ln_gains, ln_shifts, b_qkv.astype(F32), jnp.zeros((1, small), F32)], 0)
    tile = jnp.pad(tile, ((0, 0), (0, LANES - small)))
    (
        full_one, queries, key_vals, value_rows, residual, normed_two, norm_rows_all, attended_own,
        grad_branch, qkv_all, out_all, gu_all, down_all, *tables,
    ) = front(
        sizes, widest, tokens, cotangent, w_qkv.reshape(part_rows, 3 * local_width), w_out,
        w_gate_up.transpose(1, 0, 2), w_down, tile, turns, starts_row,
    )
    full_one = full_one.reshape(seq_len, model_width)

    grad_normed_two, branch_terms, sum_gu, sum_down, _, _, relay_gu, relay_down = middle(
        sizes, normed_two, grad_branch, gu_all, down_all
    )
    (
        grad_tokens, shares, near_gu, near_down, own_gu, own_down, sum_qkv, near_qkv, _, _, _, _, _, _,
        out_parts,
    ) = back(
        sizes, widest, grad_normed_two, residual, tokens, cotangent, attended_own, out_all, qkv_all,
        queries, key_vals, value_rows, full_one, sum_gu, sum_down, relay_gu, relay_down,
        norm_rows_all, tables, starts_row,
    )
    branch = reduce_rows(branch_terms.reshape(seq_len, model_width))
    result = (residual + branch).astype(BF16)
    direct = [1, 2] if n_fsdp == 8 else list(range(1, n_fsdp // 2))

    gu_share, down_share, qkv_share = last_sums(
        own_gu, near_gu, own_down, near_down, sum_qkv, near_qkv, direct
    )
    shares = shares[:, :small]
    return (
        result,
        grad_tokens,
        shares[0:2],
        shares[2:4],
        qkv_share,
        shares[4:7],
        jnp.sum(out_parts.astype(F32), axis=0),
        gu_share,
        down_share,
    )


def solution(mesh):
    placed = (
        P(("fsdp", "tp"), None),
        P("fsdp", None),
        P(None, ("fsdp", "tp")),
        P(None, ("fsdp", "tp")),
        P("fsdp", None, "tp"),
        P(None, ("tp", "fsdp")),
        P("tp", "fsdp"),
        P("fsdp", None, "tp"),
        P("tp", "fsdp"),
        P(("fsdp", "tp"), None),
    )
    return jax.shard_map(
        local,
        mesh=mesh,
        in_specs=placed,
        out_specs=(
            P(("fsdp", "tp"), None),
            P(("fsdp", "tp"), None),
            P(None, ("fsdp", "tp")),
            P(None, ("fsdp", "tp")),
            P("fsdp", None, "tp"),
            P(None, ("tp", "fsdp")),
            P("tp", "fsdp"),
            P("fsdp", None, "tp"),
            P("tp", "fsdp"),
        ),
        check_vma=False,
    )
```

```python
import functools

import jax
import jax.numpy as jnp
from jax import lax
from jax.experimental import pallas as pl
from jax.experimental.pallas import tpu as pltpu
from jax.sharding import PartitionSpec as P

HEAD = 64
ROT = 16
NORM_EPS = 1e-05
LANES = 128
MESH = pl.DeviceIdType.MESH
NN = (((1,), (0,)), ((), ()))
NT = (((1,), (1,)), ((), ()))
TN = (((0,), (0,)), ((), ()))
F32 = jnp.float32
BF16 = jnp.bfloat16


def dot(left, right, dims):
    return lax.dot_general(left, right, dims, preferred_element_type=F32)


def turn(values, cosine, sine_low, sine_high):
    return (
        values * cosine
        + pltpu.roll(values, LANES - ROT // 2, 1) * sine_low
        + pltpu.roll(values, ROT // 2, 1) * sine_high
    )


def key_range(block, rows, widest):
    first = max(0, block * rows - widest)
    return first, (block + 1) * rows


def seen_weights(key_rows, query_cols, starts_row, first_key, first_query):
    scores = dot(key_rows, query_cols, NN)
    key_ids = first_key + lax.broadcasted_iota(jnp.int32, scores.shape, 0)
    query_ids = first_query + lax.broadcasted_iota(jnp.int32, scores.shape, 1)
    seen = (key_ids <= query_ids) & (key_ids >= starts_row)
    scores = jnp.where(seen, scores, -1e30)
    top = jnp.max(scores, axis=0, keepdims=True)
    weights = jnp.exp(scores - top)
    return weights, jnp.sum(weights, axis=0, keepdims=True)


def xor(value, mask):
    bit = 1
    while bit <= mask:
        if mask & bit:
            value = value + bit * (1 - 2 * lax.rem(value // bit, 2))
        bit *= 2
    return value


class Places:
    def __init__(self, n_fsdp, n_tp):
        self.n_fsdp, self.n_tp = n_fsdp, n_tp
        self.f, self.t = lax.axis_index("fsdp"), lax.axis_index("tp")
        self.chip, self.core = self.f // 2, lax.rem(self.f, 2)

    def near_f(self, k):
        return xor(self.chip, k) * 2 + self.core

    def near(self, k):
        return (self.near_f(k), self.t)

    def sibling(self):
        return (self.chip * 2 + 1 - self.core, self.t)

    def along(self, t):
        return (self.f, t)

    def greet(self):
        barrier = pltpu.get_barrier_semaphore()
        partners = [self.near(k) for k in range(1, self.n_fsdp // 2)] + [self.sibling()]
        partners += [self.along(lax.rem(self.t + k, self.n_tp)) for k in range(1, self.n_tp)]
        for partner in partners:
            pl.semaphore_signal(barrier, inc=1, device_id=partner, device_id_type=MESH)
        pl.semaphore_wait(barrier, len(partners))


def send(src, dst, send_sem, recv_sem, device):
    return pltpu.make_async_remote_copy(
        src_ref=src,
        dst_ref=dst,
        send_sem=send_sem,
        recv_sem=recv_sem,
        device_id=device,
        device_id_type=MESH,
    )


class Line:
    def __init__(self, at, own, slots, send_sems, recv_sems):
        self.at, self.own, self.slots = at, own, slots
        self.send_sems, self.recv_sems = send_sems, recv_sems

    def copy(self, slot, way, first):
        at = self.at
        return send(
            self.own if first else self.slots.at[slot],
            self.slots.at[slot],
            self.send_sems.at[way, slot],
            self.recv_sems.at[slot],
            at.along(at.t + 1 - 2 * way),
        )

    def start(self):
        at = self.at
        pl.when(at.t < at.n_tp - 1)(lambda: self.copy(at.t, 0, True).start())
        pl.when(at.t > 0)(lambda: self.copy(at.t, 1, True).start())

    def start_inner(self):
        at = self.at
        pl.when(at.t < at.n_tp - 2)(lambda: self.copy(at.t, 0, True).start())
        pl.when(at.t > 1)(lambda: self.copy(at.t, 1, True).start())

    def start_outer(self):
        at = self.at
        pl.when(at.t == at.n_tp - 2)(lambda: self.copy(at.t, 0, True).start())
        pl.when(at.t == 1)(lambda: self.copy(at.t, 1, True).start())

    def step(self, s, on=True):
        at = self.at

        @pl.when(at.t >= s)
        def _():
            self.copy(at.t - s, 0, False).wait_recv()
            if on:
                pl.when(at.t < at.n_tp - 1)(lambda: self.copy(at.t - s, 0, False).start())

        @pl.when(at.t + s < at.n_tp)
        def _():
            self.copy(at.t + s, 1, False).wait_recv()
            if on:
                pl.when(at.t > 0)(lambda: self.copy(at.t + s, 1, False).start())

    def finish(self, last=None):
        at = self.at
        for s in range(at.n_tp if last is None else last):
            pl.when((at.t >= s) & (at.t < at.n_tp - 1))(
                lambda s=s: self.copy(at.t - s, 0, s == 0).wait_send()
            )
            pl.when((at.t + s < at.n_tp) & (at.t > 0))(
                lambda s=s: self.copy(at.t + s, 1, s == 0).wait_send()
            )


class Shards:
    def __init__(self, at, own, whole, by_rows, near_sems, sib_sems, index):
        self.at, self.own, self.whole, self.by_rows = at, own, whole, by_rows
        self.near_sems, self.sib_sems, self.index = near_sems, sib_sems, index
        self.half = at.n_fsdp // 2
        self.relay = at.n_fsdp == 8
        self.direct = [1, 2] if self.relay else list(range(1, self.half))

    def slot(self, f, part=None):
        if self.by_rows:
            rows = self.whole.shape[-2] // self.at.n_fsdp
            first = f * rows
            if part is not None:
                rows = rows // 2
                first = first + part * rows
            here = pl.ds(pl.multiple_of(first, rows), rows)
            return self.whole.at[:, here, :] if len(self.whole.shape) == 3 else self.whole.at[here, :]
        width = self.whole.shape[1] // self.at.n_fsdp
        columns = pl.ds(pl.multiple_of(f * width, LANES), width)
        if part is None:
            return self.whole.at[:, columns]
        rows = self.whole.shape[0] // 2
        return self.whole.at[pl.ds(part * rows, rows), columns]

    def near_copy(self, k):
        return send(
            self.own,
            self.slot(self.at.f),
            self.near_sems.at[self.index, 0, k],
            self.near_sems.at[self.index, 1, k],
            self.at.near(k),
        )

    def start(self):
        for k in self.direct:
            self.near_copy(k).start()
        self.sib_copy(0).start()

    def arrived(self, k):
        slot = self.slot(self.at.near_f(k))
        send(
            slot,
            slot,
            self.near_sems.at[self.index, 0, k],
            self.near_sems.at[self.index, 1, k],
            self.at.near(k),
        ).wait_recv()

    def relay_copy(self, part):
        source, target = (1, 2) if part == 0 else (2, 1)
        slot = self.slot(self.at.near_f(source), part)
        return send(
            slot,
            slot,
            self.near_sems.at[self.index, 0, 3 + part],
            self.near_sems.at[self.index, 1, 3 + part],
            self.at.near(target),
        )

    def sib_copy(self, k):
        f = self.at.near_f(k)
        return send(
            self.own if k == 0 else self.slot(f),
            self.slot(f),
            self.sib_sems.at[self.index, 0, k],
            self.sib_sems.at[self.index, 1, k],
            self.at.sibling(),
        )

    def pass_on(self):
        for k in self.direct:
            self.arrived(k)
            if self.relay:
                self.relay_copy(k - 1).start()
        for k in self.direct:
            self.sib_copy(k).start()

    def pass_last(self):
        if self.relay:
            for part in range(2):
                slot = self.slot(self.at.near_f(3), part)
                send(
                    slot,
                    slot,
                    self.near_sems.at[self.index, 0, 3 + part],
                    self.near_sems.at[self.index, 1, 3 + part],
                    self.at.near(2 - part),
                ).wait_recv()
            self.sib_copy(3).start()

    def complete(self):
        for k in range(self.half):
            f = xor(self.at.chip, k) * 2 + 1 - self.at.core
            slot = self.slot(f)
            send(
                slot,
                slot,
                self.sib_sems.at[self.index, 0, k],
                self.sib_sems.at[self.index, 1, k],
                self.at.sibling(),
            ).wait_recv()

    def finish(self):
        for k in self.direct:
            self.near_copy(k).wait_send()
        if self.relay:
            for part in range(2):
                self.relay_copy(part).wait_send()
        for k in range(self.half):
            self.sib_copy(k).wait_send()


def norm_rows(values, gain_row, shift_row):
    average = jnp.mean(values, axis=-1, keepdims=True)
    centred = values - average
    variance = jnp.mean(centred * centred, axis=-1, keepdims=True)
    return centred * lax.rsqrt(variance + NORM_EPS) * gain_row + shift_row


def front_kernel(
    sizes, widest,
    tok, cot, wq, wo, wgu, wd, tile, turns, starts,
    one, q_out, k_out, v_out, resid, two, rows_out, att_out, cot_all, wq_all, wo_all, wgu_all, wd_all,
    cos, s_low, s_high,
    toks, wq_v, wo_v, att, heads, vt, small, bias,
    tok_send, tok_recv, cot_send, cot_recv, near_sems, sib_sems, wz_sems, small_sems,
    swap_send, swap_recv, local_sems,
):
    n_fsdp, n_tp = sizes
    half = n_fsdp // 2
    at = Places(n_fsdp, n_tp)
    slab, model = tok.shape
    width = q_out.shape[1]
    each = wo.shape[0]
    at.greet()

    line = Line(at, tok, toks, tok_send, tok_recv)
    line.start()
    grads = Line(at, cot, cot_all, cot_send, cot_recv)
    weights = [
        Shards(at, wq, wq_all, True, near_sems, sib_sems, 0),
        None,
        Shards(at, wgu, wgu_all, True, near_sems, sib_sems, 2),
        Shards(at, wd, wd_all, False, near_sems, sib_sems, 3),
    ]
    weights[1] = Shards(at, None, wo_all, False, near_sems, sib_sems, 1)
    weights[1].own = weights[1].slot(at.f)
    weights[0].start()

    own_columns = pl.ds(pl.multiple_of(at.f * (model // n_fsdp), LANES), model // n_fsdp)

    def wo_rows(t):
        return wo_all.at[pl.ds(pl.multiple_of(t * each, each), each), own_columns]

    def wo_copy(k):
        return send(wo, wo_rows(at.t), wz_sems.at[0, k], wz_sems.at[1, k], at.along(lax.rem(at.t + k, n_tp)))

    for k in range(1, n_tp):
        wo_copy(k).start()
    own_copies = [
        pltpu.make_async_copy(tok, toks.at[at.t], local_sems.at[0]),
        pltpu.make_async_copy(wq, weights[0].slot(at.f), local_sems.at[1]),
        pltpu.make_async_copy(wo, wo_rows(at.t), local_sems.at[2]),
        pltpu.make_async_copy(wgu, weights[2].slot(at.f), local_sems.at[3]),
        pltpu.make_async_copy(wd, weights[3].slot(at.f), local_sems.at[4]),
        pltpu.make_async_copy(cot, cot_all.at[at.t], local_sems.at[5]),
    ]
    for copy in own_copies:
        copy.start()

    eight = ROT // 2
    cosine, sine = turns[0:eight, :], turns[eight : 2 * eight, :]
    none = jnp.zeros_like(sine)
    flat = jnp.zeros((HEAD - ROT, turns.shape[1]), F32)
    cos[...] = jnp.concatenate([cosine, cosine, flat + 1.0] * 2, axis=0).T
    s_low[...] = jnp.concatenate([-sine, none, flat] * 2, axis=0).T
    s_high[...] = jnp.concatenate([none, sine, flat] * 2, axis=0).T

    small[at.t, at.f] = tile[...]
    mine = small.at[at.t, at.f]
    to_sib = send(mine, mine, small_sems.at[0, 0], small_sems.at[1, 0], at.sibling())
    to_sib.start()
    to_sib.wait()
    pair = small.at[at.t, pl.ds(at.chip * 2, 2)]
    to_near = [
        send(pair, pair, small_sems.at[0, k], small_sems.at[1, k], at.near(k)) for k in range(1, half)
    ]
    for copy in to_near:
        copy.start()
    for k in range(1, half):
        to_near[k - 1].wait_send()
        came = small.at[at.t, pl.ds(xor(at.chip, k) * 2, 2)]
        send(came, came, small_sems.at[0, k], small_sems.at[1, k], at.near(k)).wait_recv()
    plane = small.at[at.t]
    to_line = [
        send(
            plane, plane, small_sems.at[0, half + k], small_sems.at[1, half + k],
            at.along(lax.rem(at.t + k, n_tp)),
        )
        for k in range(1, n_tp)
    ]
    for copy in to_line:
        copy.start()
    for k in range(1, n_tp):
        to_line[k - 1].wait_send()
        came = small.at[lax.rem(at.t + n_tp - k, n_tp)]
        send(
            came, came, small_sems.at[0, half + k], small_sems.at[1, half + k],
            at.along(lax.rem(at.t + k, n_tp)),
        ).wait_recv()
    lanes_each = model // (n_fsdp * n_tp)
    group = LANES // lanes_each
    for i in range(model // LANES):
        total = jnp.zeros((8, LANES), F32)
        for j in range(group):
            linear = i * group + j
            total = total + pltpu.roll(small[linear % n_tp, linear // n_tp], j * lanes_each, 1)
        rows_out[:, i * LANES : (i + 1) * LANES] = total
    for i in range(width // LANES):
        total = jnp.zeros((8, LANES), F32)
        for j in range(group):
            total = total + pltpu.roll(small[at.t, i * group + j], j * lanes_each, 1)
        bias[:, i * LANES : (i + 1) * LANES] = total
    own_copies[0].wait()

    def normalise(slot):
        step = 32

        def some(i, carry):
            here = pl.ds(pl.multiple_of(i * step, step), step)
            one[slot, here, :] = norm_rows(
                toks[slot, here, :].astype(F32), rows_out[0:1, :], rows_out[2:3, :]
            ).astype(BF16)
            return carry

        lax.fori_loop(0, slab // step, some, 0)

    wide = 256

    def project(slot):
        here = pl.ds(pl.multiple_of(slot * slab, slab), slab)
        for part, out in enumerate((q_out, k_out, v_out)):

            def some(i, carry, part=part, out=out):
                values = dot(
                    one[slot], wq_v[:, pl.ds(pl.multiple_of(part * width + i * wide, wide), wide)], NN
                )
                for j in range(wide // LANES):
                    lanes = pl.ds(pl.multiple_of(i * wide + j * LANES, LANES), LANES)
                    piece = values[:, j * LANES : (j + 1) * LANES] + bias[4 + part : 5 + part, lanes]
                    if part < 2:
                        piece = turn(piece, cos[here, :], s_low[here, :], s_high[here, :])
                    out[here, lanes] = piece.astype(BF16)
                return carry

            lax.fori_loop(0, width // wide, some, 0)

    def each_from(first, last, work):
        def some(i, carry):
            s = (i + 1) // 2
            slot = at.t + s * (2 * lax.rem(i, 2) - 1)
            pl.when((slot >= 0) & (slot < n_tp))(lambda: work(slot))
            return carry

        lax.fori_loop(max(0, 2 * first - 1), 2 * last - 1, some, 0)

    normalise(at.t)
    for s in range(1, n_tp - 1):
        line.step(s)
        if s == 1:
            weights[0].pass_on()
            own_copies[2].wait()
            for k in range(1, n_tp):
                wo_copy(k).wait_send()
                came = wo_rows(lax.rem(at.t + n_tp - k, n_tp))
                send(came, came, wz_sems.at[0, k], wz_sems.at[1, k], at.along(at.t)).wait_recv()
            weights[1].start()
        if s == 2:
            weights[0].pass_last()
            weights[2].start()
            grads.start_inner()
        each_from(s, s + 1, normalise)
    own_copies[1].wait()
    weights[0].complete()
    load = pltpu.make_async_copy(wq_all, wq_v, local_sems.at[6])
    load.start()
    load.wait()
    each_from(0, n_tp - 1, project)
    weights[1].pass_on()
    weights[3].start()
    line.step(n_tp - 1)
    grads.start_outer()
    each_from(n_tp - 1, n_tp, normalise)
    each_from(n_tp - 1, n_tp, project)

    def swap_copy(i, k):
        lanes = pl.ds(pl.multiple_of(i * LANES, LANES), LANES)
        columns = pl.ds(pl.multiple_of(at.t * width + i * LANES, LANES), LANES)
        other = lax.rem(at.t + k, n_tp)
        return send(
            heads.at[other, :, lanes], att.at[:, columns],
            swap_send.at[i, k], swap_recv.at[i, k], at.along(other),
        )

    def some_heads(i, carry):
        lanes = pl.ds(pl.multiple_of(i * LANES, LANES), LANES)
        attend(widest, q_out, k_out, v_out, starts, heads, vt, lanes, slab)
        for k in range(1, n_tp):
            swap_copy(i, k).start()
        columns = pl.ds(pl.multiple_of(at.t * width + i * LANES, LANES), LANES)
        att[:, columns] = heads[at.t, :, lanes]
        pl.when(i == width // LANES // 2 - 1)(weights[1].pass_last)
        return carry

    lax.fori_loop(0, width // LANES, some_heads, 0)
    weights[2].pass_on()
    weights[1].complete()
    load = pltpu.make_async_copy(wo_all, wo_v, local_sems.at[7])
    load.start()

    def took_heads(i, carry):
        for k in range(1, n_tp):
            swap_copy(i, k).wait_send()
            source = lax.rem(at.t + n_tp - k, n_tp)
            came = att.at[:, pl.ds(pl.multiple_of(source * width + i * LANES, LANES), LANES)]
            send(came, came, swap_send.at[i, k], swap_recv.at[i, k], at.along(source)).wait_recv()
        return carry

    lax.fori_loop(0, width // LANES, took_heads, 0)
    grads.step(1)
    keep = pltpu.make_async_copy(att, att_out, local_sems.at[8])
    keep.start()
    load.wait()

    def out_columns(i, carry):
        here = pl.ds(pl.multiple_of(i * wide, wide), wide)
        resid[:, here] = toks[at.t, :, here].astype(F32) + dot(att[...], wo_v[:, here], NN)
        return carry

    lax.fori_loop(0, model // wide, out_columns, 0)
    weights[3].pass_on()

    def second_norm(i, carry):
        here = pl.ds(pl.multiple_of(i * 32, 32), 32)
        two[here, :] = norm_rows(resid[here, :], rows_out[1:2, :], rows_out[3:4, :]).astype(BF16)
        return carry

    lax.fori_loop(0, slab // 32, second_norm, 0)

    weights[2].pass_last()
    weights[3].pass_last()
    for s in range(2, n_tp - 1):
        grads.step(s, on=s < n_tp - 2)
    for copy in own_copies[3:]:
        copy.wait()
    weights[2].complete()
    weights[3].complete()
    keep.wait()
    line.finish()
    grads.finish(n_tp - 2)
    for weight in weights:
        weight.finish()


def attend(widest, q_in, k_in, v_in, starts, heads, vt, lanes, slab):
    seq_len = q_in.shape[0]
    rows = min(256, seq_len)
    vt[...] = v_in[:, lanes].astype(F32).T.astype(BF16)
    for block in range(seq_len // rows):
        here = slice(block * rows, (block + 1) * rows)
        first, last = key_range(block, rows, widest)
        query_cols = (q_in[here, lanes].astype(F32) * HEAD**-0.5).T.astype(BF16)
        head_of = lax.broadcasted_iota(jnp.int32, query_cols.shape, 0) // HEAD
        parts = []
        for head in range(LANES // HEAD):
            own_cols = jnp.where(head_of == head, query_cols, jnp.zeros_like(query_cols))
            weights, total = seen_weights(
                k_in[first:last, lanes], own_cols, starts[:, here], first, block * rows
            )
            part = dot(vt[head * HEAD : (head + 1) * HEAD, first:last], weights.astype(BF16), NN)
            parts.append(part / total)
        found = jnp.concatenate(parts, axis=0).T.astype(BF16)
        for j in range(max(1, rows // slab)):
            count = min(slab, rows)
            row = block * rows + j * count
            heads[row // slab, row % slab : row % slab + count, lanes] = found[
                j * count : (j + 1) * count, :
            ]


def front(sizes, widest, tok, cot, wq, wo, wgu, wd, tile, turns, starts):
    n_fsdp, n_tp = sizes
    half = n_fsdp // 2
    slab, model = tok.shape
    seq_len = slab * n_tp
    width = wq.shape[1] // 3
    hidden = wd.shape[0]
    hbm = pl.BlockSpec(memory_space=pl.ANY)
    vmem = pl.BlockSpec(memory_space=pltpu.VMEM)
    shape = jax.ShapeDtypeStruct
    outs = [
        (shape((n_tp, slab, model), BF16), vmem),
        (shape((seq_len, width), BF16), vmem),
        (shape((seq_len, width), BF16), vmem),
        (shape((seq_len, width), BF16), vmem),
        (shape((slab, model), F32), vmem),
        (shape((slab, model), BF16), vmem),
        (shape((8, model), F32), vmem),
        (shape((slab, model), BF16), hbm),
        (shape((n_tp, slab, model), BF16), hbm),
        (shape((model, 3 * width), BF16), hbm),
        (shape((model, model), BF16), hbm),
        (shape((2, model, hidden), BF16), hbm),
        (shape((hidden, model), BF16), hbm),
    ] + [(shape((seq_len, LANES), F32), vmem)] * 3
    dma = pltpu.SemaphoreType.DMA
    pairs = width // LANES
    return pl.pallas_call(
        functools.partial(front_kernel, sizes, widest),
        in_specs=[vmem] * 9,
        out_specs=[spec for _, spec in outs],
        out_shape=[out for out, _ in outs],
        scratch_shapes=[
            pltpu.VMEM((n_tp, slab, model), BF16),
            pltpu.VMEM((model, 3 * width), BF16),
            pltpu.VMEM((model, model), BF16),
            pltpu.VMEM((slab, model), BF16),
            pltpu.VMEM((n_tp, slab, width), BF16),
            pltpu.VMEM((LANES, seq_len), BF16),
            pltpu.VMEM((n_tp, n_fsdp, 8, LANES), F32),
            pltpu.VMEM((8, width), F32),
            dma((2, n_tp)), dma((n_tp,)), dma((2, n_tp)), dma((n_tp,)),
            dma((4, 2, half + 1)), dma((4, 2, half)), dma((2, n_tp)), dma((2, half + n_tp)),
            dma((pairs, n_tp)), dma((pairs, n_tp)), dma((9,)),
        ],
        compiler_params=pltpu.CompilerParams(
            collective_id=1, has_side_effects=True, vmem_limit_bytes=60 * 2**20
        ),
        cost_estimate=pl.CostEstimate(flops=10**11, bytes_accessed=10**8, transcendentals=0),
    )(tok, cot, wq, wo, wgu, wd, tile, turns, starts)


def xor_any(value, mask, bits):
    total = 0
    for b in range(bits):
        both = lax.rem(value // 2**b, 2) + lax.rem(mask // 2**b, 2)
        total = total + lax.rem(both, 2) * 2**b
    return total


class Fold:
    def __init__(self, at, total, going, came, tile, send_sems, recv_sems):
        self.at, self.total, self.going, self.came, self.tile = at, total, going, came, tile
        self.send_sems, self.recv_sems = send_sems, recv_sems
        self.tiles = total.shape[1] // tile

    def lanes(self, c):
        return pl.ds(pl.multiple_of(c * self.tile, self.tile), self.tile)

    def copy(self, j, c, way):
        at = self.at
        slot = j if way == 0 else j + (at.n_tp - j) * lax.max(0, j - at.t + 2)
        return send(
            self.going.at[j, :, self.lanes(c)],
            self.came.at[slot, :, self.lanes(c)],
            self.send_sems.at[j, c],
            self.recv_sems.at[slot, c],
            at.along(at.t + 1 - 2 * way),
        )

    def put(self, j, c, values):
        at = self.at

        @pl.when(j == at.t)
        def _():
            self.total[:, self.lanes(c)] = values

        @pl.when(j != at.t)
        def _():
            self.going[j, :, self.lanes(c)] = values.astype(BF16)

        pl.when((j > at.t) & (at.t == 0))(lambda: self.copy(j, c, 0).start())
        pl.when((j < at.t) & (at.t == at.n_tp - 1))(lambda: self.copy(j, c, 1).start())

    def arrived(self, slot, c):
        tile = self.came.at[slot, :, self.lanes(c)]
        send(
            tile, tile, self.send_sems.at[0, c], self.recv_sems.at[slot, c], self.at.along(self.at.t)
        ).wait_recv()

    def forward(self, key, c):
        at = self.at

        def some(j, way):
            self.arrived(j, c)
            here = self.lanes(c)
            self.going[j, :, here] = (
                self.going[j, :, here].astype(F32) + self.came[j, :, here].astype(F32)
            ).astype(BF16)
            self.copy(j, c, way).start()

        pl.when((key > at.t) & (at.t > 0))(lambda: some(key, 0))
        down = at.n_tp - 1 - key
        pl.when((down < at.t) & (at.t < at.n_tp - 1))(lambda: some(down, 1))

    def end(self):
        at = self.at

        def some(c, carry):
            here = self.lanes(c)

            @pl.when(at.t > 0)
            def _():
                self.arrived(at.t, c)
                self.total[:, here] = self.total[:, here] + self.came[at.t, :, here].astype(F32)

            @pl.when(at.t < at.n_tp - 1)
            def _():
                self.arrived(at.n_tp, c)
                self.total[:, here] = self.total[:, here] + self.came[at.n_tp, :, here].astype(F32)

            return carry

        lax.fori_loop(0, self.tiles, some, 0)

    def finish(self):
        at = self.at

        def some(i, carry):
            j, c = i // self.tiles, lax.rem(i, self.tiles)
            pl.when(j > at.t)(lambda: self.copy(j, c, 0).wait_send())
            pl.when(j < at.t)(lambda: self.copy(j, c, 1).wait_send())
            return carry

        lax.fori_loop(0, at.n_tp * self.tiles, some, 0)


class Spread:
    def __init__(self, at, sums, near, relay, boxes, sems, local_sems):
        self.at, self.sums, self.near, self.relay, self.boxes = at, sums, near, relay, boxes
        self.sems, self.local_sems = sems, local_sems
        self.half = at.n_fsdp // 2
        self.by_relay = at.n_fsdp == 8
        self.direct = [1, 2] if self.by_relay else list(range(1, self.half))
        self.rows = sums.shape[1] // 2

    def part(self, i, part):
        return self.sums.at[i, pl.ds(part * self.rows, self.rows)]

    def relay_copy(self, part):
        return send(
            self.part(3, part), self.relay.at[part],
            self.sems.at[0, 3 + part], self.sems.at[1, 3 + part], self.at.near(1 + part),
        )

    def near_copy(self, i):
        return send(
            self.sums.at[i], self.near.at[i], self.sems.at[0, i], self.sems.at[1, i], self.at.near(i)
        )

    def start(self):
        if self.by_relay:
            for part in range(2):
                self.relay_copy(part).start()
        else:
            for i in self.direct:
                self.near_copy(i).start()

    def relayed(self):
        for part in range(2):
            self.relay_copy(part).wait_send()
            self.relay_copy(part).wait_recv()

    def add(self, here=False):
        if not self.by_relay:
            return
        for part, i in ((0, 2), (1, 1)):
            if not here:
                self.relay_copy(part).wait_recv()
            takes = [
                pltpu.make_async_copy(self.part(i, part), self.boxes.at[0], self.local_sems.at[0]),
                pltpu.make_async_copy(self.relay.at[part], self.boxes.at[1], self.local_sems.at[1]),
            ]
            for take in takes:
                take.start()
            for take in takes:
                take.wait()
            self.boxes[0] = (self.boxes[0].astype(F32) + self.boxes[1].astype(F32)).astype(BF16)
            keep = pltpu.make_async_copy(self.boxes.at[0], self.part(i, part), self.local_sems.at[0])
            keep.start()
            keep.wait()
            self.near_copy(i).start()

    def arrived(self):
        for i in self.direct:
            self.near_copy(i).wait_recv()

    def finish(self, relays=True):
        if self.by_relay and relays:
            for part in range(2):
                self.relay_copy(part).wait_send()
        for i in self.direct:
            self.near_copy(i).wait_send()


def middle_kernel(
    sizes,
    two, cot_all, wgu_all, wd_all,
    gn2, branch, sum_gu, sum_d, sib_gu, sib_d, relay_gu, relay_d,
    hidden, x, cots, wgu_v, wd_v, ggu, acts, came, going, stage_gu, stage_d, in_gu, in_d,
    line_send, line_recv, fold_send, fold_recv, sib_send, sib_recv, cot_sems, relay_sems, local_sems,
):
    n_fsdp, n_tp = sizes
    half = n_fsdp // 2
    bits = half.bit_length() - 1
    at = Places(n_fsdp, n_tp)
    slab, model = two.shape
    part_rows = model // n_fsdp
    at.greet()
    line = Line(at, two, x, line_send, line_recv)
    line.start()
    loads = [
        pltpu.make_async_copy(two, x.at[at.t], local_sems.at[0]),
        pltpu.make_async_copy(wgu_all, wgu_v, local_sems.at[1]),
        pltpu.make_async_copy(wd_all, wd_v, local_sems.at[2]),
    ]
    for load in loads:
        load.start()

    def cot_copy(j):
        return pltpu.make_async_copy(cot_all.at[j], cots.at[j], cot_sems.at[0, j])

    def cot_last(slot, way):
        return send(
            cot_all.at[slot], cots.at[slot], cot_sems.at[1, slot], cot_sems.at[2, slot], at.along(at.t + 1 - 2 * way)
        )

    for j in range(n_tp):
        pl.when((at.t - j < n_tp - 1) & (j - at.t < n_tp - 1))(cot_copy(j).start)
    for load in loads:
        load.wait()
    for j in range(n_tp):
        pl.when((at.t - j < n_tp - 1) & (j - at.t < n_tp - 1))(cot_copy(j).wait)
    fold = Fold(at, gn2, going, came, min(512, model), fold_send, fold_recv)

    def unit(slot):
        here = pl.ds(pl.multiple_of(slot * slab, slab), slab)
        acts[0] = dot(x[slot], wgu_v[0], NN)
        acts[1] = dot(x[slot], wgu_v[1], NN)
        acts[2] = dot(cots[slot], wd_v[...], NT)
        step = 16

        def some(i, carry):
            local_rows = pl.ds(pl.multiple_of(i * step, step), step)
            rows = pl.ds(pl.multiple_of(slot * slab + i * step, step), step)
            gate, up, grad = acts[0, local_rows, :], acts[1, local_rows, :], acts[2, local_rows, :]
            low = jax.nn.sigmoid(gate)
            act = gate * low
            hidden[rows, :] = (act * up).astype(BF16)
            ggu[0, rows, :] = (grad * up * low * (1.0 + gate * (1.0 - low))).astype(BF16)
            ggu[1, rows, :] = (grad * act).astype(BF16)
            return carry

        lax.fori_loop(0, slab // step, some, 0)

        def tiles(c, carry):
            rows = fold.lanes(c)
            fold.put(
                slot,
                c,
                dot(ggu[0, here, :], wgu_v[0, rows, :], NT) + dot(ggu[1, here, :], wgu_v[1, rows, :], NT),
            )
            return carry

        lax.fori_loop(0, fold.tiles, tiles, 0)

        def branch_copy(c):
            return pltpu.make_async_copy(
                stage_gu.at[c // 2 % 2, c % 2, pl.ds(0, slab), pl.ds(0, fold.tile)],
                branch.at[slot, :, fold.lanes(c)],
                local_sems.at[4 + c % 4],
            )

        for c in range(fold.tiles):
            if c >= 4:
                branch_copy(c - 4).wait()
            stage_gu[c // 2 % 2, c % 2, 0:slab, 0 : fold.tile] = dot(
                hidden[here, :], wd_v[:, c * fold.tile : (c + 1) * fold.tile], NN
            ).astype(BF16)
            branch_copy(c).start()
        for c in range(max(0, fold.tiles - 4), fold.tiles):
            branch_copy(c).wait()

    def each_from(first, last, work):
        def some(i, carry):
            s = (i + 1) // 2
            slot = at.t + s * (2 * lax.rem(i, 2) - 1)
            pl.when((slot >= 0) & (slot < n_tp))(lambda: work(slot))
            return carry

        lax.fori_loop(max(0, 2 * first - 1), 2 * last - 1, some, 0)

    for s in range(n_tp):
        if s:
            line.step(s)
        if s == 1:
            pl.when(at.t == n_tp - 2)(lambda: cot_last(0, 0).start())
            pl.when(at.t == 1)(lambda: cot_last(n_tp - 1, 1).start())
        if s == n_tp - 1:
            pl.when(at.t == n_tp - 1)(lambda: cot_last(0, 0).wait_recv())
            pl.when(at.t == 0)(lambda: cot_last(n_tp - 1, 1).wait_recv())
        each_from(s, s + 1, unit)

    for key in range(1, n_tp - 2):
        for c in range(fold.tiles):
            fold.forward(key, c)

    def block(f, take):
        columns = pl.ds(pl.multiple_of(f * part_rows, part_rows), part_rows)
        for part in range(2):
            rows = x[:, :, columns].reshape(n_tp * slab, part_rows)
            take(part, dot(rows, ggu[part], TN))
        grads = cots[:, :, columns].reshape(n_tp * slab, part_rows)
        take(2, dot(hidden[...], grads, TN))

    spreads = [
        Spread(at, sum_gu, None, relay_gu, None, relay_sems.at[0], None),
        Spread(at, sum_d, None, relay_d, None, relay_sems.at[1], None),
    ]
    by_relay = spreads[0].by_relay

    def order(n):
        return lax.rem(n + half - 1, half) if by_relay else n

    def sib_copies(n):
        i, slot = order(n), lax.rem(n, 2)
        return [
            send(stage_gu.at[slot], sib_gu.at[i], sib_send.at[0, i], sib_recv.at[0, i], at.sibling()),
            send(stage_d.at[slot], sib_d.at[i], sib_send.at[1, i], sib_recv.at[1, i], at.sibling()),
        ]

    def keep_copies(n):
        i, slot = order(n), lax.rem(n, 2)
        return [
            pltpu.make_async_copy(stage_gu.at[slot], sum_gu.at[i], local_sems.at[4 + slot]),
            pltpu.make_async_copy(stage_d.at[slot], sum_d.at[i], local_sems.at[6 + slot]),
        ]

    def others(n, carry):
        pl.when(n < fold.tiles)(lambda: fold.forward(n_tp - 2, n))

        @pl.when(n >= 2)
        def _():
            for copy in sib_copies(n - 2):
                copy.wait_send()

        def take(part, values):
            if part < 2:
                stage_gu[lax.rem(n, 2), part] = values.astype(BF16)
            else:
                stage_d[lax.rem(n, 2)] = values.astype(BF16)

        block(xor_any(at.chip, order(n), bits) * 2 + 1 - at.core, take)
        for copy in sib_copies(n):
            copy.start()
        return carry

    lax.fori_loop(0, half, others, 0)
    for n in range(half - 2, half):
        for copy in sib_copies(jnp.int32(n)):
            copy.wait_send()

    def mine(n, carry):
        for copy in sib_copies(n):
            copy.wait_recv()
        takes = [
            pltpu.make_async_copy(sib_gu.at[order(n)], in_gu, local_sems.at[8]),
            pltpu.make_async_copy(sib_d.at[order(n)], in_d, local_sems.at[9]),
        ]
        for take in takes:
            take.start()

        @pl.when(n >= 2)
        def _():
            for copy in keep_copies(n - 2):
                copy.wait()

        if by_relay:

            @pl.when(n == 2)
            def _():
                for spread in spreads:
                    spread.start()

        def take(part, values):
            if part == 0:
                for copy in takes:
                    copy.wait()
            if part < 2:
                stage_gu[lax.rem(n, 2), part] = (values + in_gu[part].astype(F32)).astype(BF16)
            else:
                stage_d[lax.rem(n, 2)] = (values + in_d[...].astype(F32)).astype(BF16)

        block(xor_any(at.chip, order(n), bits) * 2 + at.core, take)
        for copy in keep_copies(n):
            copy.start()
        return carry

    lax.fori_loop(0, half, mine, 0)
    for c in range(fold.tiles):
        fold.forward(n_tp - 1, c)
    fold.end()
    for i in range(half - 2, half):
        for copy in keep_copies(jnp.int32(i)):
            copy.wait()
    line.finish()
    pl.when(at.t == n_tp - 2)(lambda: cot_last(0, 0).wait_send())
    pl.when(at.t == 1)(lambda: cot_last(n_tp - 1, 1).wait_send())
    fold.finish()
    if by_relay:
        for spread in spreads:
            spread.relayed()


def middle(sizes, two, cot_all, wgu_all, wd_all):
    n_fsdp, n_tp = sizes
    half = n_fsdp // 2
    slab, model = two.shape
    hidden = wd_all.shape[0]
    part_rows = model // n_fsdp
    tile = min(512, model)
    hbm = pl.BlockSpec(memory_space=pl.ANY)
    vmem = pl.BlockSpec(memory_space=pltpu.VMEM)
    shape = jax.ShapeDtypeStruct
    outs = [
        (shape((slab, model), F32), vmem),
        (shape((n_tp, slab, model), BF16), hbm),
        (shape((half, 2, part_rows, hidden), BF16), hbm),
        (shape((half, hidden, part_rows), BF16), hbm),
        (shape((half, 2, part_rows, hidden), BF16), hbm),
        (shape((half, hidden, part_rows), BF16), hbm),
        (shape((2, 1, part_rows, hidden), BF16), hbm),
        (shape((2, hidden // 2, part_rows), BF16), hbm),
    ]
    dma = pltpu.SemaphoreType.DMA
    return pl.pallas_call(
        functools.partial(middle_kernel, sizes),
        in_specs=[hbm] * 4,
        out_specs=[spec for _, spec in outs],
        out_shape=[out for out, _ in outs],
        scratch_shapes=[
            pltpu.VMEM((n_tp * slab, hidden), BF16),
            pltpu.VMEM((n_tp, slab, model), BF16),
            pltpu.VMEM((n_tp, slab, model), BF16),
            pltpu.VMEM((2, model, hidden), BF16),
            pltpu.VMEM((hidden, model), BF16),
            pltpu.VMEM((2, n_tp * slab, hidden), BF16),
            pltpu.VMEM((3, slab, hidden), F32),
            pltpu.VMEM((n_tp + 1, slab, model), BF16),
            pltpu.VMEM((n_tp, slab, model), BF16),
            pltpu.VMEM((2, 2, part_rows, hidden), BF16),
            pltpu.VMEM((2, hidden, part_rows), BF16),
            pltpu.VMEM((2, part_rows, hidden), BF16),
            pltpu.VMEM((hidden, part_rows), BF16),
            dma((2, n_tp)), dma((n_tp,)), dma((n_tp, model // tile)), dma((n_tp + 1, model // tile)),
            dma((2, half)), dma((2, half)), dma((3, n_tp)), dma((2, 2, half + 1)), dma((10,)),
        ],
        compiler_params=pltpu.CompilerParams(
            collective_id=3, has_side_effects=True, vmem_limit_bytes=62 * 2**20
        ),
        cost_estimate=pl.CostEstimate(flops=10**11, bytes_accessed=10**8, transcendentals=0),
    )(two, cot_all, wgu_all, wd_all)


class Pair:
    def __init__(self, at, stage, sib, sums, inbox, sems, local_sems):
        self.at, self.stage, self.sib, self.sums, self.inbox = at, stage, sib, sums, inbox
        self.sems, self.local_sems = sems, local_sems

    def sib_copy(self, i):
        return send(
            self.stage.at[lax.rem(i, 2)], self.sib.at[i], self.sems.at[0, i], self.sems.at[1, i], self.at.sibling()
        )

    def keep_copy(self, i):
        return pltpu.make_async_copy(
            self.stage.at[lax.rem(i, 2)], self.sums.at[i], self.local_sems.at[lax.rem(i, 2)]
        )

    def give(self, i, values):
        pl.when(i >= 2)(lambda: self.sib_copy(i - 2).wait_send())
        self.stage[lax.rem(i, 2)] = values().astype(BF16)
        self.sib_copy(i).start()

    def given(self, half):
        for i in range(half - 2, half):
            self.sib_copy(jnp.int32(i)).wait_send()

    def keep(self, i, values):
        self.sib_copy(i).wait_recv()
        take = pltpu.make_async_copy(self.sib.at[i], self.inbox, self.local_sems.at[2])
        take.start()
        pl.when(i >= 2)(lambda: self.keep_copy(i - 2).wait())
        own = values()
        take.wait()
        self.stage[lax.rem(i, 2)] = (own + self.inbox[...].astype(F32)).astype(BF16)
        self.keep_copy(i).start()

    def kept(self, half):
        for i in range(half - 2, half):
            self.keep_copy(jnp.int32(i)).wait()


def norm_back(values, incoming, gain_row):
    average = jnp.mean(values, axis=-1, keepdims=True)
    centred = values - average
    scale = lax.rsqrt(jnp.mean(centred * centred, axis=-1, keepdims=True) + NORM_EPS)
    unit = centred * scale
    grads = incoming * gain_row
    inner = jnp.mean(grads * unit, axis=-1, keepdims=True)
    back = scale * (grads - jnp.mean(grads, axis=-1, keepdims=True) - unit * inner)
    return back, jnp.sum(incoming * unit, axis=0, keepdims=True), jnp.sum(incoming, axis=0, keepdims=True)


def attend_back(widest, q_in, k_in, v_in, g_in, cos, s_low, s_high, starts, g_out, bias, kt, dk, dv, first_lane):
    seq_len, width = q_in.shape
    rows = min(256, seq_len)
    lanes = pl.ds(pl.multiple_of(first_lane, LANES), LANES)
    kt[...] = k_in[:, lanes].astype(F32).T.astype(BF16)
    dk[...] = jnp.zeros_like(dk)
    dv[...] = jnp.zeros_like(dv)

    def put(part, here, values):
        columns = pl.ds(pl.multiple_of(part * width + first_lane, LANES), LANES)
        low = values.astype(BF16)
        g_out[here, columns] = low
        return jnp.sum(low.astype(F32), axis=0, keepdims=True)

    total_q = jnp.zeros((1, LANES), F32)
    for block in range(seq_len // rows):
        here = slice(block * rows, (block + 1) * rows)
        first, last = key_range(block, rows, widest)
        query_rows = (q_in[here, lanes].astype(F32) * HEAD**-0.5).astype(BF16)
        grad_rows = g_in[here, lanes]
        query_cols = query_rows.astype(F32).T.astype(BF16)
        grad_cols = grad_rows.astype(F32).T.astype(BF16)
        head_down = lax.broadcasted_iota(jnp.int32, query_cols.shape, 0) // HEAD
        head_along = lax.broadcasted_iota(jnp.int32, query_rows.shape, 1) // HEAD
        none_down, none_along = jnp.zeros_like(query_cols), jnp.zeros_like(query_rows)
        parts = []
        for head in range(LANES // HEAD):
            weights, total = seen_weights(
                k_in[first:last, lanes],
                jnp.where(head_down == head, query_cols, none_down),
                starts[:, here],
                first,
                block * rows,
            )
            probs = weights * (1.0 / total)
            grad_probs = dot(
                v_in[first:last, lanes], jnp.where(head_down == head, grad_cols, none_down), NN
            )
            inner = jnp.sum(probs * grad_probs, axis=0, keepdims=True)
            grad_scores = (probs * (grad_probs - inner)).astype(BF16)
            dk[first:last, :] += dot(
                grad_scores, jnp.where(head_along == head, query_rows, none_along), NN
            )
            dv[first:last, :] += dot(
                probs.astype(BF16), jnp.where(head_along == head, grad_rows, none_along), NN
            )
            parts.append(dot(kt[head * HEAD : (head + 1) * HEAD, first:last], grad_scores, NN))
        grad_queries = jnp.concatenate(parts, axis=0).T * HEAD**-0.5
        total_q = total_q + put(
            0, here, turn(grad_queries, cos[here, :], -s_low[here, :], -s_high[here, :])
        )
    everywhere = slice(0, seq_len)
    bias[4:5, lanes] = total_q
    bias[5:6, lanes] = put(1, everywhere, turn(dk[...], cos[...], -s_low[...], -s_high[...]))
    bias[6:7, lanes] = put(2, everywhere, dv[...])


def back_kernel(
    sizes, widest,
    gn2, resid, tok, cot, att_own, wo_all, wq_all, q_in, k_in, v_in, one, sum_gu_in, sum_d_in,
    relay_gu, relay_d, rows_in, cos, s_low, s_high, starts,
    grad_tok, small_out, near_gu, near_d, own_gu, own_d, sum_q, near_q, sib_q, relay_q,
    sum_o, near_o, sib_o, relay_o, zo,
    gres, res_v, tok_v, cot_v, att_v, gattn, wo_v, wq_v, q_v, k_v, v_v, gp, gatt, ghead, came, going,
    kt, dk, dv, stage_o, inbox_o, stage_q, inbox_q, box_gu, box_d, box_o, box_q, zo_stage, zo_box,
    norm_sums, bias, tiles, land_z, land_near, land_sib,
    swap_send, swap_recv, fold_send, fold_recv, pair_o_sems, pair_q_sems, gu_sems, d_sems, o_sems, q_sems,
    zo_sems, small_sems, local_sems, pair_o_local, pair_q_local,
):
    n_fsdp, n_tp = sizes
    half = n_fsdp // 2
    bits = half.bit_length() - 1
    at = Places(n_fsdp, n_tp)
    slab, model = tok.shape
    seq_len, width = q_in.shape
    part_rows = model // n_fsdp
    pairs = width // LANES
    loads = [
        pltpu.make_async_copy(src, dst, local_sems.at[i])
        for i, (src, dst) in enumerate(
            [
                (gn2, gres), (resid, res_v), (cot, cot_v), (wo_all, wo_v), (tok, tok_v), (att_own, att_v),
                (q_in, q_v), (k_in, k_v), (v_in, v_v), (wq_all, wq_v),
            ]
        )
    ]
    for load in loads:
        load.start()
    at.greet()
    spread_gu = Spread(at, own_gu, near_gu, relay_gu, box_gu, gu_sems, local_sems.at[pl.ds(13, 2)])
    spread_d = Spread(at, own_d, near_d, relay_d, box_d, d_sems, local_sems.at[pl.ds(13, 2)])
    spread_o = Spread(at, sum_o, near_o, relay_o, box_o, o_sems, local_sems.at[pl.ds(13, 2)])
    spread_q = Spread(at, sum_q, near_q, relay_q, box_q, q_sems, local_sems.at[pl.ds(13, 2)])
    if not spread_gu.by_relay:
        spread_gu.start()
        spread_d.start()
    norm_sums[...] = jnp.zeros_like(norm_sums)
    bias[...] = jnp.zeros_like(bias)
    for load in loads[:4]:
        load.wait()

    step = 16

    def second(i, carry):
        here = pl.ds(pl.multiple_of(i * step, step), step)
        back, gain, shift = norm_back(res_v[here, :], gres[here, :], rows_in[1:2, :])
        total = cot_v[here, :].astype(F32) + back
        gres[here, :] = total
        gattn[here, :] = total.astype(BF16)
        norm_sums[1:2, :] = norm_sums[1:2, :] + gain
        norm_sums[3:4, :] = norm_sums[3:4, :] + shift
        return carry

    lax.fori_loop(0, slab // step, second, 0)

    per = 2 if pairs % 2 == 0 else 1
    wide = per * LANES

    def swap_copy(i, k):
        lanes = pl.ds(pl.multiple_of(i * wide, wide), wide)
        other = lax.rem(at.t + k, n_tp)
        return send(
            ghead.at[other, :, lanes],
            gatt.at[pl.ds(pl.multiple_of(at.t * slab, slab), slab), lanes],
            swap_send.at[i, k], swap_recv.at[i, k], at.along(other),
        )

    def give_heads(i, carry):
        lanes = pl.ds(pl.multiple_of(i * wide, wide), wide)

        def to(k, carry):
            other = lax.rem(at.t + k, n_tp)
            rows = pl.ds(pl.multiple_of(other * width + i * wide, wide), wide)
            ghead[other, :, lanes] = dot(gattn[...], wo_v[rows, :], NT).astype(BF16)
            pl.when(k > 0)(lambda: swap_copy(i, k).start())
            return carry

        lax.fori_loop(0, n_tp, to, 0)
        gatt[pl.ds(pl.multiple_of(at.t * slab, slab), slab), lanes] = ghead[at.t, :, lanes]
        return carry

    lax.fori_loop(0, pairs // per, give_heads, 0)
    spread_gu.add(here=True)
    spread_d.add(here=True)

    loads[5].wait()
    pair_o = Pair(at, stage_o, sib_o, sum_o, inbox_o, pair_o_sems, pair_o_local)
    pair_q = Pair(at, stage_q, sib_q, sum_q, inbox_q, pair_q_sems, pair_q_local)

    def piece(f):
        return pl.ds(pl.multiple_of(f * part_rows, part_rows), part_rows)

    def owner(i, core):
        return xor_any(at.chip, i, bits) * 2 + core

    def give_o(i, carry):
        pair_o.give(i, lambda: dot(att_v[...], gattn[:, piece(owner(i, 1 - at.core))], TN))
        return carry

    lax.fori_loop(0, half, give_o, 0)
    for load in loads[6:9]:
        load.wait()
    load_one = pltpu.make_async_copy(one, wo_v.at[pl.ds(0, seq_len), :], local_sems.at[12])
    load_one.start()

    def some_heads(i, carry):
        def heads_came():
            block = i // per
            lanes = pl.ds(pl.multiple_of(block * wide, wide), wide)
            for k in range(1, n_tp):
                source = lax.rem(at.t + n_tp - k, n_tp)
                came_rows = gatt.at[pl.ds(pl.multiple_of(source * slab, slab), slab), lanes]
                send(
                    came_rows, came_rows, swap_send.at[block, k], swap_recv.at[block, k], at.along(source)
                ).wait_recv()

        pl.when(lax.rem(i, per) == 0)(heads_came)
        attend_back(
            widest, q_v, k_v, v_v, gatt, cos, s_low, s_high, starts, gp, bias, kt, dk, dv, i * LANES
        )

        def keep_o(n, carry):
            pair_o.keep(n, lambda: dot(att_v[...], gattn[:, piece(owner(n, at.core))], TN))
            return carry

        lax.fori_loop(i * half // pairs, (i + 1) * half // pairs, keep_o, 0)
        return carry

    pair_o.given(half)
    lax.fori_loop(0, pairs, some_heads, 0)
    pair_o.kept(half)
    spread_o.start()

    loads[9].wait()
    fold = Fold(at, grad_tok, going, came, min(512, model), fold_send, fold_recv)

    def term(slot):
        rows = gp[pl.ds(pl.multiple_of(slot * slab, slab), slab), :]

        def some(c, carry):
            fold.put(slot, c, dot(rows, wq_v[fold.lanes(c), :], NT))
            return carry

        lax.fori_loop(0, fold.tiles, some, 0)

    def far_first(i, carry):
        s = (2 * n_tp - 1 - i) // 2
        slot = at.t + s * (2 * lax.rem(i, 2) - 1)
        pl.when((slot >= 0) & (slot < n_tp))(lambda: term(slot))
        return carry

    lax.fori_loop(0, 2 * n_tp - 1, far_first, 0)

    load_one.wait()

    def give_q(i, carry):
        pair_q.give(i, lambda: dot(wo_v[0:seq_len, piece(owner(i, 1 - at.core))], gp[...], TN))
        return carry

    def keep_q(i, carry):
        pair_q.keep(i, lambda: dot(wo_v[0:seq_len, piece(owner(i, at.core))], gp[...], TN))
        return carry

    for c in range(fold.tiles):
        fold.forward(n_tp - 1, c)
        lax.fori_loop(half * c // fold.tiles, half * (c + 1) // fold.tiles, give_q, 0)
        if c == 1:
            spread_o.add()
    pair_q.given(half)
    for c in range(fold.tiles):
        fold.forward(n_tp - 2, c)
        lax.fori_loop(half * c // fold.tiles, half * (c + 1) // fold.tiles, keep_q, 0)
    pair_q.kept(half)
    spread_q.start()
    for key in range(n_tp - 3, 0, -1):
        for c in range(fold.tiles):
            fold.forward(key, c)

    each = model // n_tp
    spread_o.arrived()

    def zo_copy(k):
        other = lax.rem(at.t + k, n_tp)
        return send(zo_stage.at[other], zo.at[at.t], zo_sems.at[0, k], zo_sems.at[1, k], at.along(other))

    def group(k, carry):
        other = lax.rem(at.t + k, n_tp)
        rows = pl.ds(pl.multiple_of(other * each, each), each)
        takes = [
            pltpu.make_async_copy(
                (sum_o if i == 0 else near_o).at[i, rows, :], zo_box.at[n], local_sems.at[16 + n]
            )
            for n, i in enumerate([0] + spread_o.direct)
        ]
        for take in takes:
            take.start()
        total = jnp.zeros(zo_box.shape[1:], F32)
        for n, take in enumerate(takes):
            take.wait()
            total = total + zo_box[n].astype(F32)
        zo_stage[other] = total.astype(BF16)
        return carry

    lax.fori_loop(0, n_tp, group, 0)
    own_zo = pltpu.make_async_copy(zo_stage.at[at.t], zo.at[at.t], local_sems.at[15])
    own_zo.start()

    for k in range(1, n_tp):
        zo_copy(k).start()
    spread_q.add()

    fold.end()
    loads[4].wait()

    def first(i, carry):
        here = pl.ds(pl.multiple_of(i * step, step), step)
        back, gain, shift = norm_back(tok_v[here, :].astype(F32), grad_tok[here, :], rows_in[0:1, :])
        grad_tok[here, :] = gres[here, :] + back
        norm_sums[0:1, :] = norm_sums[0:1, :] + gain
        norm_sums[2:3, :] = norm_sums[2:3, :] + shift
        return carry

    lax.fori_loop(0, slab // step, first, 0)

    lanes_each = model // (n_fsdp * n_tp)
    kept = lax.broadcasted_iota(jnp.int32, (8, LANES), 1) < lanes_each

    def tile_of(ref, index):
        start = index * lanes_each
        tile = ref[:, start // LANES * LANES : start // LANES * LANES + LANES]
        return jnp.where(kept, pltpu.roll(tile, (LANES - start % LANES) % LANES, 1), 0.0)

    for f in range(n_fsdp):
        for t in range(n_tp):
            tiles[t, f] = tile_of(norm_sums, f * n_tp + t)
    for f in range(n_fsdp):
        tiles[at.t, f] = tiles[at.t, f] + tile_of(bias, f)

    def z_copy(k):
        other = lax.rem(at.t + k, n_tp)
        return send(
            tiles.at[other], land_z.at[k], small_sems.at[0, half + k], small_sems.at[1, half + k], at.along(other)
        )

    for k in range(1, n_tp):
        z_copy(k).start()
    total = tiles[at.t]
    for k in range(1, n_tp):
        z_copy(k).wait_recv()
        total = total + land_z[k]
    land_z[0] = total

    def chip_copy(k):
        return send(
            land_z.at[0, pl.ds(xor(at.chip, k) * 2, 2)], land_near.at[k],
            small_sems.at[0, k], small_sems.at[1, k], at.near(k),
        )

    for k in range(1, half):
        chip_copy(k).start()
    total = land_z[0, pl.ds(at.chip * 2, 2)]
    for k in range(1, half):
        chip_copy(k).wait_recv()
        total = total + land_near[k]
    land_near[0] = total
    to_sib = send(
        land_near.at[0, 1 - at.core], land_sib, small_sems.at[0, 0], small_sems.at[1, 0], at.sibling()
    )
    to_sib.start()
    to_sib.wait_recv()
    small_out[...] = land_near[0, at.core] + land_sib[...]

    to_sib.wait_send()
    for k in range(1, half):
        chip_copy(k).wait_send()
    for k in range(1, n_tp):
        z_copy(k).wait_send()
        zo_copy(k).wait_send()
        source = lax.rem(at.t + n_tp - k, n_tp)
        send(zo.at[source], zo.at[source], zo_sems.at[0, k], zo_sems.at[1, k], at.along(source)).wait_recv()
    own_zo.wait()

    def swapped(i, carry):
        for k in range(1, n_tp):
            swap_copy(i, k).wait_send()
        return carry

    lax.fori_loop(0, pairs // per, swapped, 0)
    fold.finish()
    for spread in (spread_gu, spread_d, spread_q):
        spread.arrived()
    for spread in (spread_gu, spread_d):
        spread.finish(relays=False)
    for spread in (spread_q, spread_o):
        spread.finish()


def back(sizes, widest, gn2, resid, tok, cot, att_own, wo_all, wq_all, q_in, k_in, v_in, one, sum_gu, sum_d, relay_gu, relay_d, rows_in, tables, starts):
    n_fsdp, n_tp = sizes
    half = n_fsdp // 2
    slab, model = tok.shape
    seq_len, width = q_in.shape
    hidden = sum_d.shape[1]
    part_rows = model // n_fsdp
    pairs = width // LANES
    each = model // n_tp
    tile = min(512, model)
    hbm = pl.BlockSpec(memory_space=pl.ANY)
    vmem = pl.BlockSpec(memory_space=pltpu.VMEM)
    shape = jax.ShapeDtypeStruct
    piece_q, piece_o = (part_rows, 3 * width), (model, part_rows)
    piece_gu, piece_d = sum_gu.shape[1:], sum_d.shape[1:]
    halved = lambda piece: (piece[0] // 2,) + tuple(piece[1:])
    outs = [
        (shape((slab, model), F32), vmem),
        (shape((8, LANES), F32), vmem),
        (shape(sum_gu.shape, BF16), hbm),
        (shape(sum_d.shape, BF16), hbm),
        (shape(sum_gu.shape, BF16), hbm),
        (shape(sum_d.shape, BF16), hbm),
        (shape((half,) + piece_q, BF16), hbm),
        (shape((half,) + piece_q, BF16), hbm),
        (shape((half,) + piece_q, BF16), hbm),
        (shape((2,) + halved(piece_q), BF16), hbm),
        (shape((half,) + piece_o, BF16), hbm),
        (shape((half,) + piece_o, BF16), hbm),
        (shape((half,) + piece_o, BF16), hbm),
        (shape((2,) + halved(piece_o), BF16), hbm),
        (shape((n_tp, each, part_rows), BF16), hbm),
    ]
    dma = pltpu.SemaphoreType.DMA
    return pl.pallas_call(
        functools.partial(back_kernel, sizes, widest),
        in_specs=[hbm] * 15 + [vmem] * 5,
        out_specs=[spec for _, spec in outs],
        out_shape=[out for out, _ in outs],
        scratch_shapes=[
            pltpu.VMEM((slab, model), F32),
            pltpu.VMEM((slab, model), F32),
            pltpu.VMEM((slab, model), BF16),
            pltpu.VMEM((slab, model), BF16),
            pltpu.VMEM((slab, model), BF16),
            pltpu.VMEM((slab, model), BF16),
            pltpu.VMEM((model, model), BF16),
            pltpu.VMEM((model, 3 * width), BF16),
            pltpu.VMEM((seq_len, width), BF16),
            pltpu.VMEM((seq_len, width), BF16),
            pltpu.VMEM((seq_len, width), BF16),
            pltpu.VMEM((seq_len, 3 * width), BF16),
            pltpu.VMEM((seq_len, width), BF16),
            pltpu.VMEM((n_tp, slab, width), BF16),
            pltpu.VMEM((n_tp + 1, slab, model), BF16),
            pltpu.VMEM((n_tp, slab, model), BF16),
            pltpu.VMEM((LANES, seq_len), BF16),
            pltpu.VMEM((seq_len, LANES), F32),
            pltpu.VMEM((seq_len, LANES), F32),
            pltpu.VMEM((2,) + piece_o, BF16),
            pltpu.VMEM(piece_o, BF16),
            pltpu.VMEM((2,) + piece_q, BF16),
            pltpu.VMEM(piece_q, BF16),
            pltpu.VMEM((2,) + halved(piece_gu), BF16),
            pltpu.VMEM((2,) + halved(piece_d), BF16),
            pltpu.VMEM((2,) + halved(piece_o), BF16),
            pltpu.VMEM((2,) + halved(piece_q), BF16),
            pltpu.VMEM((n_tp, each, part_rows), BF16),
            pltpu.VMEM((half, each, part_rows), BF16),
            pltpu.VMEM((8, model), F32),
            pltpu.VMEM((8, width), F32),
            pltpu.VMEM((n_tp, n_fsdp, 8, LANES), F32),
            pltpu.VMEM((n_tp, n_fsdp, 8, LANES), F32),
            pltpu.VMEM((half, 2, 8, LANES), F32),
            pltpu.VMEM((8, LANES), F32),
            dma((pairs, n_tp)), dma((pairs, n_tp)),
            dma((n_tp, model // tile)), dma((n_tp + 1, model // tile)),
            dma((2, half)), dma((2, half)),
            dma((2, half + 1)), dma((2, half + 1)), dma((2, half + 1)), dma((2, half + 1)),
            dma((2, n_tp)), dma((2, half + n_tp)), dma((16 + half,)), dma((3,)), dma((3,)),
        ],
        input_output_aliases={11: 4, 12: 5},
        compiler_params=pltpu.CompilerParams(
            collective_id=2, has_side_effects=True, vmem_limit_bytes=62 * 2**20
        ),
        cost_estimate=pl.CostEstimate(flops=10**11, bytes_accessed=10**8, transcendentals=0),
    )(
        gn2, resid, tok, cot, att_own, wo_all, wq_all, q_in, k_in, v_in, one, sum_gu, sum_d,
        relay_gu, relay_d, rows_in, *tables, starts,
    )


def last_kernel(count, *refs):
    gu, down, qkv = refs[:count], refs[count : 2 * count], refs[2 * count : 3 * count]
    gu_out, down_out, qkv_out = refs[3 * count :]
    width = qkv_out.shape[2]
    for part in range(2):
        gu_out[:, part, :] = sum([ref[0, part].astype(F32) for ref in gu[1:]], gu[0][0, part].astype(F32))
    down_out[...] = sum([ref[0].astype(F32) for ref in down[1:]], down[0][0].astype(F32))
    for part in range(3):
        lanes = slice(part * width, (part + 1) * width)
        qkv_out[:, part, :] = sum(
            [ref[0, :, lanes].astype(F32) for ref in qkv[1:]], qkv[0][0, :, lanes].astype(F32)
        )


def last_sums(own_gu, near_gu, own_down, near_down, own_qkv, near_qkv, direct):
    rows, hidden, part_rows = own_gu.shape[2], own_gu.shape[3], own_down.shape[2]
    width = own_qkv.shape[2] // 3
    steps = 4
    gu = lambda k: pl.BlockSpec((1, 2, rows // steps, hidden), lambda i, k=k: (k, 0, i, 0))
    down = lambda k: pl.BlockSpec((1, hidden // steps, part_rows), lambda i, k=k: (k, i, 0))
    qkv = lambda k: pl.BlockSpec((1, rows // steps, 3 * width), lambda i, k=k: (k, i, 0))
    places = [0] + direct
    return pl.pallas_call(
        functools.partial(last_kernel, len(places)),
        grid=(steps,),
        in_specs=[make(k) for make in (gu, down, qkv) for k in places],
        out_specs=[
            pl.BlockSpec((rows // steps, 2, hidden), lambda i: (i, 0, 0)),
            pl.BlockSpec((hidden // steps, part_rows), lambda i: (i, 0)),
            pl.BlockSpec((rows // steps, 3, width), lambda i: (i, 0, 0)),
        ],
        out_shape=[
            jax.ShapeDtypeStruct((rows, 2, hidden), F32),
            jax.ShapeDtypeStruct((hidden, part_rows), F32),
            jax.ShapeDtypeStruct((rows, 3, width), F32),
        ],
        compiler_params=pltpu.CompilerParams(vmem_limit_bytes=62 * 2**20),
    )(
        *[own_gu] + [near_gu] * len(direct),
        *[own_down] + [near_down] * len(direct),
        *[own_qkv] + [near_qkv] * len(direct),
    )


def reduce_rows(values):
    return lax.psum_scatter(values.astype(BF16), "tp", scatter_dimension=0, tiled=True).astype(F32)


def local(tokens, lengths, ln_gains, ln_shifts, w_qkv, b_qkv, w_out, w_gate_up, w_down, cotangent):
    n_fsdp, n_tp = lax.axis_size("fsdp"), lax.axis_size("tp")
    sizes = (n_fsdp, n_tp)
    at_tp = lax.axis_index("tp")
    slab_rows, model_width = tokens.shape
    seq_len = slab_rows * n_tp
    small = ln_gains.shape[1]
    local_width = w_qkv.shape[2]
    hidden_width = w_gate_up.shape[2]
    part_rows = w_qkv.shape[0]

    length_row = lengths[0]
    doc_ends = jnp.cumsum(length_row)
    ids = jnp.arange(seq_len, dtype=jnp.int32)
    passed = (doc_ends[None, :] <= ids[:, None]).astype(jnp.int32)
    starts = jnp.sum(passed * length_row[None, :], axis=1)
    places = (ids - starts).astype(F32)
    frequency = 10000.0 ** (-2.0 * jnp.arange(ROT // 2, dtype=F32) / ROT)
    angles = frequency[:, None] * places[None, :]
    turns = jnp.concatenate([jnp.cos(angles), jnp.sin(angles)], axis=0)
    starts_row = starts.reshape(1, seq_len).astype(jnp.int32)
    widest = seq_len // 2

    tile = jnp.concatenate([ln_gains, ln_shifts, b_qkv.astype(F32), jnp.zeros((1, small), F32)], 0)
    tile = jnp.pad(tile, ((0, 0), (0, LANES - small)))
    (
        full_one, queries, key_vals, value_rows, residual, normed_two, norm_rows_all, attended_own,
        grad_branch, qkv_all, out_all, gu_all, down_all, *tables,
    ) = front(
        sizes, widest, tokens, cotangent, w_qkv.reshape(part_rows, 3 * local_width), w_out,
        w_gate_up.transpose(1, 0, 2), w_down, tile, turns, starts_row,
    )
    full_one = full_one.reshape(seq_len, model_width)

    grad_normed_two, branch_terms, sum_gu, sum_down, _, _, relay_gu, relay_down = middle(
        sizes, normed_two, grad_branch, gu_all, down_all
    )
    (
        grad_tokens, shares, near_gu, near_down, own_gu, own_down, sum_qkv, near_qkv, _, _, _, _, _, _,
        out_parts,
    ) = back(
        sizes, widest, grad_normed_two, residual, tokens, cotangent, attended_own, out_all, qkv_all,
        queries, key_vals, value_rows, full_one, sum_gu, sum_down, relay_gu, relay_down,
        norm_rows_all, tables, starts_row,
    )
    branch = reduce_rows(branch_terms.reshape(seq_len, model_width))
    result = (residual + branch).astype(BF16)
    direct = [1, 2] if n_fsdp == 8 else list(range(1, n_fsdp // 2))

    gu_share, down_share, qkv_share = last_sums(
        own_gu, near_gu, own_down, near_down, sum_qkv, near_qkv, direct
    )
    shares = shares[:, :small]
    return (
        result,
        grad_tokens,
        shares[0:2],
        shares[2:4],
        qkv_share,
        shares[4:7],
        jnp.sum(out_parts.astype(F32), axis=0),
        gu_share,
        down_share,
    )


def solution(mesh):
    placed = (
        P(("fsdp", "tp"), None),
        P("fsdp", None),
        P(None, ("fsdp", "tp")),
        P(None, ("fsdp", "tp")),
        P("fsdp", None, "tp"),
        P(None, ("tp", "fsdp")),
        P("tp", "fsdp"),
        P("fsdp", None, "tp"),
        P("tp", "fsdp"),
        P(("fsdp", "tp"), None),
    )
    return jax.shard_map(
        local,
        mesh=mesh,
        in_specs=placed,
        out_specs=(
            P(("fsdp", "tp"), None),
            P(("fsdp", "tp"), None),
            P(None, ("fsdp", "tp")),
            P(None, ("fsdp", "tp")),
            P("fsdp", None, "tp"),
            P(None, ("tp", "fsdp")),
            P("tp", "fsdp"),
            P("fsdp", None, "tp"),
            P("tp", "fsdp"),
        ),
        check_vma=False,
    )
```
